256 devices in a mesh: section: 4 (over z_lo, core), dp: 64 (over x, y, z_hi).
Axes of the slice: x: 4, y: 4, z: 8 (z_hi: 4, z_lo: 2; z = z_hi * 2 + z_lo), core: 2. Of those that a mesh axis runs over, the one named last changes fastest.
Arguments:
- images: bfloat16 [2, 64, 12, 3840], P(None, 'dp'), may hold values from -6 to 6
- targets: bfloat16 [2, 64, 12, 3840], P(None, 'dp'), may hold values from -6 to 6
- kernels: bfloat16 [4, 2880, 640], P('section'), may hold values from -0.109375 to 0.109375
Outputs:
- kernel_grad: float32 [4, 2880, 640], P('section', 'dp')
The draws below stay inside these ranges and needn't reach their ends.
All inputs are finite; a program needn't handle non-finite values.
Results may differ from the reference program's by a relative error of at most 0.0075.
Values may be sent and summed in bfloat16 or wider, within the bound.
A program may use at most 128 MiB of HBM per device.

```python
import jax
import jax.numpy as jnp
from jax import lax

CH = 320
CW = 640
IMG = 12
MB = 2
CEN = 6
SAMPLES = 64
KR = 2880
N_SECTION = 4


def level_of(rng, shape, split, low, largest):
    loudness, own = 1.0, jax.random.fold_in(rng, 6)
    for axis_at, blocks in split:
        draws = jnp.exp(jax.random.uniform(jax.random.fold_in(own, axis_at), (blocks,), jnp.float32, low / len(split), largest / len(split)))
        loudness = loudness * jnp.repeat(draws, shape[axis_at] // blocks).reshape([-1 if axis == axis_at else 1 for axis in range(len(shape))])
    return loudness


def normal_values(own_key, shape, deviation, bound, cuts=(), dtype=jnp.bfloat16):
    entries = deviation * jax.random.normal(own_key, shape, jnp.float32)
    if cuts:
        entries = entries * level_of(own_key, shape, cuts, -0.22, 0.18)
    return jnp.clip(entries, -bound, bound).astype(dtype)


def setup_inputs(seed: int = 0) -> dict:
    keys = jax.random.split(jax.random.key(seed), 4)
    images = normal_values(keys[0], (MB, SAMPLES, IMG, IMG * CH), 1.0, 6.0, ((1, 64),))
    targets = normal_values(keys[1], (MB, SAMPLES, IMG, IMG * CH), 1.0, 6.0, ((1, 64),))
    kernels = normal_values(keys[2], (N_SECTION, KR, CW), (9 * CH) ** -0.5, 0.109375, ((0, 4),))
    return dict(images=images, targets=targets, kernels=kernels)


def patches(tensor, stride):
    height, breadth, channels = tensor.shape
    rows_out = height // stride
    cols_out = breadth // stride
    padded = jnp.pad(tensor, ((1, 1), (1, 1), (0, 0)))
    pieces = []
    for row_tap in range(3):
        for col_tap in range(3):
            limits = (row_tap + stride * (rows_out - 1) + 1, col_tap + stride * (cols_out - 1) + 1, channels)
            pieces.append(lax.slice(padded, (row_tap, col_tap, 0), limits, (stride, stride, 1)))
    return jnp.concatenate(pieces, axis=-1).reshape(rows_out * cols_out, 9 * channels)

def unpatch(columns, height, breadth, channels):
    start_field = jnp.zeros((height, breadth, channels), jnp.float32)
    unused, pullback = jax.vjp(lambda tensor: patches(tensor, 1), start_field)
    return pullback(columns)[0]

def silu_slope(values):
    logistic = jax.nn.sigmoid(values)
    return logistic * (1.0 + values * (1.0 - logistic))

def batch_patches(grids, stride):
    return jax.vmap(lambda tensor: patches(tensor, stride))(grids)

def batch_unpatch(columns, extent, channels):
    return jax.vmap(lambda column_block: unpatch(column_block, extent, extent, channels))(columns)

def group_product(first_half, second_half, kernel):
    return jnp.concatenate([jnp.dot(first_half, kernel[:, :CH], preferred_element_type=jnp.float32), jnp.dot(second_half, kernel[:, CH:], preferred_element_type=jnp.float32)], axis=1)

def group_grad(first_half, second_half, delta):
    return jnp.concatenate([jnp.dot(first_half.T, delta[:, :CH], preferred_element_type=jnp.float32), jnp.dot(second_half.T, delta[:, CH:], preferred_element_type=jnp.float32)], axis=1)

def group_back(delta, kernel, extent):
    cells = extent * extent
    back_first = batch_unpatch(jnp.dot(delta[:, :CH], kernel[:, :CH].T, preferred_element_type=jnp.float32).reshape(SAMPLES, cells, 9 * CH), extent, CH)
    back_second = batch_unpatch(jnp.dot(delta[:, CH:], kernel[:, CH:].T, preferred_element_type=jnp.float32).reshape(SAMPLES, cells, 9 * CH), extent, CH)
    return jnp.concatenate([back_first, back_second], axis=-1)

def reference(images, targets, kernels):
    centre_cells = CEN * CEN
    full_cells = IMG * IMG
    scale_loss = 1.0 / (MB * SAMPLES)
    grads_list = [jnp.zeros((9 * CH, CW), jnp.float32) for section_number in range(4)]
    for micro_batch in range(MB):
        image_grid = images[micro_batch].reshape(SAMPLES, IMG, IMG, CH)
        target_rows = targets[micro_batch].reshape(SAMPLES * full_cells, CH).astype(jnp.float32)
        encoder_cols = batch_patches(image_grid, 2).reshape(SAMPLES * centre_cells, 9 * CH)
        encoder_pre = jnp.dot(encoder_cols, kernels[0], preferred_element_type=jnp.float32)
        encoded = jax.nn.silu(encoder_pre).astype(jnp.bfloat16)
        hidden = encoded
        saved = []
        for centre_level in (1, 2):
            lattice = hidden.reshape(SAMPLES, CEN, CEN, CW)
            first_half = batch_patches(lattice[..., :CH], 1).reshape(SAMPLES * centre_cells, 9 * CH)
            second_half = batch_patches(lattice[..., CH:], 1).reshape(SAMPLES * centre_cells, 9 * CH)
            preact = group_product(first_half, second_half, kernels[centre_level])
            saved.append((first_half, second_half, preact))
            hidden = (hidden.astype(jnp.float32) + jax.nn.silu(preact)).astype(jnp.bfloat16)
        joined = (hidden.astype(jnp.float32) + encoded.astype(jnp.float32)).astype(jnp.bfloat16)
        upsampled = jnp.repeat(jnp.repeat(joined.reshape(SAMPLES, CEN, CEN, CW), 2, axis=1), 2, axis=2)
        dec_first = batch_patches(upsampled[..., :CH], 1).reshape(SAMPLES * full_cells, 9 * CH)
        dec_second = batch_patches(upsampled[..., CH:], 1).reshape(SAMPLES * full_cells, 9 * CH)
        decoder_pre = group_product(dec_first, dec_second, kernels[3])
        value_dec = decoder_pre[:, :CH]
        gate_dec = decoder_pre[:, CH:]
        residual = (value_dec * jax.nn.silu(gate_dec) - target_rows) * scale_loss
        delta_dec = jnp.concatenate([residual * jax.nn.silu(gate_dec), residual * value_dec * silu_slope(gate_dec)], axis=1).astype(jnp.bfloat16)
        grads_list[3] = grads_list[3] + group_grad(dec_first, dec_second, delta_dec)
        back_up = group_back(delta_dec, kernels[3], IMG)
        joined_grad = back_up.reshape(SAMPLES, CEN, 2, CEN, 2, CW).sum(axis=(2, 4)).reshape(SAMPLES * centre_cells, CW).astype(jnp.bfloat16)
        grad_hidden = joined_grad
        for centre_level in (2, 1):
            first_half, second_half, preact = saved[centre_level - 1]
            delta_centre = (grad_hidden.astype(jnp.float32) * silu_slope(preact)).astype(jnp.bfloat16)
            grads_list[centre_level] = grads_list[centre_level] + group_grad(first_half, second_half, delta_centre)
            back_all = group_back(delta_centre, kernels[centre_level], CEN).reshape(SAMPLES * centre_cells, CW)
            grad_hidden = (grad_hidden.astype(jnp.float32) + back_all).astype(jnp.bfloat16)
        grad_encoded = grad_hidden.astype(jnp.float32) + joined_grad.astype(jnp.float32)
        delta_enc = (grad_encoded * silu_slope(encoder_pre)).astype(jnp.bfloat16)
        grads_list[0] = grads_list[0] + group_grad(encoder_cols, encoder_cols, delta_enc)
    return jnp.stack(grads_list)
```

```python
import jax
import jax.numpy as jnp
import numpy as np
from jax import lax
from jax.experimental import pallas as pl
from jax.experimental.pallas import tpu as pltpu
from jax.sharding import PartitionSpec as P

MESH = pl.DeviceIdType.MESH
ROWS = 80
CH = 320
GW = 384
TAPS = 9
SHARE = 45
SLOT = 48


def phase_shift(phase, tap):
    alpha, beta = divmod(phase, 2)
    a, b = divmod(tap, 3)
    return ((alpha + a - 1) // 2 + 1) * 3 + ((beta + b - 1) // 2 + 1)


def tables():
    shift = np.zeros((TAPS, ROWS, ROWS), np.float32)
    encode = np.zeros((TAPS, ROWS, 288), np.float32)
    order = np.zeros((4, ROWS, 288), np.float32)
    for n in range(2):
        for i in range(6):
            for j in range(6):
                r = n * 36 + i * 6 + j
                for tap in range(TAPS):
                    a, b = divmod(tap, 3)
                    ii, jj = i + a - 1, j + b - 1
                    if 0 <= ii < 6 and 0 <= jj < 6:
                        shift[tap, r, n * 36 + ii * 6 + jj] = 1
                    ii, jj = 2 * i + a - 1, 2 * j + b - 1
                    if 0 <= ii < 12 and 0 <= jj < 12:
                        encode[tap, r, n * 144 + ii * 12 + jj] = 1
                for phase in range(4):
                    alpha, beta = divmod(phase, 2)
                    order[phase, r, n * 144 + (2 * i + alpha) * 12 + 2 * j + beta] = 1
    fold = np.zeros((TAPS, ROWS, 4, ROWS), np.float32)
    for tap in range(TAPS):
        for phase in range(4):
            fold[tap, :, phase, :] = shift[phase_shift(phase, tap)].T
    return (
        shift.reshape(TAPS * ROWS, ROWS),
        encode.reshape(TAPS * ROWS, 288),
        fold.reshape(TAPS * ROWS, 4 * ROWS),
        order.reshape(4 * ROWS, 288),
    )


def silu(v):
    return v * jax.nn.sigmoid(v)


def silu_slope(v):
    g = jax.nn.sigmoid(v)
    return g * (1.0 + v * (1.0 - g))


def mm(a, b):
    return jnp.dot(a, b, preferred_element_type=jnp.float32)


def mm_nt(a, b):
    return lax.dot_general(a, b, (((1,), (1,)), ((), ())), preferred_element_type=jnp.float32)


def mm_tn(a, b):
    return lax.dot_general(a, b, (((0,), (0,)), ((), ())), preferred_element_type=jnp.float32)


def remote(src, dst, send_sem, recv_sem, device):
    return pltpu.make_async_remote_copy(
        src_ref=src, dst_ref=dst, send_sem=send_sem, recv_sem=recv_sem, device_id=device, device_id_type=MESH
    )


def body(
    img, tgt, ker, c_shift, c_encode, c_fold, c_order, out,
    w_in, x_in, t_in, s_shift, s_encode, s_fold, s_order,
    wp, feat, act, pre, delta3, zed, target,
    h_in, skip_in, g_in, gskip_in, h_out, g_out,
    gx, gh, gd, gz, left, grad, pack, y_buf, y_sum, z_out, z_buf,
    load_sem, hop_send, hop_recv, a_send, a_recv, d_send, d_recv, y_send, y_recv, z_send, z_recv,
):
    bf = jnp.bfloat16
    f32 = jnp.float32
    sec = lax.axis_index("section")
    dp = lax.axis_index("dp")
    x, y, z = dp // 16, (dp // 4) % 4, dp % 4

    def x_peer(k):
        p = (x + k) % 4
        return p, {"dp": p * 16 + y * 4 + z}

    def y_peer(k):
        p = (y + k) % 4
        return p, {"dp": x * 16 + p * 4 + z}

    def z_peer(k):
        p = (z + k) % 4
        return p, {"dp": x * 16 + y * 4 + p}

    def load(src, dst, n):
        return pltpu.make_async_copy(src, dst, load_sem.at[n])

    w_load = load(ker, w_in, 0)
    w_load.start()

    barrier = pltpu.get_barrier_semaphore()
    for k in range(1, 4):
        pl.semaphore_signal(barrier, inc=1, device_id={"section": (sec + k) % 4}, device_id_type=MESH)
        for peer in (x_peer, y_peer, z_peer):
            pl.semaphore_signal(barrier, inc=1, device_id=peer(k)[1], device_id_type=MESH)
    pl.semaphore_wait(barrier, 12)

    row0 = pl.multiple_of(x * 160, 16)

    def gather_start(src, buf, send, recv):
        copies = []
        for k in range(1, 4):
            p, dev = x_peer(k)
            copy = remote(src, buf.at[x], send.at[p], recv.at[x], dev)
            copy.start()
            copies.append(copy)
        return copies

    def gather_wait(k, src, buf, send, recv):
        p, dev = x_peer(k)
        remote(src, buf.at[p], send.at[p], recv.at[p], dev).wait_recv()
        return p

    def group(g):
        return slice(g * GW, (g + 1) * GW)

    def pack_weights():
        lane = lax.broadcasted_iota(jnp.int32, (CH, GW), 1)

        def one(t, carry):
            rows = pl.ds(pl.multiple_of(t * CH, 16), CH)
            base = pl.multiple_of(t * GW, 16)
            first = w_in[rows, 0:GW].astype(f32)
            wp[0, pl.ds(base, CH), :] = jnp.where(lane < CH, first, 0.0).astype(bf)
            second = pltpu.roll(w_in[rows, 256:640].astype(f32), GW - 64, 1)
            wp[1, pl.ds(base, CH), :] = jnp.where(lane < CH, second, 0.0).astype(bf)
            for g in range(2):
                wp[g, pl.ds(base + CH, GW - CH), :] = jnp.zeros((GW - CH, GW), bf)
            return carry

        lax.fori_loop(0, TAPS, one, 0)

    def left_shift(p):
        part = mm(s_shift[pl.ds(row0, 240), :], gh[p]).astype(bf)
        for k in range(3):
            left[k, pl.ds(pl.multiple_of(p * ROWS, 16), ROWS), :] = part[k * ROWS:(k + 1) * ROWS]

    def left_encode(p):
        part = mm(s_encode[pl.ds(row0, 240), :], gx[p]).astype(bf)
        for k in range(3):
            left[k, pl.ds(pl.multiple_of(p * ROWS, 16), ROWS), 0:GW] = part[k * ROWS:(k + 1) * ROWS]

    @pl.when(sec == 0)
    def encoder():
        loads = [load(img, x_in, 1), load(c_encode, s_encode, 2)]
        for copy in loads:
            copy.start()
        for copy in loads:
            copy.wait()
        e_all = mm(s_encode[...], x_in[...]).astype(bf)
        w_load.wait()
        acc = jnp.zeros((ROWS, 2 * CH), f32)
        for t in range(TAPS):
            acc = acc + mm(e_all[t * ROWS:(t + 1) * ROWS, 0:CH], w_in[t * CH:(t + 1) * CH, :])
        wide = jnp.concatenate([acc, jnp.zeros((ROWS, 128), f32)], axis=1)
        moved = pltpu.roll(wide, 64, 1)
        lane = lax.broadcasted_iota(jnp.int32, (ROWS, 2 * GW), 1)
        wide = jnp.where(lane < CH, wide, jnp.where((lane >= GW) & (lane < GW + CH), moved, 0.0))
        act[...] = wide
        h_out[...] = silu(wide).astype(bf)
        sends = [
            remote(h_out, h_in, hop_send.at[0], hop_recv.at[0], {"section": 1}),
            remote(h_out, skip_in, hop_send.at[1], hop_recv.at[1], {"section": 3}),
        ]
        for copy in sends:
            copy.start()
        sends += gather_start(x_in, gx, a_send, a_recv)
        gx[x] = x_in[...]
        left_encode(x)
        for k in range(1, 4):
            left_encode(gather_wait(k, x_in, gx, a_send, a_recv))
        remote(g_out, gskip_in, hop_send.at[3], hop_recv.at[3], {"section": 3}).wait_recv()
        remote(g_out, g_in, hop_send.at[2], hop_recv.at[2], {"section": 1}).wait_recv()
        total = g_in[...].astype(f32) + gskip_in[...].astype(f32)
        h_in[...] = (total * silu_slope(act[...])).astype(bf)
        sends += gather_start(h_in, gd, d_send, d_recv)
        gd[x] = h_in[...]
        for k in range(1, 4):
            gather_wait(k, h_in, gd, d_send, d_recv)
        right = gd[...].reshape(4 * ROWS, 2 * GW)
        for k in range(3):
            grad[k * CH:(k + 1) * CH, :] = mm_tn(left[k, :, 0:GW], right)[0:CH]
        for copy in sends:
            copy.wait_send()

    @pl.when((sec == 1) | (sec == 2))
    def centre():
        s_load = load(c_shift, s_shift, 1)
        s_load.start()
        w_load.wait()
        pack_weights()
        s_load.wait()
        remote(h_out, h_in, hop_send.at[0], hop_recv.at[0], {"section": sec - 1}).wait_recv()
        h = h_in[...]
        shifted = mm(s_shift[...], h).astype(bf)
        for g in range(2):
            for t in range(TAPS):
                feat[g, 0:ROWS, t * GW:(t + 1) * GW] = shifted[t * ROWS:(t + 1) * ROWS, group(g)]
            pre_g = mm(feat[g, 0:ROWS, :], wp[g])
            act[:, group(g)] = pre_g
            h_out[:, group(g)] = (h[:, group(g)].astype(f32) + silu(pre_g)).astype(bf)
        hop = remote(h_out, h_in, hop_send.at[0], hop_recv.at[0], {"section": sec + 1})
        hop.start()
        sends = [hop]
        sends += gather_start(h_in, gh, a_send, a_recv)
        gh[x] = h
        left_shift(x)
        for k in range(1, 4):
            left_shift(gather_wait(k, h_in, gh, a_send, a_recv))
        remote(g_out, g_in, hop_send.at[2], hop_recv.at[2], {"section": sec + 1}).wait_recv()
        delta = (g_in[...].astype(f32) * silu_slope(act[...])).astype(bf)
        skip_in[...] = delta
        sends += gather_start(skip_in, gd, d_send, d_recv)
        back = mm(s_shift[...], delta).astype(bf)
        for g in range(2):
            acc = g_in[:, group(g)].astype(f32)
            for t in range(TAPS):
                piece = back[(8 - t) * ROWS:(9 - t) * ROWS, group(g)]
                acc = acc + mm_nt(piece, wp[g, t * GW:(t + 1) * GW, :])
            g_out[:, group(g)] = acc.astype(bf)
        hop = remote(g_out, g_in, hop_send.at[2], hop_recv.at[2], {"section": sec - 1})
        hop.start()
        sends.append(hop)
        gd[x] = delta
        for k in range(1, 4):
            gather_wait(k, skip_in, gd, d_send, d_recv)
        for g in range(2):
            right = gd[:, :, group(g)].reshape(4 * ROWS, GW)
            for k in range(3):
                grad[k * CH:(k + 1) * CH, group(g)] = mm_tn(left[k, :, group(g)], right)[0:CH]
        for copy in sends:
            copy.wait_send()

    @pl.when(sec == 3)
    def decoder():
        loads = [load(c_shift, s_shift, 1), load(c_fold, s_fold, 2), load(c_order, s_order, 3), load(tgt, t_in, 4)]
        for copy in loads:
            copy.start()
        w_load.wait()
        pack_weights()
        for copy in loads:
            copy.wait()
        target[...] = mm(s_order[...], t_in[...])
        remote(h_out, skip_in, hop_send.at[1], hop_recv.at[1], {"section": 0}).wait_recv()
        remote(h_out, h_in, hop_send.at[0], hop_recv.at[0], {"section": 2}).wait_recv()
        u = (h_in[...].astype(f32) + skip_in[...].astype(f32)).astype(bf)
        h_out[...] = u
        sends = gather_start(h_out, gh, a_send, a_recv)
        gh[x] = u
        shifted = mm(s_shift[...], u).astype(bf)
        for g in range(2):
            for phase in range(4):
                for t in range(TAPS):
                    s = phase_shift(phase, t)
                    feat[g, phase * ROWS:(phase + 1) * ROWS, t * GW:(t + 1) * GW] = shifted[
                        s * ROWS:(s + 1) * ROWS, group(g)
                    ]
            pre[g] = mm(feat[g], wp[g])
        value, gate = pre[0], pre[1]
        sig = jax.nn.sigmoid(gate)
        act_gate = gate * sig
        residual = (value * act_gate - target[...]) * (1.0 / 128.0)
        delta3[:, 0:GW] = (residual * act_gate).astype(bf)
        delta3[:, GW:] = (residual * value * (sig * (1.0 + gate * (1.0 - sig)))).astype(bf)
        zed[...] = mm(s_fold[...], delta3[...]).astype(bf)
        for k in range(1, 4):
            p, dev = x_peer(k)
            rows = pl.ds(pl.multiple_of(p * 160, 16), 240)
            copy = remote(zed.at[rows], gz.at[x], d_send.at[p], d_recv.at[x], dev)
            copy.start()
            sends.append(copy)
        for g in range(2):
            acc = jnp.zeros((ROWS, GW), f32)
            for t in range(TAPS):
                acc = acc + mm_nt(zed[t * ROWS:(t + 1) * ROWS, group(g)], wp[g, t * GW:(t + 1) * GW, :])
            g_out[:, group(g)] = acc.astype(bf)
        hops = [
            remote(g_out, g_in, hop_send.at[2], hop_recv.at[2], {"section": 2}),
            remote(g_out, gskip_in, hop_send.at[3], hop_recv.at[3], {"section": 0}),
        ]
        for copy in hops:
            copy.start()
        sends += hops
        gz[x] = zed[pl.ds(row0, 240), :]
        for k in range(1, 4):
            gather_wait(k, h_out, gh, a_send, a_recv)
            p, dev = x_peer(k)
            remote(zed.at[0:240], gz.at[p], d_send.at[p], d_recv.at[p], dev).wait_recv()
        for g in range(2):
            lhs = gh[:, :, group(g)].reshape(4 * ROWS, GW)
            for k in range(3):
                right = gz[:, k * ROWS:(k + 1) * ROWS, group(g)].reshape(4 * ROWS, GW)
                grad[k * CH:(k + 1) * CH, group(g)] = mm_tn(lhs, right)[0:CH]
        for copy in sends:
            copy.wait_send()

    grad[960:976, :] = jnp.zeros((16, 2 * GW), f32)
    lane = lax.broadcasted_iota(jnp.int32, (SLOT, 2 * GW), 1)
    for k in range(16):
        odd = (SHARE * k) % 8
        rows = pl.ds(pl.multiple_of(x * 80 + (SHARE * k - odd), 8), 56)
        part = grad[rows, :]
        if odd:
            part = pltpu.roll(part, 56 - odd, 0)
        part = part[0:SLOT]
        moved = pltpu.roll(part, 2 * GW - 64, 1)
        pack[k] = jnp.where(lane < CH, part, moved)[:, 0:2 * CH].astype(bf)

    sends = []
    for k in range(1, 4):
        p, dev = y_peer(k)
        copy = remote(pack.at[pl.ds(p * 4, 4)], y_buf.at[y], y_send.at[p], y_recv.at[y], dev)
        copy.start()
        sends.append(copy)
    y_sum[...] = pack[pl.ds(y * 4, 4)].astype(f32)
    for k in range(1, 4):
        p, dev = y_peer(k)
        remote(pack.at[pl.ds(0, 4)], y_buf.at[p], y_send.at[p], y_recv.at[p], dev).wait_recv()
        y_sum[...] += y_buf[p].astype(f32)
    z_out[...] = y_sum[...].astype(bf)
    for k in range(1, 4):
        p, dev = z_peer(k)
        copy = remote(z_out.at[p], z_buf.at[z], z_send.at[p], z_recv.at[z], dev)
        copy.start()
        sends.append(copy)
    total = y_sum[z]
    for k in range(1, 4):
        p, dev = z_peer(k)
        remote(z_out.at[p], z_buf.at[p], z_send.at[p], z_recv.at[p], dev).wait_recv()
        total = total + z_buf[p].astype(f32)
    out[...] = total[0:SHARE]
    for copy in sends:
        copy.wait_send()


def on_device(images, targets, kernels):
    bf = jnp.bfloat16

    def cells(grids):
        return jnp.pad(grids.reshape(288, CH), ((0, 0), (0, GW - CH)))

    consts = [jnp.asarray(t, bf) for t in tables()]
    vm = pltpu.VMEM
    dma = pltpu.SemaphoreType.DMA
    hop = vm((ROWS, 2 * GW), bf)
    result = pl.pallas_call(
        body,
        out_shape=jax.ShapeDtypeStruct((SHARE, 2 * CH), jnp.float32),
        in_specs=[pl.BlockSpec(memory_space=pl.ANY)] * 7,
        out_specs=pl.BlockSpec(memory_space=pltpu.VMEM),
        scratch_shapes=[
            vm((TAPS * CH, 2 * CH), bf),
            vm((288, GW), bf),
            vm((288, GW), bf),
            vm((TAPS * ROWS, ROWS), bf),
            vm((TAPS * ROWS, 288), bf),
            vm((TAPS * ROWS, 4 * ROWS), bf),
            vm((4 * ROWS, 288), bf),
            vm((2, TAPS * GW, GW), bf),
            vm((2, 4 * ROWS, TAPS * GW), bf),
            vm((ROWS, 2 * GW), jnp.float32),
            vm((2, 4 * ROWS, GW), jnp.float32),
            vm((4 * ROWS, 2 * GW), bf),
            vm((TAPS * ROWS, 2 * GW), bf),
            vm((4 * ROWS, GW), jnp.float32),
            hop, hop, hop, hop, hop, hop,
            vm((4, 288, GW), bf),
            vm((4, ROWS, 2 * GW), bf),
            vm((4, ROWS, 2 * GW), bf),
            vm((4, 240, 2 * GW), bf),
            vm((3, 4 * ROWS, 2 * GW), bf),
            vm((976, 2 * GW), jnp.float32),
            vm((16, SLOT, 2 * CH), bf),
            vm((4, 4, SLOT, 2 * CH), bf),
            vm((4, SLOT, 2 * CH), jnp.float32),
            vm((4, SLOT, 2 * CH), bf),
            vm((4, SLOT, 2 * CH), bf),
            dma((8,)), dma((4,)), dma((4,)),
            dma((4,)), dma((4,)), dma((4,)), dma((4,)), dma((4,)), dma((4,)), dma((4,)), dma((4,)),
        ],
        compiler_params=pltpu.CompilerParams(
            collective_id=0, has_side_effects=True, vmem_limit_bytes=48 * 1024 * 1024
        ),
    )(cells(images), cells(targets), kernels[0], *consts)
    return result[None]


def solution(mesh):
    return jax.shard_map(
        on_device,
        mesh=mesh,
        in_specs=(P(None, "dp", None, None), P(None, "dp", None, None), P("section", None, None)),
        out_specs=P("section", "dp", None),
        check_vma=False,
    )
```

```python
import jax
import jax.numpy as jnp
import numpy as np
from jax import lax
from jax.experimental import pallas as pl
from jax.experimental.pallas import tpu as pltpu
from jax.sharding import PartitionSpec as P

MESH = pl.DeviceIdType.MESH
ROWS = 80
CH = 320
GW = 384
TAPS = 9
SHARE = 45
SLOT = 48
CELLS = 12 * 32


def phase_shift(phase, tap):
    alpha, beta = divmod(phase, 2)
    a, b = divmod(tap, 3)
    return ((alpha + a - 1) // 2 + 1) * 3 + ((beta + b - 1) // 2 + 1)


def tables():
    shift = np.zeros((TAPS, ROWS, ROWS), np.float32)
    encode = np.zeros((TAPS, ROWS, CELLS), np.float32)
    order = np.zeros((4, ROWS, CELLS), np.float32)
    for n in range(2):
        for i in range(6):
            for j in range(6):
                r = n * 36 + i * 6 + j
                for tap in range(TAPS):
                    a, b = divmod(tap, 3)
                    ii, jj = i + a - 1, j + b - 1
                    if 0 <= ii < 6 and 0 <= jj < 6:
                        shift[tap, r, n * 36 + ii * 6 + jj] = 1
                    ii, jj = 2 * i + a - 1, 2 * j + b - 1
                    if 0 <= ii < 12 and 0 <= jj < 12:
                        encode[tap, r, jj * 32 + n * 16 + ii] = 1
                for phase in range(4):
                    alpha, beta = divmod(phase, 2)
                    order[phase, r, (2 * j + beta) * 32 + n * 16 + 2 * i + alpha] = 1
    fold = np.zeros((TAPS, ROWS, 4, ROWS), np.float32)
    for tap in range(TAPS):
        for phase in range(4):
            fold[tap, :, phase, :] = shift[phase_shift(phase, tap)].T
    return (
        shift.reshape(TAPS * ROWS, ROWS),
        encode.reshape(TAPS * ROWS, CELLS),
        fold.reshape(TAPS * ROWS, 4 * ROWS),
        order.reshape(4 * ROWS, CELLS),
    )


def silu(v):
    return v * jax.nn.sigmoid(v)


def silu_slope(v):
    g = jax.nn.sigmoid(v)
    return g * (1.0 + v * (1.0 - g))


def mm(a, b):
    return jnp.dot(a, b, preferred_element_type=jnp.float32)


def mm_nt(a, b):
    return lax.dot_general(a, b, (((1,), (1,)), ((), ())), preferred_element_type=jnp.float32)


def mm_tn(a, b):
    return lax.dot_general(a, b, (((0,), (0,)), ((), ())), preferred_element_type=jnp.float32)


def remote(src, dst, send_sem, recv_sem, device):
    return pltpu.make_async_remote_copy(
        src_ref=src, dst_ref=dst, send_sem=send_sem, recv_sem=recv_sem, device_id=device, device_id_type=MESH
    )


def body(
    img, tgt, ker, c_shift, c_encode, c_fold, c_order, out,
    w_in, raw, x_in, s_shift, s_encode, s_fold, s_order,
    wp, wt, feat, act, pre, delta3, zed, target,
    h_in, skip_in, g_in, gskip_in, h_out, g_out,
    gx, gh, gd, gz, left, grad, pack, y_buf, y_sum, z_out, z_buf,
    load_sem, hop_send, hop_recv, a_send, a_recv, d_send, d_recv, y_send, y_recv, z_send, z_recv,
):
    bf = jnp.bfloat16
    f32 = jnp.float32
    sec = lax.axis_index("section")
    dp = lax.axis_index("dp")
    x, y, z = dp // 16, (dp // 4) % 4, dp % 4

    def x_peer(k):
        p = (x + k) % 4
        return p, {"dp": p * 16 + y * 4 + z}

    def y_peer(k):
        p = (y + k) % 4
        return p, {"dp": x * 16 + p * 4 + z}

    def z_peer(k):
        p = (z + k) % 4
        return p, {"dp": x * 16 + y * 4 + p}

    def load(src, dst, n):
        return pltpu.make_async_copy(src, dst, load_sem.at[n])

    w_loads = [load(ker.at[0, i * 960:(i + 1) * 960], w_in.at[i * 960:(i + 1) * 960], 5 + i) for i in range(3)]
    for copy in w_loads:
        copy.start()

    barrier = pltpu.get_barrier_semaphore()
    for k in range(1, 4):
        pl.semaphore_signal(barrier, inc=1, device_id={"section": (sec + k) % 4}, device_id_type=MESH)
        for peer in (x_peer, y_peer, z_peer):
            pl.semaphore_signal(barrier, inc=1, device_id=peer(k)[1], device_id_type=MESH)

    def arrive():
        pl.semaphore_wait(barrier, 12)

    row0 = pl.multiple_of(x * 160, 16)

    def gather_start(src, buf, send, recv):
        copies = []
        for k in range(1, 4):
            p, dev = x_peer(k)
            copy = remote(src, buf.at[x], send.at[p], recv.at[x], dev)
            copy.start()
            copies.append(copy)
        return copies

    def gather_wait(k, src, buf, send, recv):
        p, dev = x_peer(k)
        remote(src, buf.at[p], send.at[p], recv.at[p], dev).wait_recv()
        return p

    def group(g):
        return slice(g * GW, (g + 1) * GW)

    def pack_weights():
        lane = lax.broadcasted_iota(jnp.int32, (CH, GW), 1)

        def one(t, carry):
            rows = pl.ds(pl.multiple_of(t * CH, 16), CH)
            base = pl.multiple_of(t * GW, 16)
            first = w_in[rows, 0:GW].astype(f32)
            wp[0, pl.ds(base, CH), :] = jnp.where(lane < CH, first, 0.0).astype(bf)
            second = pltpu.roll(w_in[rows, 256:640].astype(f32), GW - 64, 1)
            wp[1, pl.ds(base, CH), :] = jnp.where(lane < CH, second, 0.0).astype(bf)
            for g in range(2):
                wp[g, pl.ds(base + CH, GW - CH), :] = jnp.zeros((GW - CH, GW), bf)
            return carry

        lax.fori_loop(0, TAPS, one, 0)

    def left_shift(p):
        part = mm(s_shift[pl.ds(row0, 240), :], gh[p]).astype(bf)
        for k in range(3):
            left[k, pl.ds(pl.multiple_of(p * ROWS, 16), ROWS), :] = part[k * ROWS:(k + 1) * ROWS]

    def lay_out_cells():
        x_in[...] = jnp.zeros((CELLS, GW), bf)
        lane = lax.broadcasted_iota(jnp.int32, (12, GW), 1)
        for n in range(2):
            for j in range(12):
                start = j * CH - 64 * (j % 2)
                part = raw[0, :, n, start:start + GW].astype(f32)
                if j % 2:
                    part = pltpu.roll(part, GW - 64, 1)
                x_in[j * 32 + n * 16:j * 32 + n * 16 + 12, :] = jnp.where(lane < CH, part, 0.0).astype(bf)

    def turn_weights():
        def one(t, carry):
            rows = pl.ds(pl.multiple_of(t * GW, 16), GW)
            for g in range(2):
                wt[g, rows, :] = wp[g, rows, :].T
            return carry

        lax.fori_loop(0, TAPS, one, 0)

    @pl.when(sec == 0)
    def encoder():
        loads = [load(img, raw, 1), load(c_encode, s_encode, 2)]
        for copy in loads:
            copy.start()
        for copy in loads:
            copy.wait()
        lay_out_cells()
        zed[:, 0:GW] = mm(s_encode[...], x_in[...]).astype(bf)
        acc = jnp.zeros((ROWS, 2 * CH), f32)
        for t in range(TAPS):
            if t % 3 == 0:
                w_loads[t // 3].wait()
            acc = acc + mm(zed[t * ROWS:(t + 1) * ROWS, 0:CH], w_in[t * CH:(t + 1) * CH, :])
        wide = jnp.concatenate([acc, jnp.zeros((ROWS, 128), f32)], axis=1)
        moved = pltpu.roll(wide, 64, 1)
        lane = lax.broadcasted_iota(jnp.int32, (ROWS, 2 * GW), 1)
        wide = jnp.where(lane < CH, wide, jnp.where((lane >= GW) & (lane < GW + CH), moved, 0.0))
        act[...] = wide
        h_out[...] = silu(wide).astype(bf)
        arrive()
        sends = [
            remote(h_out, h_in, hop_send.at[0], hop_recv.at[0], {"section": 1}),
            remote(h_out, skip_in, hop_send.at[1], hop_recv.at[1], {"section": 3}),
        ]
        for copy in sends:
            copy.start()
        for k in range(1, 4):
            p, dev = x_peer(k)
            rows = pl.ds(pl.multiple_of(p * 160, 16), 240)
            copy = remote(zed.at[rows, 0:GW], gx.at[x], a_send.at[p], a_recv.at[x], dev)
            copy.start()
            sends.append(copy)
        gx[x] = zed[pl.ds(row0, 240), 0:GW]
        for k in range(1, 4):
            p, dev = x_peer(k)
            remote(zed.at[0:240, 0:GW], gx.at[p], a_send.at[p], a_recv.at[p], dev).wait_recv()
        remote(g_out, gskip_in, hop_send.at[3], hop_recv.at[3], {"section": 3}).wait_recv()
        remote(g_out, g_in, hop_send.at[2], hop_recv.at[2], {"section": 1}).wait_recv()
        total = g_in[...].astype(f32) + gskip_in[...].astype(f32)
        h_in[...] = (total * silu_slope(act[...])).astype(bf)
        sends += gather_start(h_in, gd, d_send, d_recv)
        gd[x] = h_in[...]
        for k in range(1, 4):
            gather_wait(k, h_in, gd, d_send, d_recv)
        right = gd[...].reshape(4 * ROWS, 2 * GW)
        for k in range(3):
            lhs = gx[:, k * ROWS:(k + 1) * ROWS, :].reshape(4 * ROWS, GW)
            grad[k * CH:(k + 1) * CH, :] = mm_tn(lhs, right)[0:CH]
        for copy in sends:
            copy.wait_send()

    @pl.when((sec == 1) | (sec == 2))
    def centre():
        s_load = load(c_shift, s_shift, 1)
        s_load.start()
        for copy in w_loads:
            copy.wait()
        pack_weights()
        s_load.wait()
        arrive()
        remote(h_out, h_in, hop_send.at[0], hop_recv.at[0], {"section": sec - 1}).wait_recv()
        h = h_in[...]
        shifted = mm(s_shift[...], h).astype(bf)
        for g in range(2):
            for t in range(TAPS):
                feat[g, 0:ROWS, t * GW:(t + 1) * GW] = shifted[t * ROWS:(t + 1) * ROWS, group(g)]
            pre_g = mm(feat[g, 0:ROWS, :], wp[g])
            act[:, group(g)] = pre_g
            h_out[:, group(g)] = (h[:, group(g)].astype(f32) + silu(pre_g)).astype(bf)
        hop = remote(h_out, h_in, hop_send.at[0], hop_recv.at[0], {"section": sec + 1})
        hop.start()
        sends = [hop]
        sends += gather_start(h_in, gh, a_send, a_recv)
        gh[x] = h
        left_shift(x)
        for k in range(1, 4):
            left_shift(gather_wait(k, h_in, gh, a_send, a_recv))
        turn_weights()
        remote(g_out, g_in, hop_send.at[2], hop_recv.at[2], {"section": sec + 1}).wait_recv()
        delta = (g_in[...].astype(f32) * silu_slope(act[...])).astype(bf)
        skip_in[...] = delta
        sends += gather_start(skip_in, gd, d_send, d_recv)
        back = mm(s_shift[...], delta).astype(bf)
        for g in range(2):
            acc = g_in[:, group(g)].astype(f32)
            for t in range(TAPS):
                piece = back[(8 - t) * ROWS:(9 - t) * ROWS, group(g)]
                acc = acc + mm(piece, wt[g, t * GW:(t + 1) * GW, :])
            g_out[:, group(g)] = acc.astype(bf)
        hop = remote(g_out, g_in, hop_send.at[2], hop_recv.at[2], {"section": sec - 1})
        hop.start()
        sends.append(hop)
        gd[x] = delta
        for k in range(1, 4):
            gather_wait(k, skip_in, gd, d_send, d_recv)
        for g in range(2):
            right = gd[:, :, group(g)].reshape(4 * ROWS, GW)
            for k in range(3):
                grad[k * CH:(k + 1) * CH, group(g)] = mm_tn(left[k, :, group(g)], right)[0:CH]
        for copy in sends:
            copy.wait_send()

    @pl.when(sec == 3)
    def decoder():
        loads = [load(c_shift, s_shift, 1), load(c_fold, s_fold, 2), load(c_order, s_order, 3), load(tgt, raw, 4)]
        for copy in loads:
            copy.start()
        for copy in w_loads:
            copy.wait()
        pack_weights()
        turn_weights()
        for copy in loads:
            copy.wait()
        lay_out_cells()
        target[...] = mm(s_order[...], x_in[...])
        arrive()
        remote(h_out, skip_in, hop_send.at[1], hop_recv.at[1], {"section": 0}).wait_recv()
        remote(h_out, h_in, hop_send.at[0], hop_recv.at[0], {"section": 2}).wait_recv()
        u = (h_in[...].astype(f32) + skip_in[...].astype(f32)).astype(bf)
        h_out[...] = u
        sends = gather_start(h_out, gh, a_send, a_recv)
        gh[x] = u
        shifted = mm(s_shift[...], u).astype(bf)
        for g in range(2):
            for phase in range(4):
                for t in range(TAPS):
                    s = phase_shift(phase, t)
                    feat[g, phase * ROWS:(phase + 1) * ROWS, t * GW:(t + 1) * GW] = shifted[
                        s * ROWS:(s + 1) * ROWS, group(g)
                    ]
            pre[g] = mm(feat[g], wp[g])
        value, gate = pre[0], pre[1]
        sig = jax.nn.sigmoid(gate)
        act_gate = gate * sig
        residual = (value * act_gate - target[...]) * (1.0 / 128.0)
        delta3[:, 0:GW] = (residual * act_gate).astype(bf)
        delta3[:, GW:] = (residual * value * (sig * (1.0 + gate * (1.0 - sig)))).astype(bf)
        zed[...] = mm(s_fold[...], delta3[...]).astype(bf)
        for k in range(1, 4):
            p, dev = x_peer(k)
            rows = pl.ds(pl.multiple_of(p * 160, 16), 240)
            copy = remote(zed.at[rows], gz.at[x], d_send.at[p], d_recv.at[x], dev)
            copy.start()
            sends.append(copy)
        for g in range(2):
            acc = jnp.zeros((ROWS, GW), f32)
            for t in range(TAPS):
                acc = acc + mm(zed[t * ROWS:(t + 1) * ROWS, group(g)], wt[g, t * GW:(t + 1) * GW, :])
            g_out[:, group(g)] = acc.astype(bf)
        hops = [
            remote(g_out, g_in, hop_send.at[2], hop_recv.at[2], {"section": 2}),
            remote(g_out, gskip_in, hop_send.at[3], hop_recv.at[3], {"section": 0}),
        ]
        for copy in hops:
            copy.start()
        sends += hops
        gz[x] = zed[pl.ds(row0, 240), :]
        for k in range(1, 4):
            gather_wait(k, h_out, gh, a_send, a_recv)
            p, dev = x_peer(k)
            remote(zed.at[0:240], gz.at[p], d_send.at[p], d_recv.at[p], dev).wait_recv()
        for g in range(2):
            lhs = gh[:, :, group(g)].reshape(4 * ROWS, GW)
            for k in range(3):
                right = gz[:, k * ROWS:(k + 1) * ROWS, group(g)].reshape(4 * ROWS, GW)
                grad[k * CH:(k + 1) * CH, group(g)] = mm_tn(lhs, right)[0:CH]
        for copy in sends:
            copy.wait_send()

    grad[960:976, :] = jnp.zeros((16, 2 * GW), f32)
    lane = lax.broadcasted_iota(jnp.int32, (SLOT, 2 * GW), 1)
    for k in range(16):
        odd = (SHARE * k) % 8
        rows = pl.ds(pl.multiple_of(x * 80 + (SHARE * k - odd), 8), 56)
        part = grad[rows, :]
        if odd:
            part = pltpu.roll(part, 56 - odd, 0)
        part = part[0:SLOT]
        moved = pltpu.roll(part, 2 * GW - 64, 1)
        pack[k] = jnp.where(lane < CH, part, moved)[:, 0:2 * CH].astype(bf)

    sends = []
    for k in range(1, 4):
        p, dev = y_peer(k)
        copy = remote(pack.at[pl.ds(p * 4, 4)], y_buf.at[y], y_send.at[p], y_recv.at[y], dev)
        copy.start()
        sends.append(copy)
    y_sum[...] = pack[pl.ds(y * 4, 4)].astype(f32)
    for k in range(1, 4):
        p, dev = y_peer(k)
        remote(pack.at[pl.ds(0, 4)], y_buf.at[p], y_send.at[p], y_recv.at[p], dev).wait_recv()
        y_sum[...] += y_buf[p].astype(f32)
    z_out[...] = y_sum[...].astype(bf)
    for k in range(1, 4):
        p, dev = z_peer(k)
        copy = remote(z_out.at[p], z_buf.at[z], z_send.at[p], z_recv.at[z], dev)
        copy.start()
        sends.append(copy)
    total = y_sum[z]
    for k in range(1, 4):
        p, dev = z_peer(k)
        remote(z_out.at[p], z_buf.at[p], z_send.at[p], z_recv.at[p], dev).wait_recv()
        total = total + z_buf[p].astype(f32)
    out[:, 0, :] = total[0:SHARE]
    for copy in sends:
        copy.wait_send()


def on_device(images, targets, kernels):
    bf = jnp.bfloat16

    def by_rows(grids):
        return jnp.transpose(grids, (1, 2, 0, 3))

    consts = [jnp.asarray(t, bf) for t in tables()]
    vm = pltpu.VMEM
    dma = pltpu.SemaphoreType.DMA
    hop = vm((ROWS, 2 * GW), bf)
    result = pl.pallas_call(
        body,
        out_shape=jax.ShapeDtypeStruct((SHARE, 1, 2 * CH), jnp.float32),
        in_specs=[pl.BlockSpec(memory_space=pltpu.HBM)] * 7,
        out_specs=pl.BlockSpec(memory_space=pltpu.VMEM),
        scratch_shapes=[
            vm((TAPS * CH, 2 * CH), bf),
            vm((1, 12, 2, 12 * CH), bf),
            vm((CELLS, GW), bf),
            vm((TAPS * ROWS, ROWS), bf),
            vm((TAPS * ROWS, CELLS), bf),
            vm((TAPS * ROWS, 4 * ROWS), bf),
            vm((4 * ROWS, CELLS), bf),
            vm((2, TAPS * GW, GW), bf),
            vm((2, TAPS * GW, GW), bf),
            vm((2, 4 * ROWS, TAPS * GW), bf),
            vm((ROWS, 2 * GW), jnp.float32),
            vm((2, 4 * ROWS, GW), jnp.float32),
            vm((4 * ROWS, 2 * GW), bf),
            vm((TAPS * ROWS, 2 * GW), bf),
            vm((4 * ROWS, GW), jnp.float32),
            hop, hop, hop, hop, hop, hop,
            vm((4, 240, GW), bf),
            vm((4, ROWS, 2 * GW), bf),
            vm((4, ROWS, 2 * GW), bf),
            vm((4, 240, 2 * GW), bf),
            vm((3, 4 * ROWS, 2 * GW), bf),
            vm((976, 2 * GW), jnp.float32),
            vm((16, SLOT, 2 * CH), bf),
            vm((4, 4, SLOT, 2 * CH), bf),
            vm((4, SLOT, 2 * CH), jnp.float32),
            vm((4, SLOT, 2 * CH), bf),
            vm((4, SLOT, 2 * CH), bf),
            dma((8,)), dma((4,)), dma((4,)),
            dma((4,)), dma((4,)), dma((4,)), dma((4,)), dma((4,)), dma((4,)), dma((4,)), dma((4,)),
        ],
        compiler_params=pltpu.CompilerParams(
            collective_id=0, has_side_effects=True, vmem_limit_bytes=63 * 1024 * 1024
        ),
    )(by_rows(images), by_rows(targets), kernels, *consts)
    return jnp.transpose(result, (1, 0, 2))


def solution(mesh):
    return jax.shard_map(
        on_device,
        mesh=mesh,
        in_specs=(P(None, "dp", None, None), P(None, "dp", None, None), P("section", None, None)),
        out_specs=P("section", "dp", None),
        check_vma=False,
    )
```

```python
import jax
import jax.numpy as jnp
import numpy as np
from jax import lax
from jax.experimental import pallas as pl
from jax.experimental.pallas import tpu as pltpu
from jax.sharding import PartitionSpec as P

MESH = pl.DeviceIdType.MESH
ROWS = 80
CH = 320
GW = 384
TAPS = 9
SHARE = 45
SLOT = 48
CELLS = 12 * 32


def phase_shift(phase, tap):
    alpha, beta = divmod(phase, 2)
    a, b = divmod(tap, 3)
    return ((alpha + a - 1) // 2 + 1) * 3 + ((beta + b - 1) // 2 + 1)


def tables():
    shift = np.zeros((TAPS, ROWS, ROWS), np.float32)
    encode = np.zeros((TAPS, ROWS, CELLS), np.float32)
    order = np.zeros((4, ROWS, CELLS), np.float32)
    for n in range(2):
        for i in range(6):
            for j in range(6):
                r = n * 36 + i * 6 + j
                for tap in range(TAPS):
                    a, b = divmod(tap, 3)
                    ii, jj = i + a - 1, j + b - 1
                    if 0 <= ii < 6 and 0 <= jj < 6:
                        shift[tap, r, n * 36 + ii * 6 + jj] = 1
                    ii, jj = 2 * i + a - 1, 2 * j + b - 1
                    if 0 <= ii < 12 and 0 <= jj < 12:
                        encode[tap, r, jj * 32 + n * 16 + ii] = 1
                for phase in range(4):
                    alpha, beta = divmod(phase, 2)
                    order[phase, r, (2 * j + beta) * 32 + n * 16 + 2 * i + alpha] = 1
    fold = np.zeros((TAPS, ROWS, 4, ROWS), np.float32)
    for tap in range(TAPS):
        for phase in range(4):
            fold[tap, :, phase, :] = shift[phase_shift(phase, tap)].T
    return (
        shift.reshape(TAPS * ROWS, ROWS),
        encode.reshape(TAPS * ROWS, CELLS),
        fold.reshape(TAPS * ROWS, 4 * ROWS),
        order.reshape(4 * ROWS, CELLS),
    )


def silu(v):
    return v * jax.nn.sigmoid(v)


def silu_slope(v):
    g = jax.nn.sigmoid(v)
    return g * (1.0 + v * (1.0 - g))


def mm(a, b):
    return jnp.dot(a, b, preferred_element_type=jnp.float32)


def mm_nt(a, b):
    return lax.dot_general(a, b, (((1,), (1,)), ((), ())), preferred_element_type=jnp.float32)


def remote(src, dst, send_sem, recv_sem, device):
    return pltpu.make_async_remote_copy(
        src_ref=src, dst_ref=dst, send_sem=send_sem, recv_sem=recv_sem, device_id=device, device_id_type=MESH
    )


def body(
    img, tgt, ker, c_shift, c_encode, c_fold, c_order, out,
    w_in, raw, x_in, s_shift, s_encode, s_fold, s_order,
    wp, wt, feat, act, pre, target, zed,
    h_in, skip_in, g_in, gskip_in, h_out, g_out,
    gx, gh, gd, gd3, taps, select, left, pack, r_buf, r_sum, z_out, z_buf,
    load_sem, hop_send, hop_recv, a_send, a_recv, d_send, d_recv, r_send, r_recv, z_send, z_recv,
):
    bf = jnp.bfloat16
    f32 = jnp.float32
    sec = lax.axis_index("section")
    dp = lax.axis_index("dp")
    x, y, z = dp // 16, (dp // 4) % 4, dp % 4

    def x_peer(k):
        return {"dp": (x + k) % 4 * 16 + y * 4 + z}

    def y_peer(k):
        return {"dp": x * 16 + (y + k) % 4 * 4 + z}

    def z_peer(k):
        return {"dp": x * 16 + y * 4 + (z + k) % 4}

    gather_peer = (x_peer, y_peer)
    reduce_peer = (y_peer, x_peer)

    def load(src, dst, n):
        return pltpu.make_async_copy(src, dst, load_sem.at[n])

    w_loads = []
    for n, (first, last) in enumerate(((0, GW), (GW, 2 * CH))):
        for i in range(3):
            part = (slice(i * 960, (i + 1) * 960), slice(first, last))
            w_loads.append(load(ker.at[(0, *part)], w_in.at[part], 4 + 3 * n + i))
    x_load = load(img, raw, 0)
    e_load = load(c_encode, s_encode, 1)

    @pl.when(sec == 0)
    def first_loads():
        x_load.start()
        e_load.start()

    for copy in w_loads:
        copy.start()

    barrier = pltpu.get_barrier_semaphore()
    for k in range(1, 4):
        pl.semaphore_signal(barrier, inc=1, device_id={"section": (sec + k) % 4}, device_id_type=MESH)
        for peer in (x_peer, y_peer, z_peer):
            pl.semaphore_signal(barrier, inc=1, device_id=peer(k), device_id_type=MESH)

    def arrive():
        pl.semaphore_wait(barrier, 12)

    def spread(src, buf, send, recv, g):
        copies = []
        for k in (1, 3, 2):
            copy = remote(src, buf.at[g, 4 - k], send.at[g, k], recv.at[g, 4 - k], gather_peer[g](k))
            copy.start()
            copies.append(copy)
        return copies

    def spread_wait(src, buf, send, recv, g, k):
        remote(src, buf.at[g, k], send.at[g, k], recv.at[g, k], gather_peer[g](k)).wait_recv()

    def hop(kind, src, dst, g, to):
        return remote(src.at[g], dst.at[g], hop_send.at[kind, g], hop_recv.at[kind, g], {"section": to})

    def rows_of(t, n=ROWS):
        return slice(t * n, (t + 1) * n)

    def pack_weights():
        lane = lax.broadcasted_iota(jnp.int32, (CH, GW), 1)

        def one(t, carry):
            rows = pl.ds(pl.multiple_of(t * CH, 16), CH)
            base = pl.multiple_of(t * GW, 16)
            first = w_in[rows, 0:GW].astype(f32)
            wp[0, pl.ds(base, CH), :] = jnp.where(lane < CH, first, 0.0).astype(bf)
            second = pltpu.roll(w_in[rows, 256:640].astype(f32), GW - 64, 1)
            wp[1, pl.ds(base, CH), :] = jnp.where(lane < CH, second, 0.0).astype(bf)
            for g in range(2):
                wp[g, pl.ds(base + CH, GW - CH), :] = jnp.zeros((GW - CH, GW), bf)
            return carry

        lax.fori_loop(0, TAPS, one, 0)

    def turn_weights():
        def one(t, carry):
            rows = pl.ds(pl.multiple_of(t * GW, 16), GW)
            for g in range(2):
                wt[g, rows, :] = wp[g, rows, :].T
            return carry

        lax.fori_loop(0, TAPS, one, 0)

    def lay_out_cells():
        x_in[...] = jnp.zeros((CELLS, GW), bf)
        lane = lax.broadcasted_iota(jnp.int32, (12, GW), 1)
        for n in range(2):
            for j in range(12):
                start = j * CH - 64 * (j % 2)
                part = raw[0, :, n, start:start + GW].astype(f32)
                if j % 2:
                    part = pltpu.roll(part, GW - 64, 1)
                x_in[j * 32 + n * 16:j * 32 + n * 16 + 12, :] = jnp.where(lane < CH, part, 0.0).astype(bf)

    def make_select():
        lane = lax.broadcasted_iota(jnp.int32, (SLOT, GW), 1)
        row = lax.broadcasted_iota(jnp.int32, (SLOT, GW), 0)
        for j in range(4):
            value = row - lane + SHARE * ((z + j) % 4)
            select[rows_of(j, SLOT), :] = jnp.where((row < SHARE) & (lane < CH), value, -100000)

    def block_start(g, k):
        return 720 * x + 180 * ((y + k) % 4) if g == 0 else 720 * ((x + k) % 4) + 180 * y

    def block_tap(g, k, i):
        return jnp.minimum(block_start(g, k) // CH + i, TAPS - 1)

    def block_rows(g, k, i, source):
        start = block_start(g, k)
        chosen = select[...] == CH * (start // CH + i) - start
        return mm_nt(jnp.where(chosen, 1.0, 0.0).astype(bf), source)

    def make_left(g):
        for k in range(4):
            rows = sum(block_rows(g, k, i, taps[block_tap(g, k, i)]) for i in range(2))
            left[0, g, rows_of(k, 4 * SLOT), :] = rows.astype(bf)

    def fill_taps(k, table, source):
        part = mm(table, source).astype(bf)
        for t in range(TAPS):
            taps[t, rows_of(k), :] = part[rows_of(t)]

    def hand_block(g, k, block):
        if k == 0:
            r_sum[g] = block
            return []
        pack[g, k] = block.astype(bf)
        copy = remote(pack.at[g, k], r_buf.at[g, 4 - k], r_send.at[g, k], r_recv.at[g, 4 - k], reduce_peer[g](k))
        copy.start()
        return [copy]

    def gradient(g):
        copies = []
        for k in (1, 3, 2):
            spread_wait(gd.at[g, 0], gd, d_send, d_recv, g, k)
        right = gd[g].reshape(4 * ROWS, GW)
        for k in (2, 1, 3, 0):
            copies += hand_block(g, k, mm(left[0, g, rows_of(k, 4 * SLOT), :], right))
        return copies

    @pl.when(sec == 0)
    def encoder():
        x_load.wait()
        lay_out_cells()
        e_load.wait()
        zed[...] = mm(s_encode[...], x_in[...]).astype(bf)
        lane = lax.broadcasted_iota(jnp.int32, (ROWS, GW), 1)
        sends = []
        for g in range(2):
            acc = jnp.zeros((ROWS, GW), f32)
            for t in range(TAPS):
                if t % 3 == 0:
                    w_loads[3 * g + t // 3].wait()
                acc = acc + mm(zed[rows_of(t), 0:CH], w_in[rows_of(t, CH), g * 256:g * 256 + GW])
            if g:
                acc = pltpu.roll(acc, GW - 64, 1)
            acc = jnp.where(lane < CH, acc, 0.0)
            act[g] = acc
            h_out[g] = silu(acc).astype(bf)
            if g == 0:
                arrive()
            for copy in (hop(0, h_out, h_in, g, 1), hop(1, h_out, skip_in, g, 3)):
                copy.start()
                sends.append(copy)
        for g in range(2):
            sends += spread(x_in, gx, a_send, a_recv, g)
        make_select()
        for g in range(2):
            for t in range(TAPS):
                taps[t, rows_of(0), :] = zed[rows_of(t)]
            for k in (1, 3, 2):
                spread_wait(x_in, gx, a_send, a_recv, g, k)
                fill_taps(k, s_encode[...], gx[g, k])
            make_left(g)
        for g in range(2):
            hop(3, g_out, gskip_in, g, 3).wait_recv()
            hop(2, g_out, g_in, g, 1).wait_recv()
            total = g_in[g].astype(f32) + gskip_in[g].astype(f32)
            gd[g, 0] = (total * silu_slope(act[g])).astype(bf)
            sends += spread(gd.at[g, 0], gd, d_send, d_recv, g)
        for g in range(2):
            sends += gradient(g)
        for copy in sends:
            copy.wait_send()

    @pl.when((sec == 1) | (sec == 2))
    def centre():
        s_load = load(c_shift, s_shift, 2)
        s_load.start()
        for copy in w_loads:
            copy.wait()
        pack_weights()
        s_load.wait()

        @pl.when(sec == 2)
        def turn_early():
            turn_weights()

        arrive()
        sends = []
        for g in range(2):
            hop(0, h_out, h_in, g, sec - 1).wait_recv()
            shifted = mm(s_shift[...], h_in[g]).astype(bf)
            acc = jnp.zeros((ROWS, GW), f32)
            for t in range(TAPS):
                acc = acc + mm(shifted[rows_of(t)], wp[g, rows_of(t, GW), :])
            act[g] = acc
            h_out[g] = (h_in[g].astype(f32) + silu(acc)).astype(bf)
            copy = hop(0, h_out, h_in, g, sec + 1)
            copy.start()
            sends.append(copy)
        for g in range(2):
            sends += spread(h_in.at[g], gh, a_send, a_recv, g)

        @pl.when(sec == 1)
        def turn_late():
            turn_weights()

        make_select()

        def prepare(g):
            fill_taps(0, s_shift[...], h_in[g])
            for k in (1, 3, 2):
                spread_wait(h_in.at[g], gh, a_send, a_recv, g, k)
                fill_taps(k, s_shift[...], gh[g, k])
            make_left(g)

        prepare(0)

        @pl.when(sec == 1)
        def prepare_early():
            prepare(1)

        for g in range(2):
            hop(2, g_out, g_in, g, sec + 1).wait_recv()
            delta = (g_in[g].astype(f32) * silu_slope(act[g])).astype(bf)
            gd[g, 0] = delta
            back = mm(s_shift[...], delta).astype(bf)
            acc = g_in[g].astype(f32)
            for t in range(TAPS):
                acc = acc + mm(back[rows_of(8 - t)], wt[g, rows_of(t, GW), :])
            g_out[g] = acc.astype(bf)
            copy = hop(2, g_out, g_in, g, sec - 1)
            copy.start()
            sends.append(copy)
            sends += spread(gd.at[g, 0], gd, d_send, d_recv, g)

        @pl.when(sec == 2)
        def prepare_late():
            prepare(1)

        for g in range(2):
            sends += gradient(g)
        for copy in sends:
            copy.wait_send()

    @pl.when(sec == 3)
    def decoder():
        loads = [load(c_shift, s_shift, 2), load(c_fold, s_fold, 3), load(c_order, s_order, 1), load(tgt, raw, 0)]
        for copy in loads:
            copy.start()
        for copy in w_loads:
            copy.wait()
        pack_weights()
        turn_weights()
        for copy in loads:
            copy.wait()
        lay_out_cells()
        target[...] = mm(s_order[...], x_in[...])
        make_select()
        arrive()
        sends = []
        for g in range(2):
            hop(1, h_out, skip_in, g, 0).wait_recv()
            hop(0, h_out, h_in, g, 2).wait_recv()
            u = (h_in[g].astype(f32) + skip_in[g].astype(f32)).astype(bf)
            gh[g, 0] = u
            sends += spread(gh.at[g, 0], gh, a_send, a_recv, g)
            shifted = mm(s_shift[...], u).astype(bf)
            for phase in range(4):
                for t in range(TAPS):
                    feat[g, rows_of(phase), rows_of(t, GW)] = shifted[rows_of(phase_shift(phase, t))]
            pre[g] = mm(feat[g], wp[g])
        value, gate = pre[0], pre[1]
        sig = jax.nn.sigmoid(gate)
        act_gate = gate * sig
        residual = (value * act_gate - target[...]) * (1.0 / 128.0)
        gd3[0, 0] = (residual * act_gate).astype(bf)
        gd3[1, 0] = (residual * value * (sig * (1.0 + gate * (1.0 - sig)))).astype(bf)
        for g in range(2):
            sends += spread(gd3.at[g, 0], gd3, d_send, d_recv, g)
        for g in range(2):
            back = mm(s_fold[...], gd3[g, 0]).astype(bf)
            acc = jnp.zeros((ROWS, GW), f32)
            for t in range(TAPS):
                acc = acc + mm(back[rows_of(t)], wt[g, rows_of(t, GW), :])
            g_out[g] = acc.astype(bf)
            for copy in (hop(2, g_out, g_in, g, 2), hop(3, g_out, gskip_in, g, 0)):
                copy.start()
                sends.append(copy)
        for g in range(2):
            for k in (1, 3, 2):
                spread_wait(gh.at[g, 0], gh, a_send, a_recv, g, k)
            source = gh[g].reshape(4 * ROWS, GW)
            for k in range(4):
                for i in range(2):
                    left[i, g, rows_of(k, 4 * SLOT), :] = block_rows(g, k, i, source).astype(bf)
        for g in range(2):
            fill_taps(0, s_fold[...], gd3[g, 0])
            for k in (1, 3, 2):
                spread_wait(gd3.at[g, 0], gd3, d_send, d_recv, g, k)
                fill_taps(k, s_fold[...], gd3[g, k])
            for k in (2, 1, 3, 0):
                block = sum(mm(left[i, g, rows_of(k, 4 * SLOT), :], taps[block_tap(g, k, i)]) for i in range(2))
                sends += hand_block(g, k, block)
        for copy in sends:
            copy.wait_send()

    sends = []
    for g in range(2):
        for k in (1, 3, 2):
            remote(pack.at[g, k], r_buf.at[g, k], r_send.at[g, k], r_recv.at[g, k], reduce_peer[g](k)).wait_recv()
        r_sum[g] = r_sum[g] + r_buf[g, 1].astype(f32) + r_buf[g, 2].astype(f32) + r_buf[g, 3].astype(f32)
        z_out[g] = r_sum[g].astype(bf)
        for k in (2, 1, 3):
            copy = remote(z_out.at[g, rows_of(k, SLOT)], z_buf.at[g, 4 - k], z_send.at[g, k], z_recv.at[g, 4 - k], z_peer(k))
            copy.start()
            sends.append(copy)
    halves = []
    for g in range(2):
        total = r_sum[g, 0:SLOT, :]
        for k in (1, 3, 2):
            remote(z_out.at[g, rows_of(k, SLOT)], z_buf.at[g, k], z_send.at[g, k], z_recv.at[g, k], z_peer(k)).wait_recv()
            total = total + z_buf[g, k].astype(f32)
        halves.append(jnp.concatenate([total, jnp.zeros((SLOT, 256), f32)], axis=1))
    whole = halves[0] + pltpu.roll(halves[1], CH, 1)
    out[:, 0, :] = whole[0:SHARE]
    for copy in sends:
        copy.wait_send()


def on_device(images, targets, kernels):
    bf = jnp.bfloat16

    def by_rows(grids):
        return jnp.transpose(grids, (1, 2, 0, 3))

    consts = [jnp.asarray(t, bf) for t in tables()]
    vm = pltpu.VMEM
    dma = pltpu.SemaphoreType.DMA
    hop = vm((2, ROWS, GW), bf)
    result = pl.pallas_call(
        body,
        out_shape=jax.ShapeDtypeStruct((SHARE, 1, 2 * CH), jnp.float32),
        in_specs=[pl.BlockSpec(memory_space=pltpu.HBM)] * 7,
        out_specs=pl.BlockSpec(memory_space=pltpu.VMEM),
        scratch_shapes=[
            vm((TAPS * CH, 2 * CH), bf),
            vm((1, 12, 2, 12 * CH), bf),
            vm((CELLS, GW), bf),
            vm((TAPS * ROWS, ROWS), bf),
            vm((TAPS * ROWS, CELLS), bf),
            vm((TAPS * ROWS, 4 * ROWS), bf),
            vm((4 * ROWS, CELLS), bf),
            vm((2, TAPS * GW, GW), bf),
            vm((2, TAPS * GW, GW), bf),
            vm((2, 4 * ROWS, TAPS * GW), bf),
            vm((2, ROWS, GW), jnp.float32),
            vm((2, 4 * ROWS, GW), jnp.float32),
            vm((4 * ROWS, GW), jnp.float32),
            vm((TAPS * ROWS, GW), bf),
            hop, hop, hop, hop, hop, hop,
            vm((2, 4, CELLS, GW), bf),
            vm((2, 4, ROWS, GW), bf),
            vm((2, 4, ROWS, GW), bf),
            vm((2, 4, 4 * ROWS, GW), bf),
            vm((TAPS, 4 * ROWS, GW), bf),
            vm((4 * SLOT, GW), jnp.int32),
            vm((2, 2, 16 * SLOT, 4 * ROWS), bf),
            vm((2, 4, 4 * SLOT, GW), bf),
            vm((2, 4, 4 * SLOT, GW), bf),
            vm((2, 4 * SLOT, GW), jnp.float32),
            vm((2, 4 * SLOT, GW), bf),
            vm((2, 4, SLOT, GW), bf),
            dma((10,)), dma((4, 2)), dma((4, 2)),
            dma((2, 4)), dma((2, 4)), dma((2, 4)), dma((2, 4)), dma((2, 4)), dma((2, 4)), dma((2, 4)), dma((2, 4)),
        ],
        compiler_params=pltpu.CompilerParams(
            collective_id=0, has_side_effects=True, vmem_limit_bytes=63 * 1024 * 1024
        ),
    )(by_rows(images), by_rows(targets), kernels, *consts)
    return jnp.transpose(result, (1, 0, 2))


def solution(mesh):
    return jax.shard_map(
        on_device,
        mesh=mesh,
        in_specs=(P(None, "dp", None, None), P(None, "dp", None, None), P("section", None, None)),
        out_specs=P("section", "dp", None),
        check_vma=False,
    )
```

```python
import jax
import jax.numpy as jnp
import numpy as np
from jax import lax
from jax.experimental import pallas as pl
from jax.experimental.pallas import tpu as pltpu
from jax.sharding import PartitionSpec as P

MESH = pl.DeviceIdType.MESH
ROWS = 80
CH = 320
GW = 384
TAPS = 9
SHARE = 45
SLOT = 48
CELLS = 12 * 32


def phase_shift(phase, tap):
    alpha, beta = divmod(phase, 2)
    a, b = divmod(tap, 3)
    return ((alpha + a - 1) // 2 + 1) * 3 + ((beta + b - 1) // 2 + 1)


def tables():
    shift = np.zeros((TAPS, ROWS, ROWS), np.float32)
    encode = np.zeros((TAPS, ROWS, CELLS), np.float32)
    order = np.zeros((4, ROWS, CELLS), np.float32)
    for n in range(2):
        for i in range(6):
            for j in range(6):
                r = n * 36 + i * 6 + j
                for tap in range(TAPS):
                    a, b = divmod(tap, 3)
                    ii, jj = i + a - 1, j + b - 1
                    if 0 <= ii < 6 and 0 <= jj < 6:
                        shift[tap, r, n * 36 + ii * 6 + jj] = 1
                    ii, jj = 2 * i + a - 1, 2 * j + b - 1
                    if 0 <= ii < 12 and 0 <= jj < 12:
                        encode[tap, r, jj * 32 + n * 16 + ii] = 1
                for phase in range(4):
                    alpha, beta = divmod(phase, 2)
                    order[phase, r, (2 * j + beta) * 32 + n * 16 + 2 * i + alpha] = 1
    fold = np.zeros((TAPS, ROWS, 4, ROWS), np.float32)
    for tap in range(TAPS):
        for phase in range(4):
            fold[tap, :, phase, :] = shift[phase_shift(phase, tap)].T
    return (
        shift.reshape(TAPS * ROWS, ROWS),
        encode.reshape(TAPS * ROWS, CELLS),
        fold.reshape(TAPS * ROWS, 4 * ROWS),
        order.reshape(4 * ROWS, CELLS),
    )


def silu(v):
    return v * jax.nn.sigmoid(v)


def silu_slope(v):
    g = jax.nn.sigmoid(v)
    return g * (1.0 + v * (1.0 - g))


def mm(a, b):
    return jnp.dot(a, b, preferred_element_type=jnp.float32)


def mm_nt(a, b):
    return lax.dot_general(a, b, (((1,), (1,)), ((), ())), preferred_element_type=jnp.float32)


def remote(src, dst, send_sem, recv_sem, device):
    return pltpu.make_async_remote_copy(
        src_ref=src, dst_ref=dst, send_sem=send_sem, recv_sem=recv_sem, device_id=device, device_id_type=MESH
    )


def body(
    img, tgt, ker, c_shift, c_encode, c_fold, c_order, out,
    w_in, raw, x_in, s_shift, s_encode, s_fold, s_order,
    wp, wt, feat, act, pre, target, zed,
    h_in, skip_in, g_in, gskip_in, h_out, g_out,
    gx, gh, gd, gd3, taps, select, left, pack, r_buf, r_sum, z_out, z_buf,
    load_sem, hop_send, hop_recv, a_send, a_recv, d_send, d_recv, r_send, r_recv, z_send, z_recv,
):
    bf = jnp.bfloat16
    f32 = jnp.float32
    sec = lax.axis_index("section")
    dp = lax.axis_index("dp")
    x, y, z = dp // 16, (dp // 4) % 4, dp % 4

    def x_peer(k):
        return {"dp": (x + k) % 4 * 16 + y * 4 + z}

    def y_peer(k):
        return {"dp": x * 16 + (y + k) % 4 * 4 + z}

    def z_peer(k):
        return {"dp": x * 16 + y * 4 + (z + k) % 4}

    gather_peer = (x_peer, y_peer)
    reduce_peer = (y_peer, x_peer)

    def load(src, dst, n):
        return pltpu.make_async_copy(src, dst, load_sem.at[n])

    w_loads = []
    for n, (first, last) in enumerate(((0, GW), (GW, 2 * CH))):
        for i in range(3):
            part = (slice(i * 960, (i + 1) * 960), slice(first, last))
            w_loads.append(load(ker.at[(0, *part)], w_in.at[part], 4 + 3 * n + i))
    x_load = load(img, raw, 0)
    e_load = load(c_encode, s_encode, 1)

    @pl.when(sec == 0)
    def first_loads():
        x_load.start()
        e_load.start()

    for copy in w_loads:
        copy.start()

    barrier = pltpu.get_barrier_semaphore()
    for k in range(1, 4):
        pl.semaphore_signal(barrier, inc=1, device_id={"section": (sec + k) % 4}, device_id_type=MESH)
        for peer in (x_peer, y_peer, z_peer):
            pl.semaphore_signal(barrier, inc=1, device_id=peer(k), device_id_type=MESH)

    def arrive():
        pl.semaphore_wait(barrier, 12)

    def spread(src, buf, send, recv, g):
        copies = []
        for k in (1, 3, 2):
            copy = remote(src, buf.at[g, 4 - k], send.at[g, k], recv.at[g, 4 - k], gather_peer[g](k))
            copy.start()
            copies.append(copy)
        return copies

    def spread_wait(src, buf, send, recv, g, k):
        remote(src, buf.at[g, k], send.at[g, k], recv.at[g, k], gather_peer[g](k)).wait_recv()

    def hop(kind, src, dst, g, to):
        return remote(src.at[g], dst.at[g], hop_send.at[kind, g], hop_recv.at[kind, g], {"section": to})

    def rows_of(t, n=ROWS):
        return slice(t * n, (t + 1) * n)

    def pack_weights():
        lane = lax.broadcasted_iota(jnp.int32, (CH, GW), 1)

        def one(t, carry):
            rows = pl.ds(pl.multiple_of(t * CH, 16), CH)
            base = pl.multiple_of(t * GW, 16)
            first = w_in[rows, 0:GW].astype(f32)
            wp[0, pl.ds(base, CH), :] = jnp.where(lane < CH, first, 0.0).astype(bf)
            second = pltpu.roll(w_in[rows, 256:640].astype(f32), GW - 64, 1)
            wp[1, pl.ds(base, CH), :] = jnp.where(lane < CH, second, 0.0).astype(bf)
            for g in range(2):
                wp[g, pl.ds(base + CH, GW - CH), :] = jnp.zeros((GW - CH, GW), bf)
            return carry

        lax.fori_loop(0, TAPS, one, 0)

    def turn_weights():
        def one(t, carry):
            rows = pl.ds(pl.multiple_of(t * GW, 16), GW)
            for g in range(2):
                wt[g, rows, :] = wp[g, rows, :].T
            return carry

        lax.fori_loop(0, TAPS, one, 0)

    def lay_out_cells():
        x_in[...] = jnp.zeros((CELLS, GW), bf)
        lane = lax.broadcasted_iota(jnp.int32, (12, GW), 1)
        for n in range(2):
            for j in range(12):
                start = j * CH - 64 * (j % 2)
                part = raw[0, :, n, start:start + GW].astype(f32)
                if j % 2:
                    part = pltpu.roll(part, GW - 64, 1)
                x_in[j * 32 + n * 16:j * 32 + n * 16 + 12, :] = jnp.where(lane < CH, part, 0.0).astype(bf)

    def make_select():
        lane = lax.broadcasted_iota(jnp.int32, (SLOT, GW), 1)
        row = lax.broadcasted_iota(jnp.int32, (SLOT, GW), 0)
        for j in range(4):
            value = row - lane + SHARE * ((z + j) % 4)
            select[rows_of(j, SLOT), :] = jnp.where((row < SHARE) & (lane < CH), value, -100000)

    def block_start(g, k):
        return 720 * x + 180 * ((y + k) % 4) if g == 0 else 720 * ((x + k) % 4) + 180 * y

    def block_tap(g, k, i):
        return jnp.minimum(block_start(g, k) // CH + i, TAPS - 1)

    def block_rows(g, k, i, source):
        start = block_start(g, k)
        chosen = select[...] == CH * (start // CH + i) - start
        return mm_nt(jnp.where(chosen, 1.0, 0.0).astype(bf), source)

    def make_left(g):
        for k in range(4):
            rows = sum(block_rows(g, k, i, taps[block_tap(g, k, i)]) for i in range(2))
            left[0, g, rows_of(k, 4 * SLOT), :] = rows.astype(bf)

    def fill_taps(k, table, source):
        part = mm(table, source).astype(bf)
        for t in range(TAPS):
            taps[t, rows_of(k), :] = part[rows_of(t)]

    def half_lanes(first, second):
        return jnp.where(lax.broadcasted_iota(jnp.int32, first.shape, 1) < 64, first, pltpu.roll(second, 64, 1))

    def squeeze(block):
        last = [block[rows_of(j, SLOT), 256:GW] for j in range(4)]
        side = jnp.concatenate([half_lanes(last[0], last[1]), half_lanes(last[2], last[3])], axis=1)
        return jnp.concatenate([block[:, 0:256], side], axis=0)

    def z_slot(j):
        side = slice(4 * SLOT, 5 * SLOT), slice(128 * (j // 2), 128 * (j // 2) + 128)
        first, second = r_sum[(0, *side)], r_sum[(1, *side)]
        if j % 2:
            first = pltpu.roll(first, 64, 1)
            second = pltpu.roll(second, 64, 1)
        return jnp.concatenate([r_sum[0, rows_of(j, SLOT), :], r_sum[1, rows_of(j, SLOT), :], half_lanes(first, second)], axis=1)

    def hand_block(g, k, block):
        if k == 0:
            r_sum[g] = squeeze(block)
            return []
        pack[g, k] = squeeze(block).astype(bf)
        copy = remote(pack.at[g, k], r_buf.at[g, 4 - k], r_send.at[g, k], r_recv.at[g, 4 - k], reduce_peer[g](k))
        copy.start()
        return [copy]

    def gradient(g):
        copies = []
        for k in (1, 3, 2):
            spread_wait(gd.at[g, 0], gd, d_send, d_recv, g, k)
        right = gd[g].reshape(4 * ROWS, GW)
        for k in (2, 1, 3, 0):
            copies += hand_block(g, k, mm(left[0, g, rows_of(k, 4 * SLOT), :], right))
        return copies

    @pl.when(sec == 0)
    def encoder():
        x_load.wait()
        lay_out_cells()
        e_load.wait()
        zed[...] = mm(s_encode[...], x_in[...]).astype(bf)
        lane = lax.broadcasted_iota(jnp.int32, (ROWS, GW), 1)
        sends = []
        for g in range(2):
            acc = jnp.zeros((ROWS, GW), f32)
            for t in range(TAPS):
                if t % 3 == 0:
                    w_loads[3 * g + t // 3].wait()
                acc = acc + mm(zed[rows_of(t), 0:CH], w_in[rows_of(t, CH), g * 256:g * 256 + GW])
            if g:
                acc = pltpu.roll(acc, GW - 64, 1)
            acc = jnp.where(lane < CH, acc, 0.0)
            act[g] = acc
            h_out[g] = silu(acc).astype(bf)
            if g == 0:
                arrive()
            for copy in (hop(0, h_out, h_in, g, 1), hop(1, h_out, skip_in, g, 3)):
                copy.start()
                sends.append(copy)
        for g in range(2):
            sends += spread(x_in, gx, a_send, a_recv, g)
        make_select()
        for g in range(2):
            for t in range(TAPS):
                taps[t, rows_of(0), :] = zed[rows_of(t)]
            for k in (1, 3, 2):
                spread_wait(x_in, gx, a_send, a_recv, g, k)
                fill_taps(k, s_encode[...], gx[g, k])
            make_left(g)
        for g in range(2):
            hop(3, g_out, gskip_in, g, 3).wait_recv()
            hop(2, g_out, g_in, g, 1).wait_recv()
            total = g_in[g].astype(f32) + gskip_in[g].astype(f32)
            gd[g, 0] = (total * silu_slope(act[g])).astype(bf)
            sends += spread(gd.at[g, 0], gd, d_send, d_recv, g)
        for g in range(2):
            sends += gradient(g)
        for copy in sends:
            copy.wait_send()

    @pl.when((sec == 1) | (sec == 2))
    def centre():
        s_load = load(c_shift, s_shift, 2)
        s_load.start()
        for copy in w_loads:
            copy.wait()
        pack_weights()
        s_load.wait()

        @pl.when(sec == 2)
        def turn_early():
            turn_weights()

        arrive()
        sends = []
        for g in range(2):
            hop(0, h_out, h_in, g, sec - 1).wait_recv()
            shifted = mm(s_shift[...], h_in[g]).astype(bf)
            acc = jnp.zeros((ROWS, GW), f32)
            for t in range(TAPS):
                acc = acc + mm(shifted[rows_of(t)], wp[g, rows_of(t, GW), :])
            act[g] = acc
            h_out[g] = (h_in[g].astype(f32) + silu(acc)).astype(bf)
            copy = hop(0, h_out, h_in, g, sec + 1)
            copy.start()
            sends.append(copy)
        for g in range(2):
            sends += spread(h_in.at[g], gh, a_send, a_recv, g)

        @pl.when(sec == 1)
        def turn_late():
            turn_weights()

        make_select()

        def prepare(g):
            fill_taps(0, s_shift[...], h_in[g])
            for k in (1, 3, 2):
                spread_wait(h_in.at[g], gh, a_send, a_recv, g, k)
                fill_taps(k, s_shift[...], gh[g, k])
            make_left(g)

        @pl.when(sec == 1)
        def prepare_early():
            for g in range(2):
                prepare(g)

        for g in range(2):
            hop(2, g_out, g_in, g, sec + 1).wait_recv()
            delta = (g_in[g].astype(f32) * silu_slope(act[g])).astype(bf)
            gd[g, 0] = delta
            back = mm(s_shift[...], delta).astype(bf)
            acc = g_in[g].astype(f32)
            for t in range(TAPS):
                acc = acc + mm(back[rows_of(8 - t)], wt[g, rows_of(t, GW), :])
            g_out[g] = acc.astype(bf)
            copy = hop(2, g_out, g_in, g, sec - 1)
            copy.start()
            sends.append(copy)
            sends += spread(gd.at[g, 0], gd, d_send, d_recv, g)

        @pl.when(sec == 2)
        def prepare_late():
            for g in range(2):
                prepare(g)

        for g in range(2):
            sends += gradient(g)
        for copy in sends:
            copy.wait_send()

    @pl.when(sec == 3)
    def decoder():
        loads = [load(c_shift, s_shift, 2), load(c_fold, s_fold, 3), load(c_order, s_order, 1), load(tgt, raw, 0)]
        for copy in loads:
            copy.start()
        for copy in w_loads:
            copy.wait()
        pack_weights()
        turn_weights()
        for copy in loads:
            copy.wait()
        lay_out_cells()
        target[...] = mm(s_order[...], x_in[...])
        make_select()
        arrive()
        sends = []
        for g in range(2):
            hop(1, h_out, skip_in, g, 0).wait_recv()
            hop(0, h_out, h_in, g, 2).wait_recv()
            u = (h_in[g].astype(f32) + skip_in[g].astype(f32)).astype(bf)
            gh[g, 0] = u
            sends += spread(gh.at[g, 0], gh, a_send, a_recv, g)
            shifted = mm(s_shift[...], u).astype(bf)
            for phase in range(4):
                for t in range(TAPS):
                    feat[g, rows_of(phase), rows_of(t, GW)] = shifted[rows_of(phase_shift(phase, t))]
            pre[g] = mm(feat[g], wp[g])
        value, gate = pre[0], pre[1]
        sig = jax.nn.sigmoid(gate)
        act_gate = gate * sig
        residual = (value * act_gate - target[...]) * (1.0 / 128.0)
        gd3[0, 0] = (residual * act_gate).astype(bf)
        gd3[1, 0] = (residual * value * (sig * (1.0 + gate * (1.0 - sig)))).astype(bf)
        for g in range(2):
            sends += spread(gd3.at[g, 0], gd3, d_send, d_recv, g)
        for g in range(2):
            back = mm(s_fold[...], gd3[g, 0]).astype(bf)
            acc = jnp.zeros((ROWS, GW), f32)
            for t in range(TAPS):
                acc = acc + mm(back[rows_of(t)], wt[g, rows_of(t, GW), :])
            g_out[g] = acc.astype(bf)
            for copy in (hop(2, g_out, g_in, g, 2), hop(3, g_out, gskip_in, g, 0)):
                copy.start()
                sends.append(copy)
        for g in range(2):
            for k in (1, 3, 2):
                spread_wait(gh.at[g, 0], gh, a_send, a_recv, g, k)
            source = gh[g].reshape(4 * ROWS, GW)
            for k in range(4):
                for i in range(2):
                    left[i, g, rows_of(k, 4 * SLOT), :] = block_rows(g, k, i, source).astype(bf)
        for g in range(2):
            fill_taps(0, s_fold[...], gd3[g, 0])
            for k in (1, 3, 2):
                spread_wait(gd3.at[g, 0], gd3, d_send, d_recv, g, k)
                fill_taps(k, s_fold[...], gd3[g, k])
            for k in (2, 1, 3, 0):
                block = sum(mm(left[i, g, rows_of(k, 4 * SLOT), :], taps[block_tap(g, k, i)]) for i in range(2))
                sends += hand_block(g, k, block)
        for copy in sends:
            copy.wait_send()

    sends = []
    for g in range(2):
        for k in (1, 3, 2):
            remote(pack.at[g, k], r_buf.at[g, k], r_send.at[g, k], r_recv.at[g, k], reduce_peer[g](k)).wait_recv()
        r_sum[g] = r_sum[g] + r_buf[g, 1].astype(f32) + r_buf[g, 2].astype(f32) + r_buf[g, 3].astype(f32)
    for k in (2, 1, 3):
        z_out[k] = z_slot(k).astype(bf)
        copy = remote(z_out.at[k], z_buf.at[4 - k], z_send.at[k], z_recv.at[4 - k], z_peer(k))
        copy.start()
        sends.append(copy)
    total = z_slot(0)
    for k in (1, 3, 2):
        remote(z_out.at[k], z_buf.at[k], z_send.at[k], z_recv.at[k], z_peer(k)).wait_recv()
        total = total + z_buf[k].astype(f32)
    lane = lax.broadcasted_iota(jnp.int32, (SLOT, GW), 1)
    side = total[:, 512:640]
    moved = pltpu.roll(jnp.concatenate([total[:, 256:512], side], axis=1), 64, 1)
    upper = jnp.where((lane < 64) | (lane >= CH), jnp.concatenate([side, side, side], axis=1), moved)
    out[:, 0, :] = jnp.concatenate([total[:, 0:256], upper], axis=1)[0:SHARE]
    for copy in sends:
        copy.wait_send()


def on_device(images, targets, kernels):
    bf = jnp.bfloat16

    def by_rows(grids):
        return jnp.transpose(grids, (1, 2, 0, 3))

    consts = [jnp.asarray(t, bf) for t in tables()]
    vm = pltpu.VMEM
    dma = pltpu.SemaphoreType.DMA
    hop = vm((2, ROWS, GW), bf)
    result = pl.pallas_call(
        body,
        out_shape=jax.ShapeDtypeStruct((SHARE, 1, 2 * CH), jnp.float32),
        in_specs=[pl.BlockSpec(memory_space=pltpu.HBM)] * 7,
        out_specs=pl.BlockSpec(memory_space=pltpu.VMEM),
        scratch_shapes=[
            vm((TAPS * CH, 2 * CH), bf),
            vm((1, 12, 2, 12 * CH), bf),
            vm((CELLS, GW), bf),
            vm((TAPS * ROWS, ROWS), bf),
            vm((TAPS * ROWS, CELLS), bf),
            vm((TAPS * ROWS, 4 * ROWS), bf),
            vm((4 * ROWS, CELLS), bf),
            vm((2, TAPS * GW, GW), bf),
            vm((2, TAPS * GW, GW), bf),
            vm((2, 4 * ROWS, TAPS * GW), bf),
            vm((2, ROWS, GW), jnp.float32),
            vm((2, 4 * ROWS, GW), jnp.float32),
            vm((4 * ROWS, GW), jnp.float32),
            vm((TAPS * ROWS, GW), bf),
            hop, hop, hop, hop, hop, hop,
            vm((2, 4, CELLS, GW), bf),
            vm((2, 4, ROWS, GW), bf),
            vm((2, 4, ROWS, GW), bf),
            vm((2, 4, 4 * ROWS, GW), bf),
            vm((TAPS, 4 * ROWS, GW), bf),
            vm((4 * SLOT, GW), jnp.int32),
            vm((2, 2, 16 * SLOT, 4 * ROWS), bf),
            vm((2, 4, 5 * SLOT, 256), bf),
            vm((2, 4, 5 * SLOT, 256), bf),
            vm((2, 5 * SLOT, 256), jnp.float32),
            vm((4, SLOT, 2 * CH), bf),
            vm((4, SLOT, 2 * CH), bf),
            dma((10,)), dma((4, 2)), dma((4, 2)),
            dma((2, 4)), dma((2, 4)), dma((2, 4)), dma((2, 4)), dma((2, 4)), dma((2, 4)), dma((4,)), dma((4,)),
        ],
        compiler_params=pltpu.CompilerParams(
            collective_id=0, has_side_effects=True, vmem_limit_bytes=63 * 1024 * 1024
        ),
    )(by_rows(images), by_rows(targets), kernels, *consts)
    return jnp.transpose(result, (1, 0, 2))


def solution(mesh):
    return jax.shard_map(
        on_device,
        mesh=mesh,
        in_specs=(P(None, "dp", None, None), P(None, "dp", None, None), P("section", None, None)),
        out_specs=P("section", "dp", None),
        check_vma=False,
    )
```

```python
import jax
import jax.numpy as jnp
import numpy as np
from jax import lax
from jax.experimental import pallas as pl
from jax.experimental.pallas import tpu as pltpu
from jax.sharding import PartitionSpec as P

MESH = pl.DeviceIdType.MESH
ROWS = 80
CH = 320
GW = 384
TAPS = 9
SHARE = 45
SLOT = 48
CELLS = 12 * 32


def phase_shift(phase, tap):
    alpha, beta = divmod(phase, 2)
    a, b = divmod(tap, 3)
    return ((alpha + a - 1) // 2 + 1) * 3 + ((beta + b - 1) // 2 + 1)


def tables():
    shift = np.zeros((TAPS, ROWS, ROWS), np.float32)
    encode = np.zeros((TAPS, ROWS, CELLS), np.float32)
    order = np.zeros((4, ROWS, CELLS), np.float32)
    for n in range(2):
        for i in range(6):
            for j in range(6):
                r = n * 36 + i * 6 + j
                for tap in range(TAPS):
                    a, b = divmod(tap, 3)
                    ii, jj = i + a - 1, j + b - 1
                    if 0 <= ii < 6 and 0 <= jj < 6:
                        shift[tap, r, n * 36 + ii * 6 + jj] = 1
                    ii, jj = 2 * i + a - 1, 2 * j + b - 1
                    if 0 <= ii < 12 and 0 <= jj < 12:
                        encode[tap, r, jj * 32 + n * 16 + ii] = 1
                for phase in range(4):
                    alpha, beta = divmod(phase, 2)
                    order[phase, r, (2 * j + beta) * 32 + n * 16 + 2 * i + alpha] = 1
    fold = np.zeros((TAPS, ROWS, 4, ROWS), np.float32)
    for tap in range(TAPS):
        for phase in range(4):
            fold[tap, :, phase, :] = shift[phase_shift(phase, tap)].T
    return (
        shift.reshape(TAPS * ROWS, ROWS),
        encode.reshape(TAPS * ROWS, CELLS),
        fold.reshape(TAPS * ROWS, 4 * ROWS),
        order.reshape(4 * ROWS, CELLS),
    )


def silu(v):
    return v * jax.nn.sigmoid(v)


def silu_slope(v):
    g = jax.nn.sigmoid(v)
    return g * (1.0 + v * (1.0 - g))


def mm(a, b):
    return jnp.dot(a, b, preferred_element_type=jnp.float32)


def mm_nt(a, b):
    return lax.dot_general(a, b, (((1,), (1,)), ((), ())), preferred_element_type=jnp.float32)


def remote(src, dst, send_sem, recv_sem, device):
    return pltpu.make_async_remote_copy(
        src_ref=src, dst_ref=dst, send_sem=send_sem, recv_sem=recv_sem, device_id=device, device_id_type=MESH
    )


def body(
    img, tgt, ker, c_shift, c_encode, c_fold, c_order, out,
    w_in, raw, x_in, s_shift, s_encode, s_fold, s_order,
    wp, wt, feat, act, pre, target, zed,
    h_in, skip_in, g_in, gskip_in, h_out, g_out,
    gx, gh, gd, gd3, g_act, g_skip, g_back, taps, select, left, pack, r_buf, r_sum, z_out, z_buf,
    load_sem, hop_send, hop_recv, a_send, a_recv, d_send, d_recv, c_send, c_recv, s_send, s_recv, b_send, b_recv,
    r_send, r_recv, z_send, z_recv,
):
    bf = jnp.bfloat16
    f32 = jnp.float32
    sec = lax.axis_index("section")
    dp = lax.axis_index("dp")
    x, y, z = dp // 16, (dp // 4) % 4, dp % 4

    def x_peer(k):
        return {"dp": (x + k) % 4 * 16 + y * 4 + z}

    def y_peer(k):
        return {"dp": x * 16 + (y + k) % 4 * 4 + z}

    def z_peer(k):
        return {"dp": x * 16 + y * 4 + (z + k) % 4}

    gather_peer = (x_peer, y_peer)
    reduce_peer = (y_peer, x_peer)

    def load(src, dst, n):
        return pltpu.make_async_copy(src, dst, load_sem.at[n])

    w_loads = []
    for n, (first, last) in enumerate(((0, GW), (GW, 2 * CH))):
        for i in range(3):
            part = (slice(i * 960, (i + 1) * 960), slice(first, last))
            w_loads.append(load(ker.at[(0, *part)], w_in.at[part], 4 + 3 * n + i))
    x_load = load(img, raw, 0)
    e_load = load(c_encode, s_encode, 1)

    @pl.when(sec == 0)
    def first_loads():
        x_load.start()
        e_load.start()

    for copy in w_loads:
        copy.start()

    barrier = pltpu.get_barrier_semaphore()
    for k in range(1, 4):
        pl.semaphore_signal(barrier, inc=1, device_id={"section": (sec + k) % 4}, device_id_type=MESH)
        for peer in (x_peer, y_peer, z_peer):
            pl.semaphore_signal(barrier, inc=1, device_id=peer(k), device_id_type=MESH)

    @pl.when(sec == 0)
    def greet_senders():
        for k in range(1, 4):
            for peer in (x_peer, y_peer):
                pl.semaphore_signal(barrier, inc=1, device_id={"section": 1, **peer(k)}, device_id_type=MESH)

    def arrive(more=0):
        pl.semaphore_wait(barrier, 12 + more)

    def spread(src, buf, send, recv, g):
        copies = []
        for k in (1, 3, 2):
            copy = remote(src, buf.at[g, 4 - k], send.at[g, k], recv.at[g, 4 - k], gather_peer[g](k))
            copy.start()
            copies.append(copy)
        return copies

    def spread_wait(src, buf, send, recv, g, k):
        remote(src, buf.at[g, k], send.at[g, k], recv.at[g, k], gather_peer[g](k)).wait_recv()

    def hop(kind, src, dst, g, to):
        return remote(src.at[g], dst.at[g], hop_send.at[kind, g], hop_recv.at[kind, g], {"section": to})

    def rows_of(t, n=ROWS):
        return slice(t * n, (t + 1) * n)

    def pack_weights():
        lane = lax.broadcasted_iota(jnp.int32, (CH, GW), 1)

        def one(t, carry):
            rows = pl.ds(pl.multiple_of(t * CH, 16), CH)
            base = pl.multiple_of(t * GW, 16)
            first = w_in[rows, 0:GW].astype(f32)
            wp[0, pl.ds(base, CH), :] = jnp.where(lane < CH, first, 0.0).astype(bf)
            second = pltpu.roll(w_in[rows, 256:640].astype(f32), GW - 64, 1)
            wp[1, pl.ds(base, CH), :] = jnp.where(lane < CH, second, 0.0).astype(bf)
            for g in range(2):
                wp[g, pl.ds(base + CH, GW - CH), :] = jnp.zeros((GW - CH, GW), bf)
            return carry

        lax.fori_loop(0, TAPS, one, 0)

    def turn_weights():
        def one(t, carry):
            rows = pl.ds(pl.multiple_of(t * GW, 16), GW)
            for g in range(2):
                wt[g, rows, :] = wp[g, rows, :].T
            return carry

        lax.fori_loop(0, TAPS, one, 0)

    def lay_out_cells(grids):
        lane = lax.broadcasted_iota(jnp.int32, (12, GW), 1)
        for n in range(2):
            for j in range(12):
                start = j * CH - 64 * (j % 2)
                part = grids[0, :, n, start:start + GW].astype(f32)
                if j % 2:
                    part = pltpu.roll(part, GW - 64, 1)
                x_in[j * 32 + n * 16:j * 32 + n * 16 + 12, :] = jnp.where(lane < CH, part, 0.0).astype(bf)

    def make_select():
        lane = lax.broadcasted_iota(jnp.int32, (SLOT, GW), 1)
        row = lax.broadcasted_iota(jnp.int32, (SLOT, GW), 0)
        for j in range(4):
            value = row - lane + SHARE * ((z + j) % 4)
            select[rows_of(j, SLOT), :] = jnp.where((row < SHARE) & (lane < CH), value, -100000)

    def block_start(g, k):
        return 720 * x + 180 * ((y + k) % 4) if g == 0 else 720 * ((x + k) % 4) + 180 * y

    def block_tap(g, k, i):
        return jnp.minimum(block_start(g, k) // CH + i, TAPS - 1)

    def block_rows(g, k, i, source):
        start = block_start(g, k)
        chosen = select[...] == CH * (start // CH + i) - start
        return mm_nt(jnp.where(chosen, 1.0, 0.0).astype(bf), source)

    def make_left(g):
        for k in range(4):
            rows = sum(block_rows(g, k, i, taps[block_tap(g, k, i)]) for i in range(2))
            left[0, g, rows_of(k, 4 * SLOT), :] = rows.astype(bf)

    def fill_taps(k, table, source):
        part = mm(table, source).astype(bf)
        for t in range(TAPS):
            taps[t, rows_of(k), :] = part[rows_of(t)]

    def half_lanes(first, second):
        return jnp.where(lax.broadcasted_iota(jnp.int32, first.shape, 1) < 64, first, pltpu.roll(second, 64, 1))

    def squeeze(block):
        last = [block[rows_of(j, SLOT), 256:GW] for j in range(4)]
        side = jnp.concatenate([half_lanes(last[0], last[1]), half_lanes(last[2], last[3])], axis=1)
        return jnp.concatenate([block[:, 0:256], side], axis=0)

    def z_slot(j):
        side = slice(4 * SLOT, 5 * SLOT), slice(128 * (j // 2), 128 * (j // 2) + 128)
        first, second = r_sum[(0, *side)], r_sum[(1, *side)]
        if j % 2:
            first = pltpu.roll(first, 64, 1)
            second = pltpu.roll(second, 64, 1)
        return jnp.concatenate([r_sum[0, rows_of(j, SLOT), :], r_sum[1, rows_of(j, SLOT), :], half_lanes(first, second)], axis=1)

    def hand_block(g, k, block):
        if k == 0:
            r_sum[g] = squeeze(block)
            return []
        pack[g, k] = squeeze(block).astype(bf)
        copy = remote(pack.at[g, k], r_buf.at[g, 4 - k], r_send.at[g, k], r_recv.at[g, 4 - k], reduce_peer[g](k))
        copy.start()
        return [copy]

    def gradient(g):
        copies = []
        right = gd[g].reshape(4 * ROWS, GW)
        for k in (2, 1, 3, 0):
            copies += hand_block(g, k, mm(left[0, g, rows_of(k, 4 * SLOT), :], right))
        return copies

    @pl.when(sec == 0)
    def encoder():
        x_in[...] = jnp.zeros((CELLS, GW), bf)
        x_load.wait()
        lay_out_cells(raw)
        e_load.wait()
        zed[...] = mm(s_encode[...], x_in[...]).astype(bf)
        lane = lax.broadcasted_iota(jnp.int32, (ROWS, GW), 1)
        sends = []
        for g in range(2):
            acc = jnp.zeros((ROWS, GW), f32)
            for t in range(TAPS):
                if t % 3 == 0:
                    w_loads[3 * g + t // 3].wait()
                acc = acc + mm(zed[rows_of(t), 0:CH], w_in[rows_of(t, CH), g * 256:g * 256 + GW])
            if g:
                acc = pltpu.roll(acc, GW - 64, 1)
            acc = jnp.where(lane < CH, acc, 0.0)
            act[g] = acc
            h_out[g] = silu(acc).astype(bf)
            if g == 0:
                arrive()
            for copy in (hop(0, h_out, h_in, g, 1), hop(1, h_out, skip_in, g, 3)):
                copy.start()
                sends.append(copy)
        for g in range(2):
            sends += spread(raw, gx, a_send, a_recv, g)
        for g in range(2):
            sends += spread(act.at[g], g_act, c_send, c_recv, g)
        make_select()
        for g in range(2):
            for t in range(TAPS):
                taps[t, rows_of(0), :] = zed[rows_of(t)]
            for k in (1, 3, 2):
                spread_wait(raw, gx, a_send, a_recv, g, k)
                lay_out_cells(gx.at[g, k])
                fill_taps(k, s_encode[...], x_in[...])
            make_left(g)
        for g in range(2):
            hop(3, g_out, gskip_in, g, 3).wait_recv()
            sends += spread(gskip_in.at[g], g_skip, s_send, s_recv, g)
        for g in range(2):
            for k in (1, 3, 2):
                spread_wait(act.at[g], g_act, c_send, c_recv, g, k)
                spread_wait(gskip_in.at[g], g_skip, s_send, s_recv, g, k)
        for g in range(2):
            for k in (0, 1, 3, 2):
                if k:
                    remote(g_out.at[g], g_back.at[g, k], b_send.at[g, k], b_recv.at[g, k], gather_peer[g](k)).wait_recv()
                    pre_k, skip_k = g_act[g, k], g_skip[g, k]
                else:
                    remote(g_out.at[g], g_back.at[g, 0], b_send.at[g, 0], b_recv.at[g, 0], {"section": 1}).wait_recv()
                    pre_k, skip_k = act[g], gskip_in[g]
                total = g_back[g, k].astype(f32) + skip_k.astype(f32)
                gd[g, k] = (total * silu_slope(pre_k)).astype(bf)
            sends += gradient(g)
        for copy in sends:
            copy.wait_send()

    @pl.when((sec == 1) | (sec == 2))
    def centre():
        s_load = load(c_shift, s_shift, 2)
        s_load.start()
        for copy in w_loads:
            copy.wait()
        pack_weights()
        s_load.wait()

        @pl.when(sec == 2)
        def turn_early():
            turn_weights()

        arrive(jnp.where(sec == 1, 6, 0))
        sends = []
        for g in range(2):
            hop(0, h_out, h_in, g, sec - 1).wait_recv()
            shifted = mm(s_shift[...], h_in[g]).astype(bf)
            acc = jnp.zeros((ROWS, GW), f32)
            for t in range(TAPS):
                acc = acc + mm(shifted[rows_of(t)], wp[g, rows_of(t, GW), :])
            act[g] = acc
            h_out[g] = (h_in[g].astype(f32) + silu(acc)).astype(bf)
            copy = hop(0, h_out, h_in, g, sec + 1)
            copy.start()
            sends.append(copy)
        for g in range(2):
            sends += spread(h_in.at[g], gh, a_send, a_recv, g)

        @pl.when(sec == 1)
        def turn_late():
            turn_weights()

        make_select()

        def to_encoders(g):
            copies = []
            for k in (1, 3, 2, 0):
                to = {"section": 0, **gather_peer[g](k)} if k else {"section": 0}
                copies.append(remote(g_out.at[g], g_back.at[g, (4 - k) % 4], b_send.at[g, k], b_recv.at[g, (4 - k) % 4], to))
            return copies

        def prepare(g):
            fill_taps(0, s_shift[...], h_in[g])
            for k in (1, 3, 2):
                spread_wait(h_in.at[g], gh, a_send, a_recv, g, k)
                fill_taps(k, s_shift[...], gh[g, k])
            make_left(g)

        @pl.when(sec == 1)
        def prepare_early():
            for g in range(2):
                prepare(g)

        for g in range(2):
            hop(2, g_out, g_in, g, sec + 1).wait_recv()
            delta = (g_in[g].astype(f32) * silu_slope(act[g])).astype(bf)
            gd[g, 0] = delta
            back = mm(s_shift[...], delta).astype(bf)
            acc = g_in[g].astype(f32)
            for t in range(TAPS):
                acc = acc + mm(back[rows_of(8 - t)], wt[g, rows_of(t, GW), :])
            g_out[g] = acc.astype(bf)

            @pl.when(sec == 2)
            def hop_back():
                hop(2, g_out, g_in, g, 1).start()

            @pl.when(sec == 1)
            def hop_to_encoders():
                for copy in to_encoders(g):
                    copy.start()

            sends += spread(gd.at[g, 0], gd, d_send, d_recv, g)

        @pl.when(sec == 2)
        def prepare_late():
            for g in range(2):
                prepare(g)
                hop(2, g_out, g_in, g, 1).wait_send()

        @pl.when(sec == 1)
        def encoders_sent():
            for g in range(2):
                for copy in to_encoders(g):
                    copy.wait_send()

        for g in range(2):
            for k in (1, 3, 2):
                spread_wait(gd.at[g, 0], gd, d_send, d_recv, g, k)
            sends += gradient(g)
        for copy in sends:
            copy.wait_send()

    @pl.when(sec == 3)
    def decoder():
        loads = [load(c_shift, s_shift, 2), load(c_fold, s_fold, 3), load(c_order, s_order, 1), load(tgt, raw, 0)]
        for copy in loads:
            copy.start()
        for copy in w_loads:
            copy.wait()
        pack_weights()
        turn_weights()
        for copy in loads:
            copy.wait()
        x_in[...] = jnp.zeros((CELLS, GW), bf)
        lay_out_cells(raw)
        target[...] = mm(s_order[...], x_in[...])
        make_select()
        arrive()
        sends = []
        for g in range(2):
            hop(1, h_out, skip_in, g, 0).wait_recv()
            hop(0, h_out, h_in, g, 2).wait_recv()
            u = (h_in[g].astype(f32) + skip_in[g].astype(f32)).astype(bf)
            gh[g, 0] = u
            sends += spread(gh.at[g, 0], gh, a_send, a_recv, g)
            shifted = mm(s_shift[...], u).astype(bf)
            for phase in range(4):
                for t in range(TAPS):
                    feat[g, rows_of(phase), rows_of(t, GW)] = shifted[rows_of(phase_shift(phase, t))]
            pre[g] = mm(feat[g], wp[g])
        value, gate = pre[0], pre[1]
        sig = jax.nn.sigmoid(gate)
        act_gate = gate * sig
        residual = (value * act_gate - target[...]) * (1.0 / 128.0)
        gd3[0, 0] = (residual * act_gate).astype(bf)
        gd3[1, 0] = (residual * value * (sig * (1.0 + gate * (1.0 - sig)))).astype(bf)
        for g in range(2):
            sends += spread(gd3.at[g, 0], gd3, d_send, d_recv, g)
        for g in range(2):
            back = mm(s_fold[...], gd3[g, 0]).astype(bf)
            acc = jnp.zeros((ROWS, GW), f32)
            for t in range(TAPS):
                acc = acc + mm(back[rows_of(t)], wt[g, rows_of(t, GW), :])
            g_out[g] = acc.astype(bf)
            for copy in (hop(2, g_out, g_in, g, 2), hop(3, g_out, gskip_in, g, 0)):
                copy.start()
                sends.append(copy)
        for g in range(2):
            for k in (1, 3, 2):
                spread_wait(gh.at[g, 0], gh, a_send, a_recv, g, k)
            source = gh[g].reshape(4 * ROWS, GW)
            for k in range(4):
                for i in range(2):
                    left[i, g, rows_of(k, 4 * SLOT), :] = block_rows(g, k, i, source).astype(bf)
        for g in range(2):
            fill_taps(0, s_fold[...], gd3[g, 0])
            for k in (1, 3, 2):
                spread_wait(gd3.at[g, 0], gd3, d_send, d_recv, g, k)
                fill_taps(k, s_fold[...], gd3[g, k])
            for k in (2, 1, 3, 0):
                block = sum(mm(left[i, g, rows_of(k, 4 * SLOT), :], taps[block_tap(g, k, i)]) for i in range(2))
                sends += hand_block(g, k, block)
        for copy in sends:
            copy.wait_send()

    sends = []
    for g in range(2):
        for k in (1, 3, 2):
            remote(pack.at[g, k], r_buf.at[g, k], r_send.at[g, k], r_recv.at[g, k], reduce_peer[g](k)).wait_recv()
        r_sum[g] = r_sum[g] + r_buf[g, 1].astype(f32) + r_buf[g, 2].astype(f32) + r_buf[g, 3].astype(f32)
    for k in (2, 1, 3):
        z_out[k] = z_slot(k).astype(bf)
        copy = remote(z_out.at[k], z_buf.at[4 - k], z_send.at[k], z_recv.at[4 - k], z_peer(k))
        copy.start()
        sends.append(copy)
    total = z_slot(0)
    for k in (1, 3, 2):
        remote(z_out.at[k], z_buf.at[k], z_send.at[k], z_recv.at[k], z_peer(k)).wait_recv()
        total = total + z_buf[k].astype(f32)
    lane = lax.broadcasted_iota(jnp.int32, (SLOT, GW), 1)
    side = total[:, 512:640]
    moved = pltpu.roll(jnp.concatenate([total[:, 256:512], side], axis=1), 64, 1)
    upper = jnp.where((lane < 64) | (lane >= CH), jnp.concatenate([side, side, side], axis=1), moved)
    out[:, 0, :] = jnp.concatenate([total[:, 0:256], upper], axis=1)[0:SHARE]
    for copy in sends:
        copy.wait_send()


def on_device(images, targets, kernels):
    bf = jnp.bfloat16

    def by_rows(grids):
        return jnp.transpose(grids, (1, 2, 0, 3))

    consts = [jnp.asarray(t, bf) for t in tables()]
    vm = pltpu.VMEM
    dma = pltpu.SemaphoreType.DMA
    hop = vm((2, ROWS, GW), bf)
    result = pl.pallas_call(
        body,
        out_shape=jax.ShapeDtypeStruct((SHARE, 1, 2 * CH), jnp.float32),
        in_specs=[pl.BlockSpec(memory_space=pltpu.HBM)] * 7,
        out_specs=pl.BlockSpec(memory_space=pltpu.VMEM),
        scratch_shapes=[
            vm((TAPS * CH, 2 * CH), bf),
            vm((1, 12, 2, 12 * CH), bf),
            vm((CELLS, GW), bf),
            vm((TAPS * ROWS, ROWS), bf),
            vm((TAPS * ROWS, CELLS), bf),
            vm((TAPS * ROWS, 4 * ROWS), bf),
            vm((4 * ROWS, CELLS), bf),
            vm((2, TAPS * GW, GW), bf),
            vm((2, TAPS * GW, GW), bf),
            vm((2, 4 * ROWS, TAPS * GW), bf),
            vm((2, ROWS, GW), jnp.float32),
            vm((2, 4 * ROWS, GW), jnp.float32),
            vm((4 * ROWS, GW), jnp.float32),
            vm((TAPS * ROWS, GW), bf),
            hop, hop, hop, hop, hop, hop,
            vm((2, 4, 1, 12, 2, 12 * CH), bf),
            vm((2, 4, ROWS, GW), bf),
            vm((2, 4, ROWS, GW), bf),
            vm((2, 4, 4 * ROWS, GW), bf),
            vm((2, 4, ROWS, GW), jnp.float32),
            vm((2, 4, ROWS, GW), bf),
            vm((2, 4, ROWS, GW), bf),
            vm((TAPS, 4 * ROWS, GW), bf),
            vm((4 * SLOT, GW), jnp.int32),
            vm((2, 2, 16 * SLOT, 4 * ROWS), bf),
            vm((2, 4, 5 * SLOT, 256), bf),
            vm((2, 4, 5 * SLOT, 256), bf),
            vm((2, 5 * SLOT, 256), jnp.float32),
            vm((4, SLOT, 2 * CH), bf),
            vm((4, SLOT, 2 * CH), bf),
            dma((10,)), dma((4, 2)), dma((4, 2)),
            *[dma((2, 4))] * 12, dma((4,)), dma((4,)),
        ],
        compiler_params=pltpu.CompilerParams(
            collective_id=0, has_side_effects=True, vmem_limit_bytes=63 * 1024 * 1024
        ),
    )(by_rows(images), by_rows(targets), kernels, *consts)
    return jnp.transpose(result, (1, 0, 2))


def solution(mesh):
    return jax.shard_map(
        on_device,
        mesh=mesh,
        in_specs=(P(None, "dp", None, None), P(None, "dp", None, None), P("section", None, None)),
        out_specs=P("section", "dp", None),
        check_vma=False,
    )
```

```python
import jax
import jax.numpy as jnp
import numpy as np
from jax import lax
from jax.experimental import pallas as pl
from jax.experimental.pallas import tpu as pltpu
from jax.sharding import PartitionSpec as P

MESH = pl.DeviceIdType.MESH
ROWS = 80
CH = 320
GW = 384
TAPS = 9
KW = TAPS * CH + 64
SHARE = 45
SLOT = 48
CELLS = 12 * 32


def phase_shift(phase, tap):
    alpha, beta = divmod(phase, 2)
    a, b = divmod(tap, 3)
    return ((alpha + a - 1) // 2 + 1) * 3 + ((beta + b - 1) // 2 + 1)


def tables():
    shift = np.zeros((TAPS, ROWS, ROWS), np.float32)
    encode = np.zeros((TAPS, ROWS, CELLS), np.float32)
    order = np.zeros((4, ROWS, CELLS), np.float32)
    for n in range(2):
        for i in range(6):
            for j in range(6):
                r = n * 36 + i * 6 + j
                for tap in range(TAPS):
                    a, b = divmod(tap, 3)
                    ii, jj = i + a - 1, j + b - 1
                    if 0 <= ii < 6 and 0 <= jj < 6:
                        shift[tap, r, n * 36 + ii * 6 + jj] = 1
                    ii, jj = 2 * i + a - 1, 2 * j + b - 1
                    if 0 <= ii < 12 and 0 <= jj < 12:
                        encode[tap, r, jj * 32 + n * 16 + ii] = 1
                for phase in range(4):
                    alpha, beta = divmod(phase, 2)
                    order[phase, r, (2 * j + beta) * 32 + n * 16 + 2 * i + alpha] = 1
    fold = np.zeros((TAPS, ROWS, 4, ROWS), np.float32)
    for tap in range(TAPS):
        for phase in range(4):
            fold[tap, :, phase, :] = shift[phase_shift(phase, tap)].T
    return (
        shift.reshape(TAPS * ROWS, ROWS),
        encode.reshape(TAPS * ROWS, CELLS),
        fold.reshape(TAPS * ROWS, 4 * ROWS),
        order.reshape(4 * ROWS, CELLS),
    )


def silu(v):
    return v * jax.nn.sigmoid(v)


def silu_slope(v):
    g = jax.nn.sigmoid(v)
    return g * (1.0 + v * (1.0 - g))


def mm(a, b):
    return jnp.dot(a, b, preferred_element_type=jnp.float32)


def mm_nt(a, b):
    return lax.dot_general(a, b, (((1,), (1,)), ((), ())), preferred_element_type=jnp.float32)


def remote(src, dst, send_sem, recv_sem, device):
    return pltpu.make_async_remote_copy(
        src_ref=src, dst_ref=dst, send_sem=send_sem, recv_sem=recv_sem, device_id=device, device_id_type=MESH
    )


def body(
    img, tgt, ker, c_shift, c_encode, c_fold, c_order, out,
    w_in, raw, x_in, s_shift, s_encode, s_fold, s_order,
    wp, wt, feat, act, pre, target, zed,
    h_in, skip_in, g_in, gskip_in, h_out, g_out,
    gx, gh, gd, gd3, taps, select, left, pack, r_buf, r_sum, z_out, z_buf,
    load_sem, hop_send, hop_recv, a_send, a_recv, d_send, d_recv, r_send, r_recv, z_send, z_recv,
):
    bf = jnp.bfloat16
    f32 = jnp.float32
    sec = lax.axis_index("section")
    dp = lax.axis_index("dp")
    x, y, z = dp // 16, (dp // 4) % 4, dp % 4

    def x_peer(k):
        return {"dp": (x + k) % 4 * 16 + y * 4 + z}

    def y_peer(k):
        return {"dp": x * 16 + (y + k) % 4 * 4 + z}

    def z_peer(k):
        return {"dp": x * 16 + y * 4 + (z + k) % 4}

    gather_peer = (x_peer, y_peer)
    reduce_peer = (y_peer, x_peer)

    def load(src, dst, n):
        return pltpu.make_async_copy(src, dst, load_sem.at[n])

    w_loads = []
    for n, (first, last) in enumerate(((0, GW), (GW, 2 * CH))):
        for i in range(3):
            part = (slice(i * 4 * CH, min((i + 1) * 4, TAPS) * CH), slice(first, last))
            w_loads.append(load(ker.at[(0, *part)], w_in.at[part], 4 + 3 * n + i))
    x_load = load(img, raw, 0)
    e_load = load(c_encode, s_encode, 1)

    @pl.when(sec == 0)
    def first_loads():
        x_load.start()
        e_load.start()

    for copy in w_loads:
        copy.start()

    barrier = pltpu.get_barrier_semaphore()
    for k in range(1, 4):
        pl.semaphore_signal(barrier, inc=1, device_id={"section": (sec + k) % 4}, device_id_type=MESH)
        for peer in (x_peer, y_peer, z_peer):
            pl.semaphore_signal(barrier, inc=1, device_id=peer(k), device_id_type=MESH)

    def arrive():
        pl.semaphore_wait(barrier, 12)

    def spread(src, buf, send, recv, g):
        copies = []
        for k in (1, 3, 2):
            copy = remote(src, buf.at[g, 4 - k], send.at[g, k], recv.at[g, 4 - k], gather_peer[g](k))
            copy.start()
            copies.append(copy)
        return copies

    def spread_wait(src, buf, send, recv, g, k):
        remote(src, buf.at[g, k], send.at[g, k], recv.at[g, k], gather_peer[g](k)).wait_recv()

    def hop(kind, src, dst, g, to):
        return remote(src.at[g], dst.at[g], hop_send.at[kind, g], hop_recv.at[kind, g], {"section": to})

    def rows_of(t, n=ROWS):
        return slice(t * n, (t + 1) * n)

    def pack_weights():
        lane = lax.broadcasted_iota(jnp.int32, (CH, GW), 1)

        def one(t, carry):
            rows = pl.ds(pl.multiple_of(t * CH, 16), CH)
            first = w_in[rows, 0:GW].astype(f32)
            wp[0, rows, :] = jnp.where(lane < CH, first, 0.0).astype(bf)
            second = pltpu.roll(w_in[rows, 256:640].astype(f32), GW - 64, 1)
            wp[1, rows, :] = jnp.where(lane < CH, second, 0.0).astype(bf)
            return carry

        for g in range(2):
            wp[g, TAPS * CH:KW, :] = jnp.zeros((64, GW), bf)
            wt[g, TAPS * CH:KW, :] = jnp.zeros((64, GW), bf)
        lax.fori_loop(0, TAPS, one, 0)

    def turn_weights():
        def one(t, carry):
            rows = pl.ds(pl.multiple_of(t * CH, 16), CH)
            for g in range(2):
                block = jnp.concatenate([wp[g, rows, :], jnp.zeros((GW - CH, GW), bf)], axis=0)
                wt[g, rows, :] = block.T[0:CH]
            return carry

        lax.fori_loop(0, TAPS, one, 0)

    def side_by_side(part, order):
        moved = {}
        columns = []
        for t in range(0, TAPS - 1, 2):
            n = order(t + 1)
            if n not in moved:
                moved[n] = pltpu.roll(part[rows_of(n)], 64, 1).astype(bf)
            a, b = part[rows_of(order(t))].astype(bf), moved[n]
            columns += [a[:, 0:256], a[:, 256:GW] + b[:, 0:128], b[:, 128:GW]]
        columns.append(part[rows_of(order(TAPS - 1))].astype(bf))
        return jnp.concatenate(columns, axis=1)

    def lay_out_cells():
        x_in[...] = jnp.zeros((CELLS, GW), bf)
        lane = lax.broadcasted_iota(jnp.int32, (12, GW), 1)
        for n in range(2):
            for j in range(12):
                start = j * CH - 64 * (j % 2)
                part = raw[0, :, n, start:start + GW].astype(f32)
                if j % 2:
                    part = pltpu.roll(part, GW - 64, 1)
                x_in[j * 32 + n * 16:j * 32 + n * 16 + 12, :] = jnp.where(lane < CH, part, 0.0).astype(bf)

    def make_select():
        lane = lax.broadcasted_iota(jnp.int32, (SLOT, GW), 1)
        row = lax.broadcasted_iota(jnp.int32, (SLOT, GW), 0)
        for j in range(4):
            value = row - lane + SHARE * ((z + j) % 4)
            select[rows_of(j, SLOT), :] = jnp.where((row < SHARE) & (lane < CH), value, -100000)

    def block_start(g, k):
        return 720 * x + 180 * ((y + k) % 4) if g == 0 else 720 * ((x + k) % 4) + 180 * y

    def block_tap(g, k, i):
        return jnp.minimum(block_start(g, k) // CH + i, TAPS - 1)

    def block_rows(g, k, i, source):
        start = block_start(g, k)
        chosen = select[...] == CH * (start // CH + i) - start
        return mm_nt(jnp.where(chosen, 1.0, 0.0).astype(bf), source)

    def make_left(g):
        for k in range(4):
            rows = sum(block_rows(g, k, i, taps[block_tap(g, k, i)]) for i in range(2))
            left[0, g, rows_of(k, 4 * SLOT), :] = rows.astype(bf)

    def fill_taps(k, table, source):
        part = mm(table, source).astype(bf)
        for t in range(TAPS):
            taps[t, rows_of(k), :] = part[rows_of(t)]

    def half_lanes(first, second):
        return jnp.where(lax.broadcasted_iota(jnp.int32, first.shape, 1) < 64, first, pltpu.roll(second, 64, 1))

    def squeeze(block):
        last = [block[rows_of(j, SLOT), 256:GW] for j in range(4)]
        side = jnp.concatenate([half_lanes(last[0], last[1]), half_lanes(last[2], last[3])], axis=1)
        return jnp.concatenate([block[:, 0:256], side], axis=0)

    def z_slot(j):
        side = slice(4 * SLOT, 5 * SLOT), slice(128 * (j // 2), 128 * (j // 2) + 128)
        first, second = r_sum[(0, *side)], r_sum[(1, *side)]
        if j % 2:
            first = pltpu.roll(first, 64, 1)
            second = pltpu.roll(second, 64, 1)
        return jnp.concatenate([r_sum[0, rows_of(j, SLOT), :], r_sum[1, rows_of(j, SLOT), :], half_lanes(first, second)], axis=1)

    def hand_block(g, k, block):
        if k == 0:
            r_sum[g] = squeeze(block)
            return []
        pack[g, k] = squeeze(block).astype(bf)
        copy = remote(pack.at[g, k], r_buf.at[g, 4 - k], r_send.at[g, k], r_recv.at[g, 4 - k], reduce_peer[g](k))
        copy.start()
        return [copy]

    def gradient(g):
        copies = []
        for k in (1, 3, 2):
            spread_wait(gd.at[g, 0], gd, d_send, d_recv, g, k)
        right = gd[g].reshape(4 * ROWS, GW)
        for k in (2, 1, 3, 0):
            copies += hand_block(g, k, mm(left[0, g, rows_of(k, 4 * SLOT), :], right))
        return copies

    @pl.when(sec == 0)
    def encoder():
        x_load.wait()
        lay_out_cells()
        e_load.wait()
        part = mm(s_encode[...], x_in[...])
        zed[...] = part.astype(bf)
        feat[0, 0:ROWS, :] = side_by_side(part, lambda t: t)
        lane = lax.broadcasted_iota(jnp.int32, (ROWS, GW), 1)
        sends = []
        for g in range(2):
            acc = jnp.zeros((ROWS, GW), f32)
            for i in range(3):
                w_loads[3 * g + i].wait()
                rows = slice(i * 4 * CH, min((i + 1) * 4, TAPS) * CH)
                acc = acc + mm(feat[0, 0:ROWS, rows], w_in[rows, g * 256:g * 256 + GW])
            if g:
                acc = pltpu.roll(acc, GW - 64, 1)
            acc = jnp.where(lane < CH, acc, 0.0)
            act[g] = acc
            h_out[g] = silu(acc).astype(bf)
            if g == 0:
                arrive()
            for copy in (hop(0, h_out, h_in, g, 1), hop(1, h_out, skip_in, g, 3)):
                copy.start()
                sends.append(copy)
        for g in range(2):
            sends += spread(x_in, gx, a_send, a_recv, g)
        make_select()
        for g in range(2):
            for t in range(TAPS):
                taps[t, rows_of(0), :] = zed[rows_of(t)]
            for k in (1, 3, 2):
                spread_wait(x_in, gx, a_send, a_recv, g, k)
                fill_taps(k, s_encode[...], gx[g, k])
            make_left(g)
        for g in range(2):
            hop(3, g_out, gskip_in, g, 3).wait_recv()
            hop(2, g_out, g_in, g, 1).wait_recv()
            total = g_in[g].astype(f32) + gskip_in[g].astype(f32)
            gd[g, 0] = (total * silu_slope(act[g])).astype(bf)
            sends += spread(gd.at[g, 0], gd, d_send, d_recv, g)
        for g in range(2):
            sends += gradient(g)
        for copy in sends:
            copy.wait_send()

    @pl.when((sec == 1) | (sec == 2))
    def centre():
        s_load = load(c_shift, s_shift, 2)
        s_load.start()
        for copy in w_loads:
            copy.wait()
        pack_weights()
        s_load.wait()

        @pl.when(sec == 2)
        def turn_early():
            turn_weights()

        arrive()
        sends = []
        for g in range(2):
            hop(0, h_out, h_in, g, sec - 1).wait_recv()
            acc = mm(side_by_side(mm(s_shift[...], h_in[g]), lambda t: t), wp[g])
            act[g] = acc
            h_out[g] = (h_in[g].astype(f32) + silu(acc)).astype(bf)
            copy = hop(0, h_out, h_in, g, sec + 1)
            copy.start()
            sends.append(copy)
        for g in range(2):
            sends += spread(h_in.at[g], gh, a_send, a_recv, g)

        @pl.when(sec == 1)
        def turn_late():
            turn_weights()

        make_select()

        def prepare(g):
            fill_taps(0, s_shift[...], h_in[g])
            for k in (1, 3, 2):
                spread_wait(h_in.at[g], gh, a_send, a_recv, g, k)
                fill_taps(k, s_shift[...], gh[g, k])
            make_left(g)

        @pl.when(sec == 1)
        def prepare_early():
            for g in range(2):
                prepare(g)

        for g in range(2):
            hop(2, g_out, g_in, g, sec + 1).wait_recv()
            delta = (g_in[g].astype(f32) * silu_slope(act[g])).astype(bf)
            gd[g, 0] = delta
            back = mm(side_by_side(mm(s_shift[...], delta), lambda t: 8 - t), wt[g])
            g_out[g] = (g_in[g].astype(f32) + back).astype(bf)
            copy = hop(2, g_out, g_in, g, sec - 1)
            copy.start()
            sends.append(copy)
            sends += spread(gd.at[g, 0], gd, d_send, d_recv, g)

        @pl.when(sec == 2)
        def prepare_late():
            for g in range(2):
                prepare(g)

        for g in range(2):
            sends += gradient(g)
        for copy in sends:
            copy.wait_send()

    @pl.when(sec == 3)
    def decoder():
        loads = [load(c_shift, s_shift, 2), load(c_fold, s_fold, 3), load(c_order, s_order, 1), load(tgt, raw, 0)]
        for copy in loads:
            copy.start()
        for copy in w_loads:
            copy.wait()
        pack_weights()
        turn_weights()
        for copy in loads:
            copy.wait()
        lay_out_cells()
        target[...] = mm(s_order[...], x_in[...])
        make_select()
        arrive()
        sends = []
        for g in range(2):
            hop(1, h_out, skip_in, g, 0).wait_recv()
            hop(0, h_out, h_in, g, 2).wait_recv()
            u = (h_in[g].astype(f32) + skip_in[g].astype(f32)).astype(bf)
            gh[g, 0] = u
            sends += spread(gh.at[g, 0], gh, a_send, a_recv, g)
            shifted = mm(s_shift[...], u)
            for phase in range(4):
                feat[g, rows_of(phase), :] = side_by_side(shifted, lambda t: phase_shift(phase, t))
            pre[g] = mm(feat[g], wp[g])
        value, gate = pre[0], pre[1]
        sig = jax.nn.sigmoid(gate)
        act_gate = gate * sig
        residual = (value * act_gate - target[...]) * (1.0 / 128.0)
        gd3[0, 0] = (residual * act_gate).astype(bf)
        gd3[1, 0] = (residual * value * (sig * (1.0 + gate * (1.0 - sig)))).astype(bf)
        for g in range(2):
            sends += spread(gd3.at[g, 0], gd3, d_send, d_recv, g)
        for g in range(2):
            g_out[g] = mm(side_by_side(mm(s_fold[...], gd3[g, 0]), lambda t: t), wt[g]).astype(bf)
            for copy in (hop(2, g_out, g_in, g, 2), hop(3, g_out, gskip_in, g, 0)):
                copy.start()
                sends.append(copy)
        for g in range(2):
            for k in (1, 3, 2):
                spread_wait(gh.at[g, 0], gh, a_send, a_recv, g, k)
            source = gh[g].reshape(4 * ROWS, GW)
            for k in range(4):
                for i in range(2):
                    left[i, g, rows_of(k, 4 * SLOT), :] = block_rows(g, k, i, source).astype(bf)
        for g in range(2):
            fill_taps(0, s_fold[...], gd3[g, 0])
            for k in (1, 3, 2):
                spread_wait(gd3.at[g, 0], gd3, d_send, d_recv, g, k)
                fill_taps(k, s_fold[...], gd3[g, k])
            for k in (2, 1, 3, 0):
                block = sum(mm(left[i, g, rows_of(k, 4 * SLOT), :], taps[block_tap(g, k, i)]) for i in range(2))
                sends += hand_block(g, k, block)
        for copy in sends:
            copy.wait_send()

    sends = []
    for g in range(2):
        for k in (1, 3, 2):
            remote(pack.at[g, k], r_buf.at[g, k], r_send.at[g, k], r_recv.at[g, k], reduce_peer[g](k)).wait_recv()
        r_sum[g] = r_sum[g] + r_buf[g, 1].astype(f32) + r_buf[g, 2].astype(f32) + r_buf[g, 3].astype(f32)
    for k in (2, 1, 3):
        z_out[k] = z_slot(k).astype(bf)
        copy = remote(z_out.at[k], z_buf.at[4 - k], z_send.at[k], z_recv.at[4 - k], z_peer(k))
        copy.start()
        sends.append(copy)
    total = z_slot(0)
    for k in (1, 3, 2):
        remote(z_out.at[k], z_buf.at[k], z_send.at[k], z_recv.at[k], z_peer(k)).wait_recv()
        total = total + z_buf[k].astype(f32)
    lane = lax.broadcasted_iota(jnp.int32, (SLOT, GW), 1)
    side = total[:, 512:640]
    moved = pltpu.roll(jnp.concatenate([total[:, 256:512], side], axis=1), 64, 1)
    upper = jnp.where((lane < 64) | (lane >= CH), jnp.concatenate([side, side, side], axis=1), moved)
    out[:, 0, :] = jnp.concatenate([total[:, 0:256], upper], axis=1)[0:SHARE]
    for copy in sends:
        copy.wait_send()


def on_device(images, targets, kernels):
    bf = jnp.bfloat16

    def by_rows(grids):
        return jnp.transpose(grids, (1, 2, 0, 3))

    consts = [jnp.asarray(t, bf) for t in tables()]
    vm = pltpu.VMEM
    dma = pltpu.SemaphoreType.DMA
    hop = vm((2, ROWS, GW), bf)
    result = pl.pallas_call(
        body,
        out_shape=jax.ShapeDtypeStruct((SHARE, 1, 2 * CH), jnp.float32),
        in_specs=[pl.BlockSpec(memory_space=pltpu.HBM)] * 7,
        out_specs=pl.BlockSpec(memory_space=pltpu.VMEM),
        scratch_shapes=[
            vm((TAPS * CH, 2 * CH), bf),
            vm((1, 12, 2, 12 * CH), bf),
            vm((CELLS, GW), bf),
            vm((TAPS * ROWS, ROWS), bf),
            vm((TAPS * ROWS, CELLS), bf),
            vm((TAPS * ROWS, 4 * ROWS), bf),
            vm((4 * ROWS, CELLS), bf),
            vm((2, KW, GW), bf),
            vm((2, KW, GW), bf),
            vm((2, 4 * ROWS, KW), bf),
            vm((2, ROWS, GW), jnp.float32),
            vm((2, 4 * ROWS, GW), jnp.float32),
            vm((4 * ROWS, GW), jnp.float32),
            vm((TAPS * ROWS, GW), bf),
            hop, hop, hop, hop, hop, hop,
            vm((2, 4, CELLS, GW), bf),
            vm((2, 4, ROWS, GW), bf),
            vm((2, 4, ROWS, GW), bf),
            vm((2, 4, 4 * ROWS, GW), bf),
            vm((TAPS, 4 * ROWS, GW), bf),
            vm((4 * SLOT, GW), jnp.int32),
            vm((2, 2, 16 * SLOT, 4 * ROWS), bf),
            vm((2, 4, 5 * SLOT, 256), bf),
            vm((2, 4, 5 * SLOT, 256), bf),
            vm((2, 5 * SLOT, 256), jnp.float32),
            vm((4, SLOT, 2 * CH), bf),
            vm((4, SLOT, 2 * CH), bf),
            dma((10,)), dma((4, 2)), dma((4, 2)),
            dma((2, 4)), dma((2, 4)), dma((2, 4)), dma((2, 4)), dma((2, 4)), dma((2, 4)), dma((4,)), dma((4,)),
        ],
        compiler_params=pltpu.CompilerParams(
            collective_id=0, has_side_effects=True, vmem_limit_bytes=63 * 1024 * 1024
        ),
    )(by_rows(images), by_rows(targets), kernels, *consts)
    return jnp.transpose(result, (1, 0, 2))


def solution(mesh):
    return jax.shard_map(
        on_device,
        mesh=mesh,
        in_specs=(P(None, "dp", None, None), P(None, "dp", None, None), P("section", None, None)),
        out_specs=P("section", "dp", None),
        check_vma=False,
    )
```

```python
import jax
import jax.numpy as jnp
import numpy as np
from jax import lax
from jax.experimental import pallas as pl
from jax.experimental.pallas import tpu as pltpu
from jax.sharding import PartitionSpec as P

MESH = pl.DeviceIdType.MESH
ROWS = 80
CH = 320
GW = 384
TAPS = 9
KW = TAPS * CH + 64
SHARE = 45
SLOT = 48
CELLS = 12 * 32


def phase_shift(phase, tap):
    alpha, beta = divmod(phase, 2)
    a, b = divmod(tap, 3)
    return ((alpha + a - 1) // 2 + 1) * 3 + ((beta + b - 1) // 2 + 1)


def tables():
    shift = np.zeros((TAPS, ROWS, ROWS), np.float32)
    encode = np.zeros((TAPS, ROWS, CELLS), np.float32)
    order = np.zeros((4, ROWS, CELLS), np.float32)
    for n in range(2):
        for i in range(6):
            for j in range(6):
                r = n * 36 + i * 6 + j
                for tap in range(TAPS):
                    a, b = divmod(tap, 3)
                    ii, jj = i + a - 1, j + b - 1
                    if 0 <= ii < 6 and 0 <= jj < 6:
                        shift[tap, r, n * 36 + ii * 6 + jj] = 1
                    ii, jj = 2 * i + a - 1, 2 * j + b - 1
                    if 0 <= ii < 12 and 0 <= jj < 12:
                        encode[tap, r, jj * 32 + n * 16 + ii] = 1
                for phase in range(4):
                    alpha, beta = divmod(phase, 2)
                    order[phase, r, (2 * j + beta) * 32 + n * 16 + 2 * i + alpha] = 1
    fold = np.zeros((TAPS, ROWS, 4, ROWS), np.float32)
    for tap in range(TAPS):
        for phase in range(4):
            fold[tap, :, phase, :] = shift[phase_shift(phase, tap)].T
    return (
        shift.reshape(TAPS * ROWS, ROWS),
        encode.reshape(TAPS * ROWS, CELLS),
        fold.reshape(TAPS * ROWS, 4 * ROWS),
        order.reshape(4 * ROWS, CELLS),
    )


def silu(v):
    return v * jax.nn.sigmoid(v)


def silu_slope(v):
    g = jax.nn.sigmoid(v)
    return g * (1.0 + v * (1.0 - g))


def mm(a, b):
    return jnp.dot(a, b, preferred_element_type=jnp.float32)


def mm_nt(a, b):
    return lax.dot_general(a, b, (((1,), (1,)), ((), ())), preferred_element_type=jnp.float32)


def remote(src, dst, send_sem, recv_sem, device):
    return pltpu.make_async_remote_copy(
        src_ref=src, dst_ref=dst, send_sem=send_sem, recv_sem=recv_sem, device_id=device, device_id_type=MESH
    )


def body(
    img, tgt, ker, c_shift, c_encode, c_fold, c_order, out,
    w_in, raw, x_in, s_shift, s_encode, s_fold, s_order,
    wp, wt, feat, act, pre, target, zed,
    h_in, skip_in, g_in, gskip_in, h_out, g_out,
    gx, gh, gd, gd3, taps, select, left, pack, r_buf, r_sum, z_out, z_buf,
    load_sem, hop_send, hop_recv, a_send, a_recv, d_send, d_recv, r_send, r_recv, z_send, z_recv,
):
    bf = jnp.bfloat16
    f32 = jnp.float32
    sec = lax.axis_index("section")
    dp = lax.axis_index("dp")
    x, y, z = dp // 16, (dp // 4) % 4, dp % 4

    def x_peer(k):
        return {"dp": (x + k) % 4 * 16 + y * 4 + z}

    def y_peer(k):
        return {"dp": x * 16 + (y + k) % 4 * 4 + z}

    def z_peer(k):
        return {"dp": x * 16 + y * 4 + (z + k) % 4}

    gather_peer = (x_peer, y_peer)
    reduce_peer = (y_peer, x_peer)

    def load(src, dst, n):
        return pltpu.make_async_copy(src, dst, load_sem.at[n])

    w_loads = []
    for n, (first, last) in enumerate(((0, GW), (GW, 2 * CH))):
        for i in range(3):
            part = (slice(i * 4 * CH, min((i + 1) * 4, TAPS) * CH), slice(first, last))
            w_loads.append(load(ker.at[(0, *part)], w_in.at[part], 4 + 3 * n + i))
    x_load = load(img, raw, 0)
    e_load = load(c_encode, s_encode, 1)

    @pl.when(sec == 0)
    def first_loads():
        x_load.start()
        e_load.start()

    for copy in w_loads:
        copy.start()

    barrier = pltpu.get_barrier_semaphore()
    for k in range(1, 4):
        pl.semaphore_signal(barrier, inc=1, device_id={"section": (sec + k) % 4}, device_id_type=MESH)
        for peer in (x_peer, y_peer, z_peer):
            pl.semaphore_signal(barrier, inc=1, device_id=peer(k), device_id_type=MESH)

    def arrive():
        pl.semaphore_wait(barrier, 12)

    def spread(src, buf, send, recv, g):
        copies = []
        for k in (2, 1, 3):
            copy = remote(src, buf.at[g, 4 - k], send.at[g, k], recv.at[g, 4 - k], gather_peer[g](k))
            copy.start()
            copies.append(copy)
        return copies

    def spread_wait(src, buf, send, recv, g, k):
        remote(src, buf.at[g, k], send.at[g, k], recv.at[g, k], gather_peer[g](k)).wait_recv()

    def hop(kind, src, dst, g, to):
        return remote(src.at[g], dst.at[g], hop_send.at[kind, g], hop_recv.at[kind, g], {"section": to})

    def rows_of(t, n=ROWS):
        return slice(t * n, (t + 1) * n)

    def pack_weights():
        lane = lax.broadcasted_iota(jnp.int32, (CH, GW), 1)

        def one(t, carry):
            rows = pl.ds(pl.multiple_of(t * CH, 16), CH)
            first = w_in[rows, 0:GW].astype(f32)
            wp[0, rows, :] = jnp.where(lane < CH, first, 0.0).astype(bf)
            second = pltpu.roll(w_in[rows, 256:640].astype(f32), GW - 64, 1)
            wp[1, rows, :] = jnp.where(lane < CH, second, 0.0).astype(bf)
            return carry

        for g in range(2):
            wp[g, TAPS * CH:KW, :] = jnp.zeros((64, GW), bf)
            wt[g, TAPS * CH:KW, :] = jnp.zeros((64, GW), bf)
        lax.fori_loop(0, TAPS, one, 0)

    def turn_weights():
        def one(t, carry):
            rows = pl.ds(pl.multiple_of(t * CH, 16), CH)
            for g in range(2):
                block = jnp.concatenate([wp[g, rows, :], jnp.zeros((GW - CH, GW), bf)], axis=0)
                wt[g, rows, :] = block.T[0:CH]
            return carry

        lax.fori_loop(0, TAPS, one, 0)

    def side_by_side(part, order):
        moved = {}
        columns = []
        for t in range(0, TAPS - 1, 2):
            n = order(t + 1)
            if n not in moved:
                moved[n] = pltpu.roll(part[rows_of(n)], 64, 1).astype(bf)
            a, b = part[rows_of(order(t))].astype(bf), moved[n]
            columns += [a[:, 0:256], a[:, 256:GW] + b[:, 0:128], b[:, 128:GW]]
        columns.append(part[rows_of(order(TAPS - 1))].astype(bf))
        return jnp.concatenate(columns, axis=1)

    def lay_out_cells():
        x_in[...] = jnp.zeros((CELLS, GW), bf)
        lane = lax.broadcasted_iota(jnp.int32, (12, GW), 1)
        for n in range(2):
            for j in range(12):
                start = j * CH - 64 * (j % 2)
                part = raw[0, :, n, start:start + GW].astype(f32)
                if j % 2:
                    part = pltpu.roll(part, GW - 64, 1)
                x_in[j * 32 + n * 16:j * 32 + n * 16 + 12, :] = jnp.where(lane < CH, part, 0.0).astype(bf)

    def make_select():
        lane = lax.broadcasted_iota(jnp.int32, (SLOT, GW), 1)
        row = lax.broadcasted_iota(jnp.int32, (SLOT, GW), 0)
        for j in range(4):
            value = row - lane + SHARE * ((z + j) % 4)
            select[rows_of(j, SLOT), :] = jnp.where((row < SHARE) & (lane < CH), value, -100000)

    def block_start(g, k):
        return 720 * x + 180 * ((y + k) % 4) if g == 0 else 720 * ((x + k) % 4) + 180 * y

    def block_tap(g, k, i):
        return jnp.minimum(block_start(g, k) // CH + i, TAPS - 1)

    def block_rows(g, k, i, source):
        start = block_start(g, k)
        chosen = select[...] == CH * (start // CH + i) - start
        return mm_nt(jnp.where(chosen, 1.0, 0.0).astype(bf), source)

    def make_left(g):
        for k in range(4):
            rows = sum(block_rows(g, k, i, taps[block_tap(g, k, i)]) for i in range(2))
            left[0, g, rows_of(k, 4 * SLOT), :] = rows.astype(bf)

    def fill_taps(k, table, source):
        part = mm(table, source).astype(bf)
        for t in range(TAPS):
            taps[t, rows_of(k), :] = part[rows_of(t)]

    def half_lanes(first, second):
        return jnp.where(lax.broadcasted_iota(jnp.int32, first.shape, 1) < 64, first, pltpu.roll(second, 64, 1))

    def squeeze(block):
        last = [block[rows_of(j, SLOT), 256:GW] for j in range(4)]
        side = jnp.concatenate([half_lanes(last[0], last[1]), half_lanes(last[2], last[3])], axis=1)
        return jnp.concatenate([block[:, 0:256], side], axis=0)

    def z_slot(j):
        side = slice(4 * SLOT, 5 * SLOT), slice(128 * (j // 2), 128 * (j // 2) + 128)
        first, second = r_sum[(0, *side)], r_sum[(1, *side)]
        if j % 2:
            first = pltpu.roll(first, 64, 1)
            second = pltpu.roll(second, 64, 1)
        return jnp.concatenate([r_sum[0, rows_of(j, SLOT), :], r_sum[1, rows_of(j, SLOT), :], half_lanes(first, second)], axis=1)

    def hand_block(g, k, block):
        if k == 0:
            r_sum[g] = squeeze(block)
            return []
        pack[g, k] = squeeze(block).astype(bf)
        copy = remote(pack.at[g, k], r_buf.at[g, 4 - k], r_send.at[g, k], r_recv.at[g, 4 - k], reduce_peer[g](k))
        copy.start()
        return [copy]

    def gradient(g):
        copies = []
        for k in (1, 3, 2):
            spread_wait(gd.at[g, 0], gd, d_send, d_recv, g, k)
        right = gd[g].reshape(4 * ROWS, GW)
        for k in (2, 1, 3, 0):
            copies += hand_block(g, k, mm(left[0, g, rows_of(k, 4 * SLOT), :], right))
        return copies

    @pl.when(sec == 0)
    def encoder():
        x_load.wait()
        lay_out_cells()
        e_load.wait()
        part = mm(s_encode[...], x_in[...])
        zed[...] = part.astype(bf)
        feat[0, 0:ROWS, :] = side_by_side(part, lambda t: t)
        lane = lax.broadcasted_iota(jnp.int32, (ROWS, GW), 1)
        sends = []
        for g in range(2):
            acc = jnp.zeros((ROWS, GW), f32)
            for i in range(3):
                w_loads[3 * g + i].wait()
                rows = slice(i * 4 * CH, min((i + 1) * 4, TAPS) * CH)
                acc = acc + mm(feat[0, 0:ROWS, rows], w_in[rows, g * 256:g * 256 + GW])
            if g:
                acc = pltpu.roll(acc, GW - 64, 1)
            acc = jnp.where(lane < CH, acc, 0.0)
            act[g] = acc
            h_out[g] = silu(acc).astype(bf)
            if g == 0:
                arrive()
            for copy in (hop(0, h_out, h_in, g, 1), hop(1, h_out, skip_in, g, 3)):
                copy.start()
                sends.append(copy)
        for g in range(2):
            sends += spread(x_in, gx, a_send, a_recv, g)
        make_select()
        for g in range(2):
            for t in range(TAPS):
                taps[t, rows_of(0), :] = zed[rows_of(t)]
            for k in (1, 3, 2):
                spread_wait(x_in, gx, a_send, a_recv, g, k)
                fill_taps(k, s_encode[...], gx[g, k])
            make_left(g)
        for g in range(2):
            hop(3, g_out, gskip_in, g, 3).wait_recv()
            hop(2, g_out, g_in, g, 1).wait_recv()
            total = g_in[g].astype(f32) + gskip_in[g].astype(f32)
            gd[g, 0] = (total * silu_slope(act[g])).astype(bf)
            sends += spread(gd.at[g, 0], gd, d_send, d_recv, g)
        for g in range(2):
            sends += gradient(g)
        for copy in sends:
            copy.wait_send()

    @pl.when((sec == 1) | (sec == 2))
    def centre():
        s_load = load(c_shift, s_shift, 2)
        s_load.start()
        for copy in w_loads:
            copy.wait()
        pack_weights()
        s_load.wait()

        @pl.when(sec == 2)
        def turn_early():
            turn_weights()

        arrive()
        sends = []
        for g in range(2):
            hop(0, h_out, h_in, g, sec - 1).wait_recv()
            acc = mm(side_by_side(mm(s_shift[...], h_in[g]), lambda t: t), wp[g])
            act[g] = acc
            h_out[g] = (h_in[g].astype(f32) + silu(acc)).astype(bf)
            copy = hop(0, h_out, h_in, g, sec + 1)
            copy.start()
            sends.append(copy)
        for g in range(2):
            sends += spread(h_in.at[g], gh, a_send, a_recv, g)

        @pl.when(sec == 1)
        def turn_late():
            turn_weights()

        make_select()

        def prepare(g):
            fill_taps(0, s_shift[...], h_in[g])
            for k in (1, 3, 2):
                spread_wait(h_in.at[g], gh, a_send, a_recv, g, k)
                fill_taps(k, s_shift[...], gh[g, k])
            make_left(g)

        @pl.when(sec == 1)
        def prepare_early():
            for g in range(2):
                prepare(g)

        for g in range(2):
            hop(2, g_out, g_in, g, sec + 1).wait_recv()
            delta = (g_in[g].astype(f32) * silu_slope(act[g])).astype(bf)
            gd[g, 0] = delta
            back = mm(side_by_side(mm(s_shift[...], delta), lambda t: 8 - t), wt[g])
            g_out[g] = (g_in[g].astype(f32) + back).astype(bf)
            copy = hop(2, g_out, g_in, g, sec - 1)
            copy.start()
            sends.append(copy)
        for g in range(2):
            sends += spread(gd.at[g, 0], gd, d_send, d_recv, g)

        @pl.when(sec == 2)
        def prepare_late():
            for g in range(2):
                prepare(g)

        for g in range(2):
            sends += gradient(g)
        for copy in sends:
            copy.wait_send()

    @pl.when(sec == 3)
    def decoder():
        loads = [load(c_shift, s_shift, 2), load(c_fold, s_fold, 3), load(c_order, s_order, 1), load(tgt, raw, 0)]
        for copy in loads:
            copy.start()
        for copy in w_loads:
            copy.wait()
        pack_weights()
        turn_weights()
        for copy in loads:
            copy.wait()
        lay_out_cells()
        target[...] = mm(s_order[...], x_in[...])
        make_select()
        arrive()
        sends = []
        for g in range(2):
            hop(1, h_out, skip_in, g, 0).wait_recv()
            hop(0, h_out, h_in, g, 2).wait_recv()
            u = (h_in[g].astype(f32) + skip_in[g].astype(f32)).astype(bf)
            gh[g, 0] = u
            shifted = mm(s_shift[...], u)
            for phase in range(4):
                feat[g, rows_of(phase), :] = side_by_side(shifted, lambda t: phase_shift(phase, t))
            pre[g] = mm(feat[g], wp[g])
            sends += spread(gh.at[g, 0], gh, a_send, a_recv, g)
        value, gate = pre[0], pre[1]
        sig = jax.nn.sigmoid(gate)
        act_gate = gate * sig
        residual = (value * act_gate - target[...]) * (1.0 / 128.0)
        gd3[0, 0] = (residual * act_gate).astype(bf)
        gd3[1, 0] = (residual * value * (sig * (1.0 + gate * (1.0 - sig)))).astype(bf)
        for g in range(2):
            g_out[g] = mm(side_by_side(mm(s_fold[...], gd3[g, 0]), lambda t: t), wt[g]).astype(bf)
            for copy in (hop(2, g_out, g_in, g, 2), hop(3, g_out, gskip_in, g, 0)):
                copy.start()
                sends.append(copy)
            sends += spread(gd3.at[g, 0], gd3, d_send, d_recv, g)
        for g in range(2):
            for k in (1, 3, 2):
                spread_wait(gh.at[g, 0], gh, a_send, a_recv, g, k)
            source = gh[g].reshape(4 * ROWS, GW)
            for k in range(4):
                for i in range(2):
                    left[i, g, rows_of(k, 4 * SLOT), :] = block_rows(g, k, i, source).astype(bf)
        for g in range(2):
            fill_taps(0, s_fold[...], gd3[g, 0])
            for k in (1, 3, 2):
                spread_wait(gd3.at[g, 0], gd3, d_send, d_recv, g, k)
                fill_taps(k, s_fold[...], gd3[g, k])
            for k in (2, 1, 3, 0):
                block = sum(mm(left[i, g, rows_of(k, 4 * SLOT), :], taps[block_tap(g, k, i)]) for i in range(2))
                sends += hand_block(g, k, block)
        for copy in sends:
            copy.wait_send()

    sends = []
    for g in range(2):
        for k in (1, 3, 2):
            remote(pack.at[g, k], r_buf.at[g, k], r_send.at[g, k], r_recv.at[g, k], reduce_peer[g](k)).wait_recv()
        r_sum[g] = r_sum[g] + r_buf[g, 1].astype(f32) + r_buf[g, 2].astype(f32) + r_buf[g, 3].astype(f32)
    for k in (2, 1, 3):
        z_out[k] = z_slot(k).astype(bf)
        copy = remote(z_out.at[k], z_buf.at[4 - k], z_send.at[k], z_recv.at[4 - k], z_peer(k))
        copy.start()
        sends.append(copy)
    total = z_slot(0)
    for k in (1, 3, 2):
        remote(z_out.at[k], z_buf.at[k], z_send.at[k], z_recv.at[k], z_peer(k)).wait_recv()
        total = total + z_buf[k].astype(f32)
    lane = lax.broadcasted_iota(jnp.int32, (SLOT, GW), 1)
    side = total[:, 512:640]
    moved = pltpu.roll(jnp.concatenate([total[:, 256:512], side], axis=1), 64, 1)
    upper = jnp.where((lane < 64) | (lane >= CH), jnp.concatenate([side, side, side], axis=1), moved)
    out[:, 0, :] = jnp.concatenate([total[:, 0:256], upper], axis=1)[0:SHARE]
    for copy in sends:
        copy.wait_send()


def on_device(images, targets, kernels):
    bf = jnp.bfloat16

    def by_rows(grids):
        return jnp.transpose(grids, (1, 2, 0, 3))

    consts = [jnp.asarray(t, bf) for t in tables()]
    vm = pltpu.VMEM
    dma = pltpu.SemaphoreType.DMA
    hop = vm((2, ROWS, GW), bf)
    result = pl.pallas_call(
        body,
        out_shape=jax.ShapeDtypeStruct((SHARE, 1, 2 * CH), jnp.float32),
        in_specs=[pl.BlockSpec(memory_space=pltpu.HBM)] * 7,
        out_specs=pl.BlockSpec(memory_space=pltpu.VMEM),
        scratch_shapes=[
            vm((TAPS * CH, 2 * CH), bf),
            vm((1, 12, 2, 12 * CH), bf),
            vm((CELLS, GW), bf),
            vm((TAPS * ROWS, ROWS), bf),
            vm((TAPS * ROWS, CELLS), bf),
            vm((TAPS * ROWS, 4 * ROWS), bf),
            vm((4 * ROWS, CELLS), bf),
            vm((2, KW, GW), bf),
            vm((2, KW, GW), bf),
            vm((2, 4 * ROWS, KW), bf),
            vm((2, ROWS, GW), jnp.float32),
            vm((2, 4 * ROWS, GW), jnp.float32),
            vm((4 * ROWS, GW), jnp.float32),
            vm((TAPS * ROWS, GW), bf),
            hop, hop, hop, hop, hop, hop,
            vm((2, 4, CELLS, GW), bf),
            vm((2, 4, ROWS, GW), bf),
            vm((2, 4, ROWS, GW), bf),
            vm((2, 4, 4 * ROWS, GW), bf),
            vm((TAPS, 4 * ROWS, GW), bf),
            vm((4 * SLOT, GW), jnp.int32),
            vm((2, 2, 16 * SLOT, 4 * ROWS), bf),
            vm((2, 4, 5 * SLOT, 256), bf),
            vm((2, 4, 5 * SLOT, 256), bf),
            vm((2, 5 * SLOT, 256), jnp.float32),
            vm((4, SLOT, 2 * CH), bf),
            vm((4, SLOT, 2 * CH), bf),
            dma((10,)), dma((4, 2)), dma((4, 2)),
            dma((2, 4)), dma((2, 4)), dma((2, 4)), dma((2, 4)), dma((2, 4)), dma((2, 4)), dma((4,)), dma((4,)),
        ],
        compiler_params=pltpu.CompilerParams(
            collective_id=0, has_side_effects=True, vmem_limit_bytes=63 * 1024 * 1024
        ),
    )(by_rows(images), by_rows(targets), kernels, *consts)
    return jnp.transpose(result, (1, 0, 2))


def solution(mesh):
    return jax.shard_map(
        on_device,
        mesh=mesh,
        in_specs=(P(None, "dp", None, None), P(None, "dp", None, None), P("section", None, None)),
        out_specs=P("section", "dp", None),
        check_vma=False,
    )
```

```python
import jax
import jax.numpy as jnp
import numpy as np
from jax import lax
from jax.experimental import pallas as pl
from jax.experimental.pallas import tpu as pltpu
from jax.sharding import PartitionSpec as P

MESH = pl.DeviceIdType.MESH
ROWS = 80
CH = 320
GW = 384
TAPS = 9
KW = TAPS * CH + 64
SHARE = 45
SLOT = 48
CELLS = 12 * 32


def phase_shift(phase, tap):
    alpha, beta = divmod(phase, 2)
    a, b = divmod(tap, 3)
    return ((alpha + a - 1) // 2 + 1) * 3 + ((beta + b - 1) // 2 + 1)


def tables():
    shift = np.zeros((TAPS, ROWS, ROWS), np.float32)
    encode = np.zeros((TAPS, ROWS, CELLS), np.float32)
    order = np.zeros((4, ROWS, CELLS), np.float32)
    for n in range(2):
        for i in range(6):
            for j in range(6):
                r = n * 36 + i * 6 + j
                for tap in range(TAPS):
                    a, b = divmod(tap, 3)
                    ii, jj = i + a - 1, j + b - 1
                    if 0 <= ii < 6 and 0 <= jj < 6:
                        shift[tap, r, n * 36 + ii * 6 + jj] = 1
                    ii, jj = 2 * i + a - 1, 2 * j + b - 1
                    if 0 <= ii < 12 and 0 <= jj < 12:
                        encode[tap, r, jj * 32 + n * 16 + ii] = 1
                for phase in range(4):
                    alpha, beta = divmod(phase, 2)
                    order[phase, r, (2 * j + beta) * 32 + n * 16 + 2 * i + alpha] = 1
    fold = np.zeros((TAPS, ROWS, 4, ROWS), np.float32)
    for tap in range(TAPS):
        for phase in range(4):
            fold[tap, :, phase, :] = shift[phase_shift(phase, tap)].T
    return (
        shift.reshape(TAPS * ROWS, ROWS),
        encode.reshape(TAPS * ROWS, CELLS),
        fold.reshape(TAPS * ROWS, 4 * ROWS),
        order.reshape(4 * ROWS, CELLS),
    )


def silu(v):
    return v * jax.nn.sigmoid(v)


def silu_slope(v):
    g = jax.nn.sigmoid(v)
    return g * (1.0 + v * (1.0 - g))


def mm(a, b):
    return jnp.dot(a, b, preferred_element_type=jnp.float32)


def mm_nt(a, b):
    return lax.dot_general(a, b, (((1,), (1,)), ((), ())), preferred_element_type=jnp.float32)


def remote(src, dst, send_sem, recv_sem, device):
    return pltpu.make_async_remote_copy(
        src_ref=src, dst_ref=dst, send_sem=send_sem, recv_sem=recv_sem, device_id=device, device_id_type=MESH
    )


def body(
    img, tgt, ker, c_shift, c_encode, c_fold, c_order, out,
    w_in, raw, x_in, s_shift, s_encode, s_fold, s_order,
    wp, wt, feat, act, pre, target, zed,
    h_in, skip_in, g_in, gskip_in, h_out, g_out,
    gx, gh, gd, gd3, taps, select, left, pack, r_buf, r_sum, z_out, z_buf,
    load_sem, hop_send, hop_recv, a_send, a_recv, d_send, d_recv, r_send, r_recv, z_send, z_recv,
):
    bf = jnp.bfloat16
    f32 = jnp.float32
    sec = lax.axis_index("section")
    dp = lax.axis_index("dp")
    x, y, z = dp // 16, (dp // 4) % 4, dp % 4

    def x_peer(k):
        return {"dp": (x + k) % 4 * 16 + y * 4 + z}

    def y_peer(k):
        return {"dp": x * 16 + (y + k) % 4 * 4 + z}

    def z_peer(k):
        return {"dp": x * 16 + y * 4 + (z + k) % 4}

    gather_peer = (x_peer, y_peer)
    reduce_peer = (y_peer, x_peer)

    def load(src, dst, n):
        return pltpu.make_async_copy(src, dst, load_sem.at[n])

    w_loads = []
    for n, (first, last) in enumerate(((0, GW), (GW, 2 * CH))):
        for i in range(3):
            part = (slice(i * 4 * CH, min((i + 1) * 4, TAPS) * CH), slice(first, last))
            w_loads.append(load(ker.at[(0, *part)], w_in.at[part], 4 + 3 * n + i))
    x_load = load(img, raw, 0)
    e_load = load(c_encode, s_encode, 1)

    @pl.when(sec == 0)
    def first_loads():
        x_load.start()
        e_load.start()

    for copy in w_loads:
        copy.start()

    barrier = pltpu.get_barrier_semaphore()
    for k in range(1, 4):
        pl.semaphore_signal(barrier, inc=1, device_id={"section": (sec + k) % 4}, device_id_type=MESH)
        for peer in (x_peer, y_peer, z_peer):
            pl.semaphore_signal(barrier, inc=1, device_id=peer(k), device_id_type=MESH)

    def arrive():
        pl.semaphore_wait(barrier, 12)

    def spread(src, buf, send, recv, g):
        copies = []
        for k in (1, 3, 2):
            copy = remote(src, buf.at[g, 4 - k], send.at[g, k], recv.at[g, 4 - k], gather_peer[g](k))
            copy.start()
            copies.append(copy)
        return copies

    def spread_wait(src, buf, send, recv, g, k):
        remote(src, buf.at[g, k], send.at[g, k], recv.at[g, k], gather_peer[g](k)).wait_recv()

    def hop(kind, src, dst, g, to):
        return remote(src.at[g], dst.at[g], hop_send.at[kind, g], hop_recv.at[kind, g], {"section": to})

    def rows_of(t, n=ROWS):
        return slice(t * n, (t + 1) * n)

    def pack_weights():
        lane = lax.broadcasted_iota(jnp.int32, (CH, GW), 1)

        def one(t, carry):
            rows = pl.ds(pl.multiple_of(t * CH, 16), CH)
            first = w_in[rows, 0:GW].astype(f32)
            wp[0, rows, :] = jnp.where(lane < CH, first, 0.0).astype(bf)
            second = pltpu.roll(w_in[rows, 256:640].astype(f32), GW - 64, 1)
            wp[1, rows, :] = jnp.where(lane < CH, second, 0.0).astype(bf)
            return carry

        for g in range(2):
            wp[g, TAPS * CH:KW, :] = jnp.zeros((64, GW), bf)
            wt[g, TAPS * CH:KW, :] = jnp.zeros((64, GW), bf)
        lax.fori_loop(0, TAPS, one, 0)

    def turn_weights():
        def one(t, carry):
            rows = pl.ds(pl.multiple_of(t * CH, 16), CH)
            for g in range(2):
                block = jnp.concatenate([wp[g, rows, :], jnp.zeros((GW - CH, GW), bf)], axis=0)
                wt[g, rows, :] = block.T[0:CH]
            return carry

        lax.fori_loop(0, TAPS, one, 0)

    def side_by_side(part, order):
        moved = {}
        columns = []
        for t in range(0, TAPS - 1, 2):
            n = order(t + 1)
            if n not in moved:
                moved[n] = pltpu.roll(part[rows_of(n)], 64, 1).astype(bf)
            a, b = part[rows_of(order(t))].astype(bf), moved[n]
            columns += [a[:, 0:256], a[:, 256:GW] + b[:, 0:128], b[:, 128:GW]]
        columns.append(part[rows_of(order(TAPS - 1))].astype(bf))
        return jnp.concatenate(columns, axis=1)

    def lay_out_cells():
        x_in[...] = jnp.zeros((CELLS, GW), bf)
        lane = lax.broadcasted_iota(jnp.int32, (12, GW), 1)
        for n in range(2):
            for j in range(12):
                start = j * CH - 64 * (j % 2)
                part = raw[0, :, n, start:start + GW].astype(f32)
                if j % 2:
                    part = pltpu.roll(part, GW - 64, 1)
                x_in[j * 32 + n * 16:j * 32 + n * 16 + 12, :] = jnp.where(lane < CH, part, 0.0).astype(bf)

    def make_select():
        lane = lax.broadcasted_iota(jnp.int32, (SLOT, GW), 1)
        row = lax.broadcasted_iota(jnp.int32, (SLOT, GW), 0)
        for j in range(4):
            value = row - lane + SHARE * ((z + j) % 4)
            select[rows_of(j, SLOT), :] = jnp.where((row < SHARE) & (lane < CH), value, -100000)

    def block_start(g, k):
        return 720 * x + 180 * ((y + k) % 4) if g == 0 else 720 * ((x + k) % 4) + 180 * y

    def block_tap(g, k, i):
        return jnp.minimum(block_start(g, k) // CH + i, TAPS - 1)

    def block_rows(g, k, i, source):
        start = block_start(g, k)
        chosen = select[...] == CH * (start // CH + i) - start
        return mm_nt(jnp.where(chosen, 1.0, 0.0).astype(bf), source)

    def make_left(g):
        for k in range(4):
            rows = sum(block_rows(g, k, i, taps[block_tap(g, k, i)]) for i in range(2))
            left[0, g, rows_of(k, 4 * SLOT), :] = rows.astype(bf)

    def fill_taps(k, table, source):
        part = mm(table, source).astype(bf)
        for t in range(TAPS):
            taps[t, rows_of(k), :] = part[rows_of(t)]

    def half_lanes(first, second):
        return jnp.where(lax.broadcasted_iota(jnp.int32, first.shape, 1) < 64, first, pltpu.roll(second, 64, 1))

    def squeeze(block):
        last = [block[rows_of(j, SLOT), 256:GW] for j in range(4)]
        side = jnp.concatenate([half_lanes(last[0], last[1]), half_lanes(last[2], last[3])], axis=1)
        return jnp.concatenate([block[:, 0:256], side], axis=0)

    def z_slot(j):
        side = slice(4 * SLOT, 5 * SLOT), slice(128 * (j // 2), 128 * (j // 2) + 128)
        first, second = r_sum[(0, *side)], r_sum[(1, *side)]
        if j % 2:
            first = pltpu.roll(first, 64, 1)
            second = pltpu.roll(second, 64, 1)
        return jnp.concatenate([r_sum[0, rows_of(j, SLOT), :], r_sum[1, rows_of(j, SLOT), :], half_lanes(first, second)], axis=1)

    def hand_block(g, k, block):
        if k == 0:
            r_sum[g] = squeeze(block)
            return []
        pack[g, k] = squeeze(block).astype(bf)
        copy = remote(pack.at[g, k], r_buf.at[g, 4 - k], r_send.at[g, k], r_recv.at[g, 4 - k], reduce_peer[g](k))
        copy.start()
        return [copy]

    def gradient(g):
        copies = []
        for k in (1, 3, 2):
            spread_wait(gd.at[g, 0], gd, d_send, d_recv, g, k)
        right = gd[g].reshape(4 * ROWS, GW)
        for k in (2, 1, 3, 0):
            copies += hand_block(g, k, mm(left[0, g, rows_of(k, 4 * SLOT), :], right))
        return copies

    @pl.when(sec == 0)
    def encoder():
        x_load.wait()
        lay_out_cells()
        e_load.wait()
        part = mm(s_encode[...], x_in[...])
        zed[...] = part.astype(bf)
        feat[0, 0:ROWS, :] = side_by_side(part, lambda t: t)
        lane = lax.broadcasted_iota(jnp.int32, (ROWS, GW), 1)
        sends = []
        for g in range(2):
            acc = jnp.zeros((ROWS, GW), f32)
            for i in range(3):
                w_loads[3 * g + i].wait()
                rows = slice(i * 4 * CH, min((i + 1) * 4, TAPS) * CH)
                acc = acc + mm(feat[0, 0:ROWS, rows], w_in[rows, g * 256:g * 256 + GW])
            if g:
                acc = pltpu.roll(acc, GW - 64, 1)
            acc = jnp.where(lane < CH, acc, 0.0)
            act[g] = acc
            h_out[g] = silu(acc).astype(bf)
            if g == 0:
                arrive()
            for copy in (hop(0, h_out, h_in, g, 1), hop(1, h_out, skip_in, g, 3)):
                copy.start()
                sends.append(copy)
        for g in range(2):
            sends += spread(x_in, gx, a_send, a_recv, g)
        make_select()
        for g in range(2):
            for t in range(TAPS):
                taps[t, rows_of(0), :] = zed[rows_of(t)]
            for k in (1, 3, 2):
                spread_wait(x_in, gx, a_send, a_recv, g, k)
                fill_taps(k, s_encode[...], gx[g, k])
            make_left(g)
        for g in range(2):
            hop(3, g_out, gskip_in, g, 3).wait_recv()
            hop(2, g_out, g_in, g, 1).wait_recv()
            total = g_in[g].astype(f32) + gskip_in[g].astype(f32)
            gd[g, 0] = (total * silu_slope(act[g])).astype(bf)
            sends += spread(gd.at[g, 0], gd, d_send, d_recv, g)
        for g in range(2):
            sends += gradient(g)
        for copy in sends:
            copy.wait_send()

    @pl.when((sec == 1) | (sec == 2))
    def centre():
        s_load = load(c_shift, s_shift, 2)
        s_load.start()
        for copy in w_loads:
            copy.wait()
        pack_weights()
        s_load.wait()

        @pl.when(sec == 2)
        def turn_early():
            turn_weights()

        arrive()
        sends = []
        for g in range(2):
            hop(0, h_out, h_in, g, sec - 1).wait_recv()
            acc = mm(side_by_side(mm(s_shift[...], h_in[g]), lambda t: t), wp[g])
            act[g] = acc
            h_out[g] = (h_in[g].astype(f32) + silu(acc)).astype(bf)
            copy = hop(0, h_out, h_in, g, sec + 1)
            copy.start()
            sends.append(copy)
        for g in range(2):
            sends += spread(h_in.at[g], gh, a_send, a_recv, g)

        @pl.when(sec == 1)
        def turn_late():
            turn_weights()

        make_select()

        def prepare(g):
            fill_taps(0, s_shift[...], h_in[g])
            for k in (1, 3, 2):
                spread_wait(h_in.at[g], gh, a_send, a_recv, g, k)
                fill_taps(k, s_shift[...], gh[g, k])
            make_left(g)

        @pl.when(sec == 1)
        def prepare_early():
            for g in range(2):
                prepare(g)

        for g in range(2):
            hop(2, g_out, g_in, g, sec + 1).wait_recv()
            delta = (g_in[g].astype(f32) * silu_slope(act[g])).astype(bf)
            gd[g, 0] = delta
            sends += spread(gd.at[g, 0], gd, d_send, d_recv, g)
            back = mm(side_by_side(mm(s_shift[...], delta), lambda t: 8 - t), wt[g])
            g_out[g] = (g_in[g].astype(f32) + back).astype(bf)
            copy = hop(2, g_out, g_in, g, sec - 1)
            copy.start()
            sends.append(copy)

        @pl.when(sec == 2)
        def prepare_late():
            for g in range(2):
                prepare(g)

        for g in range(2):
            sends += gradient(g)
        for copy in sends:
            copy.wait_send()

    @pl.when(sec == 3)
    def decoder():
        loads = [load(c_shift, s_shift, 2), load(c_fold, s_fold, 3), load(c_order, s_order, 1), load(tgt, raw, 0)]
        for copy in loads:
            copy.start()
        for copy in w_loads:
            copy.wait()
        pack_weights()
        turn_weights()
        for copy in loads:
            copy.wait()
        lay_out_cells()
        target[...] = mm(s_order[...], x_in[...])
        make_select()
        arrive()
        sends = []
        for g in range(2):
            hop(1, h_out, skip_in, g, 0).wait_recv()
            hop(0, h_out, h_in, g, 2).wait_recv()
            u = (h_in[g].astype(f32) + skip_in[g].astype(f32)).astype(bf)
            gh[g, 0] = u
            shifted = mm(s_shift[...], u)
            for phase in range(4):
                feat[g, rows_of(phase), :] = side_by_side(shifted, lambda t: phase_shift(phase, t))
            pre[g] = mm(feat[g], wp[g])
            sends += spread(gh.at[g, 0], gh, a_send, a_recv, g)
        value, gate = pre[0], pre[1]
        sig = jax.nn.sigmoid(gate)
        act_gate = gate * sig
        residual = (value * act_gate - target[...]) * (1.0 / 128.0)
        gd3[0, 0] = (residual * act_gate).astype(bf)
        gd3[1, 0] = (residual * value * (sig * (1.0 + gate * (1.0 - sig)))).astype(bf)
        for g in range(2):
            g_out[g] = mm(side_by_side(mm(s_fold[...], gd3[g, 0]), lambda t: t), wt[g]).astype(bf)
            for copy in (hop(2, g_out, g_in, g, 2), hop(3, g_out, gskip_in, g, 0)):
                copy.start()
                sends.append(copy)
            sends += spread(gd3.at[g, 0], gd3, d_send, d_recv, g)
        for g in range(2):
            for k in (1, 3, 2):
                spread_wait(gh.at[g, 0], gh, a_send, a_recv, g, k)
            source = gh[g].reshape(4 * ROWS, GW)
            for k in range(4):
                for i in range(2):
                    left[i, g, rows_of(k, 4 * SLOT), :] = block_rows(g, k, i, source).astype(bf)
        for g in range(2):
            fill_taps(0, s_fold[...], gd3[g, 0])
            for k in (1, 3, 2):
                spread_wait(gd3.at[g, 0], gd3, d_send, d_recv, g, k)
                fill_taps(k, s_fold[...], gd3[g, k])
            for k in (2, 1, 3, 0):
                block = sum(mm(left[i, g, rows_of(k, 4 * SLOT), :], taps[block_tap(g, k, i)]) for i in range(2))
                sends += hand_block(g, k, block)
        for copy in sends:
            copy.wait_send()

    sends = []
    for g in range(2):
        for k in (1, 3, 2):
            remote(pack.at[g, k], r_buf.at[g, k], r_send.at[g, k], r_recv.at[g, k], reduce_peer[g](k)).wait_recv()
        r_sum[g] = r_sum[g] + r_buf[g, 1].astype(f32) + r_buf[g, 2].astype(f32) + r_buf[g, 3].astype(f32)
    for k in (2, 1, 3):
        z_out[k] = z_slot(k).astype(bf)
        copy = remote(z_out.at[k], z_buf.at[4 - k], z_send.at[k], z_recv.at[4 - k], z_peer(k))
        copy.start()
        sends.append(copy)
    total = z_slot(0)
    for k in (1, 3, 2):
        remote(z_out.at[k], z_buf.at[k], z_send.at[k], z_recv.at[k], z_peer(k)).wait_recv()
        total = total + z_buf[k].astype(f32)
    lane = lax.broadcasted_iota(jnp.int32, (SLOT, GW), 1)
    side = total[:, 512:640]
    moved = pltpu.roll(jnp.concatenate([total[:, 256:512], side], axis=1), 64, 1)
    upper = jnp.where((lane < 64) | (lane >= CH), jnp.concatenate([side, side, side], axis=1), moved)
    out[:, 0, :] = jnp.concatenate([total[:, 0:256], upper], axis=1)[0:SHARE]
    for copy in sends:
        copy.wait_send()


def on_device(images, targets, kernels):
    bf = jnp.bfloat16

    def by_rows(grids):
        return jnp.transpose(grids, (1, 2, 0, 3))

    consts = [jnp.asarray(t, bf) for t in tables()]
    vm = pltpu.VMEM
    dma = pltpu.SemaphoreType.DMA
    hop = vm((2, ROWS, GW), bf)
    result = pl.pallas_call(
        body,
        out_shape=jax.ShapeDtypeStruct((SHARE, 1, 2 * CH), jnp.float32),
        in_specs=[pl.BlockSpec(memory_space=pltpu.HBM)] * 7,
        out_specs=pl.BlockSpec(memory_space=pltpu.VMEM),
        scratch_shapes=[
            vm((TAPS * CH, 2 * CH), bf),
            vm((1, 12, 2, 12 * CH), bf),
            vm((CELLS, GW), bf),
            vm((TAPS * ROWS, ROWS), bf),
            vm((TAPS * ROWS, CELLS), bf),
            vm((TAPS * ROWS, 4 * ROWS), bf),
            vm((4 * ROWS, CELLS), bf),
            vm((2, KW, GW), bf),
            vm((2, KW, GW), bf),
            vm((2, 4 * ROWS, KW), bf),
            vm((2, ROWS, GW), jnp.float32),
            vm((2, 4 * ROWS, GW), jnp.float32),
            vm((4 * ROWS, GW), jnp.float32),
            vm((TAPS * ROWS, GW), bf),
            hop, hop, hop, hop, hop, hop,
            vm((2, 4, CELLS, GW), bf),
            vm((2, 4, ROWS, GW), bf),
            vm((2, 4, ROWS, GW), bf),
            vm((2, 4, 4 * ROWS, GW), bf),
            vm((TAPS, 4 * ROWS, GW), bf),
            vm((4 * SLOT, GW), jnp.int32),
            vm((2, 2, 16 * SLOT, 4 * ROWS), bf),
            vm((2, 4, 5 * SLOT, 256), bf),
            vm((2, 4, 5 * SLOT, 256), bf),
            vm((2, 5 * SLOT, 256), jnp.float32),
            vm((4, SLOT, 2 * CH), bf),
            vm((4, SLOT, 2 * CH), bf),
            dma((10,)), dma((4, 2)), dma((4, 2)),
            dma((2, 4)), dma((2, 4)), dma((2, 4)), dma((2, 4)), dma((2, 4)), dma((2, 4)), dma((4,)), dma((4,)),
        ],
        compiler_params=pltpu.CompilerParams(
            collective_id=0, has_side_effects=True, vmem_limit_bytes=63 * 1024 * 1024
        ),
    )(by_rows(images), by_rows(targets), kernels, *consts)
    return jnp.transpose(result, (1, 0, 2))


def solution(mesh):
    return jax.shard_map(
        on_device,
        mesh=mesh,
        in_specs=(P(None, "dp", None, None), P(None, "dp", None, None), P("section", None, None)),
        out_specs=P("section", "dp", None),
        check_vma=False,
    )
```

```python
import jax
import jax.numpy as jnp
import numpy as np
from jax import lax
from jax.experimental import pallas as pl
from jax.experimental.pallas import tpu as pltpu
from jax.sharding import PartitionSpec as P

MESH = pl.DeviceIdType.MESH
ROWS = 80
CH = 320
GW = 384
TAPS = 9
KW = TAPS * CH + 64
SHARE = 45
SLOT = 48
CELLS = 12 * 32


def phase_shift(phase, tap):
    alpha, beta = divmod(phase, 2)
    a, b = divmod(tap, 3)
    return ((alpha + a - 1) // 2 + 1) * 3 + ((beta + b - 1) // 2 + 1)


def tables():
    shift = np.zeros((TAPS, ROWS, ROWS), np.float32)
    encode = np.zeros((TAPS, ROWS, CELLS), np.float32)
    order = np.zeros((4, ROWS, CELLS), np.float32)
    for n in range(2):
        for i in range(6):
            for j in range(6):
                r = n * 36 + i * 6 + j
                for tap in range(TAPS):
                    a, b = divmod(tap, 3)
                    ii, jj = i + a - 1, j + b - 1
                    if 0 <= ii < 6 and 0 <= jj < 6:
                        shift[tap, r, n * 36 + ii * 6 + jj] = 1
                    ii, jj = 2 * i + a - 1, 2 * j + b - 1
                    if 0 <= ii < 12 and 0 <= jj < 12:
                        encode[tap, r, jj * 32 + n * 16 + ii] = 1
                for phase in range(4):
                    alpha, beta = divmod(phase, 2)
                    order[phase, r, (2 * j + beta) * 32 + n * 16 + 2 * i + alpha] = 1
    fold = np.zeros((TAPS, ROWS, 4, ROWS), np.float32)
    for tap in range(TAPS):
        for phase in range(4):
            fold[tap, :, phase, :] = shift[phase_shift(phase, tap)].T
    return (
        shift.reshape(TAPS * ROWS, ROWS),
        encode.reshape(TAPS * ROWS, CELLS),
        fold.reshape(TAPS * ROWS, 4 * ROWS),
        order.reshape(4 * ROWS, CELLS),
    )


def silu(v):
    return v * jax.nn.sigmoid(v)


def silu_slope(v):
    g = jax.nn.sigmoid(v)
    return g * (1.0 + v * (1.0 - g))


def mm(a, b):
    return jnp.dot(a, b, preferred_element_type=jnp.float32)


def mm_nt(a, b):
    return lax.dot_general(a, b, (((1,), (1,)), ((), ())), preferred_element_type=jnp.float32)


def remote(src, dst, send_sem, recv_sem, device):
    return pltpu.make_async_remote_copy(
        src_ref=src, dst_ref=dst, send_sem=send_sem, recv_sem=recv_sem, device_id=device, device_id_type=MESH
    )


def body(
    img, tgt, ker, c_shift, c_encode, c_fold, c_order, out,
    w_in, raw, x_in, s_shift, s_encode, s_fold, s_order,
    wp, wt, feat, act, pre, target, zed,
    h_in, skip_in, g_in, gskip_in, h_out, g_out,
    gx, gh, gd, gd3, taps, select, left, pack, r_buf, r_sum, z_out, z_buf,
    load_sem, hop_send, hop_recv, a_send, a_recv, d_send, d_recv, r_send, r_recv, z_send, z_recv,
):
    bf = jnp.bfloat16
    f32 = jnp.float32
    sec = lax.axis_index("section")
    dp = lax.axis_index("dp")
    x, y, z = dp // 16, (dp // 4) % 4, dp % 4

    def x_peer(k):
        return {"dp": (x + k) % 4 * 16 + y * 4 + z}

    def y_peer(k):
        return {"dp": x * 16 + (y + k) % 4 * 4 + z}

    def z_peer(k):
        return {"dp": x * 16 + y * 4 + (z + k) % 4}

    gather_peer = (x_peer, y_peer)
    reduce_peer = (y_peer, x_peer)

    def load(src, dst, n):
        return pltpu.make_async_copy(src, dst, load_sem.at[n])

    w_loads = []
    for n, (first, last) in enumerate(((0, GW), (GW, 2 * CH))):
        for i in range(3):
            part = (slice(i * 4 * CH, min((i + 1) * 4, TAPS) * CH), slice(first, last))
            w_loads.append(load(ker.at[(0, *part)], w_in.at[part], 4 + 3 * n + i))
    x_load = load(img, raw, 0)
    e_load = load(c_encode, s_encode, 1)

    @pl.when(sec == 0)
    def first_loads():
        x_load.start()
        e_load.start()

    for copy in w_loads:
        copy.start()

    barrier = pltpu.get_barrier_semaphore()
    for k in range(1, 4):
        pl.semaphore_signal(barrier, inc=1, device_id={"section": (sec + k) % 4}, device_id_type=MESH)
        for peer in (x_peer, y_peer, z_peer):
            pl.semaphore_signal(barrier, inc=1, device_id=peer(k), device_id_type=MESH)

    def arrive():
        pl.semaphore_wait(barrier, 12)

    def spread(src, buf, send, recv, g):
        copies = []
        for k in (2, 1, 3):
            copy = remote(src, buf.at[g, 4 - k], send.at[g, k], recv.at[g, 4 - k], gather_peer[g](k))
            copy.start()
            copies.append(copy)
        return copies

    def spread_wait(src, buf, send, recv, g, k):
        remote(src, buf.at[g, k], send.at[g, k], recv.at[g, k], gather_peer[g](k)).wait_recv()

    def hop(kind, src, dst, g, to):
        return remote(src.at[g], dst.at[g], hop_send.at[kind, g], hop_recv.at[kind, g], {"section": to})

    def rows_of(t, n=ROWS):
        return slice(t * n, (t + 1) * n)

    def pack_weights():
        lane = lax.broadcasted_iota(jnp.int32, (CH, GW), 1)

        def one(t, carry):
            rows = pl.ds(pl.multiple_of(t * CH, 16), CH)
            first = w_in[rows, 0:GW].astype(f32)
            wp[0, rows, :] = jnp.where(lane < CH, first, 0.0).astype(bf)
            second = pltpu.roll(w_in[rows, 256:640].astype(f32), GW - 64, 1)
            wp[1, rows, :] = jnp.where(lane < CH, second, 0.0).astype(bf)
            return carry

        for g in range(2):
            wp[g, TAPS * CH:KW, :] = jnp.zeros((64, GW), bf)
            wt[g, TAPS * CH:KW, :] = jnp.zeros((64, GW), bf)
        lax.fori_loop(0, TAPS, one, 0)

    def turn_weights():
        def one(t, carry):
            rows = pl.ds(pl.multiple_of(t * CH, 16), CH)
            for g in range(2):
                block = jnp.concatenate([wp[g, rows, :], jnp.zeros((GW - CH, GW), bf)], axis=0)
                wt[g, rows, :] = block.T[0:CH]
            return carry

        lax.fori_loop(0, TAPS, one, 0)

    def side_by_side(part, order):
        moved = {}
        columns = []
        for t in range(0, TAPS - 1, 2):
            n = order(t + 1)
            if n not in moved:
                moved[n] = pltpu.roll(part[rows_of(n)], 64, 1).astype(bf)
            a, b = part[rows_of(order(t))].astype(bf), moved[n]
            columns += [a[:, 0:256], a[:, 256:GW] + b[:, 0:128], b[:, 128:GW]]
        columns.append(part[rows_of(order(TAPS - 1))].astype(bf))
        return jnp.concatenate(columns, axis=1)

    def lay_out_cells():
        x_in[...] = jnp.zeros((CELLS, GW), bf)
        lane = lax.broadcasted_iota(jnp.int32, (12, GW), 1)
        for n in range(2):
            for j in range(12):
                start = j * CH - 64 * (j % 2)
                part = raw[0, :, n, start:start + GW].astype(f32)
                if j % 2:
                    part = pltpu.roll(part, GW - 64, 1)
                x_in[j * 32 + n * 16:j * 32 + n * 16 + 12, :] = jnp.where(lane < CH, part, 0.0).astype(bf)

    def make_select():
        lane = lax.broadcasted_iota(jnp.int32, (SLOT, GW), 1)
        row = lax.broadcasted_iota(jnp.int32, (SLOT, GW), 0)
        for j in range(4):
            value = row - lane + SHARE * ((z + j) % 4)
            select[rows_of(j, SLOT), :] = jnp.where((row < SHARE) & (lane < CH), value, -100000)

    def block_start(g, k):
        return 720 * x + 180 * ((y + k) % 4) if g == 0 else 720 * ((x + k) % 4) + 180 * y

    def block_tap(g, k, i):
        return jnp.minimum(block_start(g, k) // CH + i, TAPS - 1)

    def block_rows(g, k, i, source):
        start = block_start(g, k)
        chosen = select[...] == CH * (start // CH + i) - start
        return mm_nt(jnp.where(chosen, 1.0, 0.0).astype(bf), source)

    def make_left(g):
        for k in range(4):
            rows = sum(block_rows(g, k, i, taps[block_tap(g, k, i)]) for i in range(2))
            left[0, g, rows_of(k, 4 * SLOT), :] = rows.astype(bf)

    def fill_taps(k, table, source):
        part = mm(table, source).astype(bf)
        for t in range(TAPS):
            taps[t, rows_of(k), :] = part[rows_of(t)]

    def half_lanes(first, second):
        return jnp.where(lax.broadcasted_iota(jnp.int32, first.shape, 1) < 64, first, pltpu.roll(second, 64, 1))

    def squeeze(block):
        last = [block[rows_of(j, SLOT), 256:GW] for j in range(4)]
        side = jnp.concatenate([half_lanes(last[0], last[1]), half_lanes(last[2], last[3])], axis=1)
        return jnp.concatenate([block[:, 0:256], side], axis=0)

    def z_slot(j):
        side = slice(4 * SLOT, 5 * SLOT), slice(128 * (j // 2), 128 * (j // 2) + 128)
        first, second = r_sum[(0, *side)], r_sum[(1, *side)]
        if j % 2:
            first = pltpu.roll(first, 64, 1)
            second = pltpu.roll(second, 64, 1)
        return jnp.concatenate([r_sum[0, rows_of(j, SLOT), :], r_sum[1, rows_of(j, SLOT), :], half_lanes(first, second)], axis=1)

    def hand_block(g, k, block):
        if k == 0:
            r_sum[g] = squeeze(block)
            return []
        pack[g, k] = squeeze(block).astype(bf)
        copy = remote(pack.at[g, k], r_buf.at[g, 4 - k], r_send.at[g, k], r_recv.at[g, 4 - k], reduce_peer[g](k))
        copy.start()
        return [copy]

    def gradient(g):
        copies = []
        for k in (1, 3, 2):
            spread_wait(gd.at[g, 0], gd, d_send, d_recv, g, k)
        right = gd[g].reshape(4 * ROWS, GW)
        for k in (2, 1, 3, 0):
            copies += hand_block(g, k, mm(left[0, g, rows_of(k, 4 * SLOT), :], right))
        return copies

    @pl.when(sec == 0)
    def encoder():
        x_load.wait()
        lay_out_cells()
        e_load.wait()
        part = mm(s_encode[...], x_in[...])
        zed[...] = part.astype(bf)
        feat[0, 0:ROWS, :] = side_by_side(part, lambda t: t)
        lane = lax.broadcasted_iota(jnp.int32, (ROWS, GW), 1)
        sends = []
        for g in range(2):
            acc = jnp.zeros((ROWS, GW), f32)
            for i in range(3):
                w_loads[3 * g + i].wait()
                rows = slice(i * 4 * CH, min((i + 1) * 4, TAPS) * CH)
                acc = acc + mm(feat[0, 0:ROWS, rows], w_in[rows, g * 256:g * 256 + GW])
            if g:
                acc = pltpu.roll(acc, GW - 64, 1)
            acc = jnp.where(lane < CH, acc, 0.0)
            act[g] = acc
            h_out[g] = silu(acc).astype(bf)
            if g == 0:
                arrive()
            for copy in (hop(0, h_out, h_in, g, 1), hop(1, h_out, skip_in, g, 3)):
                copy.start()
                sends.append(copy)
        for g in range(2):
            sends += spread(x_in, gx, a_send, a_recv, g)
        make_select()
        for g in range(2):
            for t in range(TAPS):
                taps[t, rows_of(0), :] = zed[rows_of(t)]
            for k in (1, 3, 2):
                spread_wait(x_in, gx, a_send, a_recv, g, k)
                fill_taps(k, s_encode[...], gx[g, k])
            make_left(g)
        for g in range(2):
            hop(3, g_out, gskip_in, g, 3).wait_recv()
            hop(2, g_out, g_in, g, 1).wait_recv()
            total = g_in[g].astype(f32) + gskip_in[g].astype(f32)
            gd[g, 0] = (total * silu_slope(act[g])).astype(bf)
            sends += spread(gd.at[g, 0], gd, d_send, d_recv, g)
        for g in range(2):
            sends += gradient(g)
        for copy in sends:
            copy.wait_send()

    @pl.when((sec == 1) | (sec == 2))
    def centre():
        s_load = load(c_shift, s_shift, 2)
        s_load.start()
        for copy in w_loads:
            copy.wait()
        pack_weights()
        s_load.wait()

        @pl.when(sec == 2)
        def turn_early():
            turn_weights()

        arrive()
        sends = []
        for g in range(2):
            hop(0, h_out, h_in, g, sec - 1).wait_recv()
            acc = mm(side_by_side(mm(s_shift[...], h_in[g]), lambda t: t), wp[g])
            act[g] = acc
            h_out[g] = (h_in[g].astype(f32) + silu(acc)).astype(bf)
            copy = hop(0, h_out, h_in, g, sec + 1)
            copy.start()
            sends.append(copy)
        for g in range(2):
            sends += spread(h_in.at[g], gh, a_send, a_recv, g)

        @pl.when(sec == 1)
        def turn_late():
            turn_weights()

        make_select()

        def prepare(g):
            fill_taps(0, s_shift[...], h_in[g])
            for k in (1, 3, 2):
                spread_wait(h_in.at[g], gh, a_send, a_recv, g, k)
                fill_taps(k, s_shift[...], gh[g, k])
            make_left(g)

        @pl.when(sec == 1)
        def prepare_early():
            for g in range(2):
                prepare(g)

        for g in range(2):
            hop(2, g_out, g_in, g, sec + 1).wait_recv()
            delta = (g_in[g].astype(f32) * silu_slope(act[g])).astype(bf)
            gd[g, 0] = delta
            sends += spread(gd.at[g, 0], gd, d_send, d_recv, g)
            back = mm(side_by_side(mm(s_shift[...], delta), lambda t: 8 - t), wt[g])
            g_out[g] = (g_in[g].astype(f32) + back).astype(bf)
            copy = hop(2, g_out, g_in, g, sec - 1)
            copy.start()
            sends.append(copy)

        @pl.when(sec == 2)
        def prepare_late():
            for g in range(2):
                prepare(g)

        for g in range(2):
            sends += gradient(g)
        for copy in sends:
            copy.wait_send()

    @pl.when(sec == 3)
    def decoder():
        loads = [load(c_shift, s_shift, 2), load(c_fold, s_fold, 3), load(c_order, s_order, 1), load(tgt, raw, 0)]
        for copy in loads:
            copy.start()
        for copy in w_loads:
            copy.wait()
        pack_weights()
        turn_weights()
        for copy in loads:
            copy.wait()
        lay_out_cells()
        target[...] = mm(s_order[...], x_in[...])
        make_select()
        arrive()
        sends = []
        for g in range(2):
            hop(1, h_out, skip_in, g, 0).wait_recv()
            hop(0, h_out, h_in, g, 2).wait_recv()
            u = (h_in[g].astype(f32) + skip_in[g].astype(f32)).astype(bf)
            gh[g, 0] = u
            shifted = mm(s_shift[...], u)
            for phase in range(4):
                feat[g, rows_of(phase), :] = side_by_side(shifted, lambda t: phase_shift(phase, t))
            pre[g] = mm(feat[g], wp[g])
            sends += spread(gh.at[g, 0], gh, a_send, a_recv, g)
        value, gate = pre[0], pre[1]
        sig = jax.nn.sigmoid(gate)
        act_gate = gate * sig
        residual = (value * act_gate - target[...]) * (1.0 / 128.0)
        gd3[0, 0] = (residual * act_gate).astype(bf)
        gd3[1, 0] = (residual * value * (sig * (1.0 + gate * (1.0 - sig)))).astype(bf)
        for g in range(2):
            g_out[g] = mm(side_by_side(mm(s_fold[...], gd3[g, 0]), lambda t: t), wt[g]).astype(bf)
            for copy in (hop(2, g_out, g_in, g, 2), hop(3, g_out, gskip_in, g, 0)):
                copy.start()
                sends.append(copy)
            sends += spread(gd3.at[g, 0], gd3, d_send, d_recv, g)
        for g in range(2):
            for k in (1, 3, 2):
                spread_wait(gh.at[g, 0], gh, a_send, a_recv, g, k)
            source = gh[g].reshape(4 * ROWS, GW)
            for k in range(4):
                for i in range(2):
                    left[i, g, rows_of(k, 4 * SLOT), :] = block_rows(g, k, i, source).astype(bf)
        for g in range(2):
            fill_taps(0, s_fold[...], gd3[g, 0])
            for k in (1, 3, 2):
                spread_wait(gd3.at[g, 0], gd3, d_send, d_recv, g, k)
                fill_taps(k, s_fold[...], gd3[g, k])
            for k in (2, 1, 3, 0):
                block = sum(mm(left[i, g, rows_of(k, 4 * SLOT), :], taps[block_tap(g, k, i)]) for i in range(2))
                sends += hand_block(g, k, block)
        for copy in sends:
            copy.wait_send()

    sends = []
    for g in range(2):
        for k in (1, 3, 2):
            remote(pack.at[g, k], r_buf.at[g, k], r_send.at[g, k], r_recv.at[g, k], reduce_peer[g](k)).wait_recv()
        r_sum[g] = r_sum[g] + r_buf[g, 1].astype(f32) + r_buf[g, 2].astype(f32) + r_buf[g, 3].astype(f32)
    for k in (2, 1, 3):
        z_out[k] = z_slot(k).astype(bf)
        copy = remote(z_out.at[k], z_buf.at[4 - k], z_send.at[k], z_recv.at[4 - k], z_peer(k))
        copy.start()
        sends.append(copy)
    total = z_slot(0)
    for k in (1, 3, 2):
        remote(z_out.at[k], z_buf.at[k], z_send.at[k], z_recv.at[k], z_peer(k)).wait_recv()
        total = total + z_buf[k].astype(f32)
    lane = lax.broadcasted_iota(jnp.int32, (SLOT, GW), 1)
    side = total[:, 512:640]
    moved = pltpu.roll(jnp.concatenate([total[:, 256:512], side], axis=1), 64, 1)
    upper = jnp.where((lane < 64) | (lane >= CH), jnp.concatenate([side, side, side], axis=1), moved)
    out[:, 0, :] = jnp.concatenate([total[:, 0:256], upper], axis=1)[0:SHARE]
    for copy in sends:
        copy.wait_send()


def on_device(images, targets, kernels):
    bf = jnp.bfloat16

    def by_rows(grids):
        return jnp.transpose(grids, (1, 2, 0, 3))

    consts = [jnp.asarray(t, bf) for t in tables()]
    vm = pltpu.VMEM
    dma = pltpu.SemaphoreType.DMA
    hop = vm((2, ROWS, GW), bf)
    result = pl.pallas_call(
        body,
        out_shape=jax.ShapeDtypeStruct((SHARE, 1, 2 * CH), jnp.float32),
        in_specs=[pl.BlockSpec(memory_space=pltpu.HBM)] * 7,
        out_specs=pl.BlockSpec(memory_space=pltpu.VMEM),
        scratch_shapes=[
            vm((TAPS * CH, 2 * CH), bf),
            vm((1, 12, 2, 12 * CH), bf),
            vm((CELLS, GW), bf),
            vm((TAPS * ROWS, ROWS), bf),
            vm((TAPS * ROWS, CELLS), bf),
            vm((TAPS * ROWS, 4 * ROWS), bf),
            vm((4 * ROWS, CELLS), bf),
            vm((2, KW, GW), bf),
            vm((2, KW, GW), bf),
            vm((2, 4 * ROWS, KW), bf),
            vm((2, ROWS, GW), jnp.float32),
            vm((2, 4 * ROWS, GW), jnp.float32),
            vm((4 * ROWS, GW), jnp.float32),
            vm((TAPS * ROWS, GW), bf),
            hop, hop, hop, hop, hop, hop,
            vm((2, 4, CELLS, GW), bf),
            vm((2, 4, ROWS, GW), bf),
            vm((2, 4, ROWS, GW), bf),
            vm((2, 4, 4 * ROWS, GW), bf),
            vm((TAPS, 4 * ROWS, GW), bf),
            vm((4 * SLOT, GW), jnp.int32),
            vm((2, 2, 16 * SLOT, 4 * ROWS), bf),
            vm((2, 4, 5 * SLOT, 256), bf),
            vm((2, 4, 5 * SLOT, 256), bf),
            vm((2, 5 * SLOT, 256), jnp.float32),
            vm((4, SLOT, 2 * CH), bf),
            vm((4, SLOT, 2 * CH), bf),
            dma((10,)), dma((4, 2)), dma((4, 2)),
            dma((2, 4)), dma((2, 4)), dma((2, 4)), dma((2, 4)), dma((2, 4)), dma((2, 4)), dma((4,)), dma((4,)),
        ],
        compiler_params=pltpu.CompilerParams(
            collective_id=0, has_side_effects=True, vmem_limit_bytes=63 * 1024 * 1024
        ),
    )(by_rows(images), by_rows(targets), kernels, *consts)
    return jnp.transpose(result, (1, 0, 2))


def solution(mesh):
    return jax.shard_map(
        on_device,
        mesh=mesh,
        in_specs=(P(None, "dp", None, None), P(None, "dp", None, None), P("section", None, None)),
        out_specs=P("section", "dp", None),
        check_vma=False,
    )
```

```python
import jax
import jax.numpy as jnp
import numpy as np
from jax import lax
from jax.experimental import pallas as pl
from jax.experimental.pallas import tpu as pltpu
from jax.sharding import PartitionSpec as P

MESH = pl.DeviceIdType.MESH
ROWS = 80
CH = 320
GW = 384
TAPS = 9
KW = TAPS * CH + 64
SHARE = 45
SLOT = 48
CELLS = 12 * 32


def phase_shift(phase, tap):
    alpha, beta = divmod(phase, 2)
    a, b = divmod(tap, 3)
    return ((alpha + a - 1) // 2 + 1) * 3 + ((beta + b - 1) // 2 + 1)


def tables():
    shift = np.zeros((TAPS, ROWS, ROWS), np.float32)
    encode = np.zeros((TAPS, ROWS, CELLS), np.float32)
    order = np.zeros((4, ROWS, CELLS), np.float32)
    for n in range(2):
        for i in range(6):
            for j in range(6):
                r = n * 36 + i * 6 + j
                for tap in range(TAPS):
                    a, b = divmod(tap, 3)
                    ii, jj = i + a - 1, j + b - 1
                    if 0 <= ii < 6 and 0 <= jj < 6:
                        shift[tap, r, n * 36 + ii * 6 + jj] = 1
                    ii, jj = 2 * i + a - 1, 2 * j + b - 1
                    if 0 <= ii < 12 and 0 <= jj < 12:
                        encode[tap, r, jj * 32 + n * 16 + ii] = 1
                for phase in range(4):
                    alpha, beta = divmod(phase, 2)
                    order[phase, r, (2 * j + beta) * 32 + n * 16 + 2 * i + alpha] = 1
    fold = np.zeros((TAPS, ROWS, 4, ROWS), np.float32)
    for tap in range(TAPS):
        for phase in range(4):
            fold[tap, :, phase, :] = shift[phase_shift(phase, tap)].T
    return (
        shift.reshape(TAPS * ROWS, ROWS),
        encode.reshape(TAPS * ROWS, CELLS),
        fold.reshape(TAPS * ROWS, 4 * ROWS),
        order.reshape(4 * ROWS, CELLS),
    )


def silu(v):
    return v * jax.nn.sigmoid(v)


def silu_slope(v):
    g = jax.nn.sigmoid(v)
    return g * (1.0 + v * (1.0 - g))


def mm(a, b):
    return jnp.dot(a, b, preferred_element_type=jnp.float32)


def mm_nt(a, b):
    return lax.dot_general(a, b, (((1,), (1,)), ((), ())), preferred_element_type=jnp.float32)


def remote(src, dst, send_sem, recv_sem, device):
    return pltpu.make_async_remote_copy(
        src_ref=src, dst_ref=dst, send_sem=send_sem, recv_sem=recv_sem, device_id=device, device_id_type=MESH
    )


def body(
    img, tgt, ker, c_shift, c_encode, c_fold, c_order, out,
    w_in, raw, x_in, s_shift, s_encode, s_fold, s_order,
    wp, wt, feat, act, pre, target, zed,
    h_in, skip_in, g_in, gskip_in, h_out, g_out,
    gx, gh, gd, gd3, taps, select, left, pack, r_buf, r_sum, z_out, z_buf,
    load_sem, hop_send, hop_recv, a_send, a_recv, d_send, d_recv, r_send, r_recv, z_send, z_recv,
):
    bf = jnp.bfloat16
    f32 = jnp.float32
    sec = lax.axis_index("section")
    dp = lax.axis_index("dp")
    x, y, z = dp // 16, (dp // 4) % 4, dp % 4

    def x_peer(k):
        return {"dp": (x + k) % 4 * 16 + y * 4 + z}

    def y_peer(k):
        return {"dp": x * 16 + (y + k) % 4 * 4 + z}

    def z_peer(k):
        return {"dp": x * 16 + y * 4 + (z + k) % 4}

    gather_peer = (x_peer, y_peer)
    reduce_peer = (y_peer, x_peer)

    def load(src, dst, n):
        return pltpu.make_async_copy(src, dst, load_sem.at[n])

    w_loads = []
    for n, (first, last) in enumerate(((0, GW), (GW, 2 * CH))):
        for i in range(3):
            part = (slice(i * 4 * CH, min((i + 1) * 4, TAPS) * CH), slice(first, last))
            w_loads.append(load(ker.at[(0, *part)], w_in.at[part], 4 + 3 * n + i))
    x_load = load(img, raw, 0)
    e_load = load(c_encode, s_encode, 1)

    @pl.when(sec == 0)
    def first_loads():
        x_load.start()
        e_load.start()

    for copy in w_loads:
        copy.start()

    barrier = pltpu.get_barrier_semaphore()
    for k in range(1, 4):
        pl.semaphore_signal(barrier, inc=1, device_id={"section": (sec + k) % 4}, device_id_type=MESH)
        for peer in (x_peer, y_peer, z_peer):
            pl.semaphore_signal(barrier, inc=1, device_id=peer(k), device_id_type=MESH)

    def arrive():
        pl.semaphore_wait(barrier, 12)

    def spread(src, buf, send, recv, g):
        copies = []
        for k in (1, 3, 2):
            copy = remote(src, buf.at[g, 4 - k], send.at[g, k], recv.at[g, 4 - k], gather_peer[g](k))
            copy.start()
            copies.append(copy)
        return copies

    def spread_wait(src, buf, send, recv, g, k):
        remote(src, buf.at[g, k], send.at[g, k], recv.at[g, k], gather_peer[g](k)).wait_recv()

    def hop(kind, src, dst, g, to):
        return remote(src.at[g], dst.at[g], hop_send.at[kind, g], hop_recv.at[kind, g], {"section": to})

    def rows_of(t, n=ROWS):
        return slice(t * n, (t + 1) * n)

    def pack_weights():
        lane = lax.broadcasted_iota(jnp.int32, (CH, GW), 1)

        def one(t, carry):
            rows = pl.ds(pl.multiple_of(t * CH, 16), CH)
            first = w_in[rows, 0:GW].astype(f32)
            wp[0, rows, :] = jnp.where(lane < CH, first, 0.0).astype(bf)
            second = pltpu.roll(w_in[rows, 256:640].astype(f32), GW - 64, 1)
            wp[1, rows, :] = jnp.where(lane < CH, second, 0.0).astype(bf)
            return carry

        for g in range(2):
            wp[g, TAPS * CH:KW, :] = jnp.zeros((64, GW), bf)
            wt[g, TAPS * CH:KW, :] = jnp.zeros((64, GW), bf)
        lax.fori_loop(0, TAPS, one, 0)

    def turn_weights():
        def one(t, carry):
            rows = pl.ds(pl.multiple_of(t * CH, 16), CH)
            for g in range(2):
                block = jnp.concatenate([wp[g, rows, :], jnp.zeros((GW - CH, GW), bf)], axis=0)
                wt[g, rows, :] = block.T[0:CH]
            return carry

        lax.fori_loop(0, TAPS, one, 0)

    def side_by_side(part, order):
        moved = {}
        columns = []
        for t in range(0, TAPS - 1, 2):
            n = order(t + 1)
            if n not in moved:
                moved[n] = pltpu.roll(part[rows_of(n)], 64, 1).astype(bf)
            a, b = part[rows_of(order(t))].astype(bf), moved[n]
            columns += [a[:, 0:256], a[:, 256:GW] + b[:, 0:128], b[:, 128:GW]]
        columns.append(part[rows_of(order(TAPS - 1))].astype(bf))
        return jnp.concatenate(columns, axis=1)

    def lay_out_cells(grids):
        lane = lax.broadcasted_iota(jnp.int32, (12, GW), 1)
        for n in range(2):
            for j in range(12):
                start = j * CH - 64 * (j % 2)
                part = grids[0, :, n, start:start + GW].astype(f32)
                if j % 2:
                    part = pltpu.roll(part, GW - 64, 1)
                x_in[j * 32 + n * 16:j * 32 + n * 16 + 12, :] = jnp.where(lane < CH, part, 0.0).astype(bf)

    def make_select():
        lane = lax.broadcasted_iota(jnp.int32, (SLOT, GW), 1)
        row = lax.broadcasted_iota(jnp.int32, (SLOT, GW), 0)
        for j in range(4):
            value = row - lane + SHARE * ((z + j) % 4)
            select[rows_of(j, SLOT), :] = jnp.where((row < SHARE) & (lane < CH), value, -100000)

    def block_start(g, k):
        return 720 * x + 180 * ((y + k) % 4) if g == 0 else 720 * ((x + k) % 4) + 180 * y

    def block_tap(g, k, i):
        return jnp.minimum(block_start(g, k) // CH + i, TAPS - 1)

    def block_rows(g, k, i, source):
        start = block_start(g, k)
        chosen = select[...] == CH * (start // CH + i) - start
        return mm_nt(jnp.where(chosen, 1.0, 0.0).astype(bf), source)

    def make_left(g):
        for k in range(4):
            rows = sum(block_rows(g, k, i, taps[block_tap(g, k, i)]) for i in range(2))
            left[0, g, rows_of(k, 4 * SLOT), :] = rows.astype(bf)

    def fill_taps(k, table, source):
        part = mm(table, source).astype(bf)
        for t in range(TAPS):
            taps[t, rows_of(k), :] = part[rows_of(t)]

    def half_lanes(first, second):
        return jnp.where(lax.broadcasted_iota(jnp.int32, first.shape, 1) < 64, first, pltpu.roll(second, 64, 1))

    def squeeze(block):
        last = [block[rows_of(j, SLOT), 256:GW] for j in range(4)]
        side = jnp.concatenate([half_lanes(last[0], last[1]), half_lanes(last[2], last[3])], axis=1)
        return jnp.concatenate([block[:, 0:256], side], axis=0)

    def z_slot(j):
        side = slice(4 * SLOT, 5 * SLOT), slice(128 * (j // 2), 128 * (j // 2) + 128)
        first, second = r_sum[(0, *side)], r_sum[(1, *side)]
        if j % 2:
            first = pltpu.roll(first, 64, 1)
            second = pltpu.roll(second, 64, 1)
        return jnp.concatenate([r_sum[0, rows_of(j, SLOT), :], r_sum[1, rows_of(j, SLOT), :], half_lanes(first, second)], axis=1)

    def hand_block(g, k, block):
        if k == 0:
            r_sum[g] = squeeze(block)
            return []
        pack[g, k] = squeeze(block).astype(bf)
        copy = remote(pack.at[g, k], r_buf.at[g, 4 - k], r_send.at[g, k], r_recv.at[g, 4 - k], reduce_peer[g](k))
        copy.start()
        return [copy]

    def gradient(g):
        copies = []
        for k in (1, 3, 2):
            spread_wait(gd.at[g, 0], gd, d_send, d_recv, g, k)
        right = gd[g].reshape(4 * ROWS, GW)
        for k in (2, 1, 3, 0):
            copies += hand_block(g, k, mm(left[0, g, rows_of(k, 4 * SLOT), :], right))
        return copies

    @pl.when(sec == 0)
    def encoder():
        x_in[...] = jnp.zeros((CELLS, GW), bf)
        x_load.wait()
        lay_out_cells(raw)
        e_load.wait()
        part = mm(s_encode[...], x_in[...])
        zed[...] = part.astype(bf)
        feat[0, 0:ROWS, :] = side_by_side(part, lambda t: t)
        lane = lax.broadcasted_iota(jnp.int32, (ROWS, GW), 1)
        sends = []
        for g in range(2):
            acc = jnp.zeros((ROWS, GW), f32)
            for i in range(3):
                w_loads[3 * g + i].wait()
                rows = slice(i * 4 * CH, min((i + 1) * 4, TAPS) * CH)
                acc = acc + mm(feat[0, 0:ROWS, rows], w_in[rows, g * 256:g * 256 + GW])
            if g:
                acc = pltpu.roll(acc, GW - 64, 1)
            acc = jnp.where(lane < CH, acc, 0.0)
            act[g] = acc
            h_out[g] = silu(acc).astype(bf)
            if g == 0:
                arrive()
            for copy in (hop(0, h_out, h_in, g, 1), hop(1, h_out, skip_in, g, 3)):
                copy.start()
                sends.append(copy)
        for g in range(2):
            sends += spread(raw, gx, a_send, a_recv, g)
        make_select()
        for g in range(2):
            for t in range(TAPS):
                taps[t, rows_of(0), :] = zed[rows_of(t)]
            for k in (1, 3, 2):
                spread_wait(raw, gx, a_send, a_recv, g, k)
                lay_out_cells(gx.at[g, k])
                fill_taps(k, s_encode[...], x_in[...])
            make_left(g)
        for g in range(2):
            hop(3, g_out, gskip_in, g, 3).wait_recv()
            hop(2, g_out, g_in, g, 1).wait_recv()
            total = g_in[g].astype(f32) + gskip_in[g].astype(f32)
            gd[g, 0] = (total * silu_slope(act[g])).astype(bf)
            sends += spread(gd.at[g, 0], gd, d_send, d_recv, g)
        for g in range(2):
            sends += gradient(g)
        for copy in sends:
            copy.wait_send()

    @pl.when((sec == 1) | (sec == 2))
    def centre():
        s_load = load(c_shift, s_shift, 2)
        s_load.start()
        for copy in w_loads:
            copy.wait()
        pack_weights()
        s_load.wait()

        @pl.when(sec == 2)
        def turn_early():
            turn_weights()

        arrive()
        sends = []
        for g in range(2):
            hop(0, h_out, h_in, g, sec - 1).wait_recv()
            acc = mm(side_by_side(mm(s_shift[...], h_in[g]), lambda t: t), wp[g])
            act[g] = acc
            h_out[g] = (h_in[g].astype(f32) + silu(acc)).astype(bf)
            copy = hop(0, h_out, h_in, g, sec + 1)
            copy.start()
            sends.append(copy)
        for g in range(2):
            sends += spread(h_in.at[g], gh, a_send, a_recv, g)

        @pl.when(sec == 1)
        def turn_late():
            turn_weights()

        make_select()

        def prepare(g):
            fill_taps(0, s_shift[...], h_in[g])
            for k in (1, 3, 2):
                spread_wait(h_in.at[g], gh, a_send, a_recv, g, k)
                fill_taps(k, s_shift[...], gh[g, k])
            make_left(g)

        @pl.when(sec == 1)
        def prepare_early():
            for g in range(2):
                prepare(g)

        for g in range(2):
            hop(2, g_out, g_in, g, sec + 1).wait_recv()
            delta = (g_in[g].astype(f32) * silu_slope(act[g])).astype(bf)
            gd[g, 0] = delta
            sends += spread(gd.at[g, 0], gd, d_send, d_recv, g)
            back = mm(side_by_side(mm(s_shift[...], delta), lambda t: 8 - t), wt[g])
            g_out[g] = (g_in[g].astype(f32) + back).astype(bf)
            copy = hop(2, g_out, g_in, g, sec - 1)
            copy.start()
            sends.append(copy)

        @pl.when(sec == 2)
        def prepare_late():
            for g in range(2):
                prepare(g)

        for g in range(2):
            sends += gradient(g)
        for copy in sends:
            copy.wait_send()

    @pl.when(sec == 3)
    def decoder():
        loads = [load(c_shift, s_shift, 2), load(c_fold, s_fold, 3), load(c_order, s_order, 1), load(tgt, raw, 0)]
        for copy in loads:
            copy.start()
        for copy in w_loads:
            copy.wait()
        pack_weights()
        turn_weights()
        for copy in loads:
            copy.wait()
        x_in[...] = jnp.zeros((CELLS, GW), bf)
        lay_out_cells(raw)
        target[...] = mm(s_order[...], x_in[...])
        make_select()
        arrive()
        sends = []
        for g in range(2):
            hop(1, h_out, skip_in, g, 0).wait_recv()
            hop(0, h_out, h_in, g, 2).wait_recv()
            u = (h_in[g].astype(f32) + skip_in[g].astype(f32)).astype(bf)
            gh[g, 0] = u
            shifted = mm(s_shift[...], u)
            for phase in range(4):
                feat[g, rows_of(phase), :] = side_by_side(shifted, lambda t: phase_shift(phase, t))
            pre[g] = mm(feat[g], wp[g])
            sends += spread(gh.at[g, 0], gh, a_send, a_recv, g)
        value, gate = pre[0], pre[1]
        sig = jax.nn.sigmoid(gate)
        act_gate = gate * sig
        residual = (value * act_gate - target[...]) * (1.0 / 128.0)
        gd3[0, 0] = (residual * act_gate).astype(bf)
        gd3[1, 0] = (residual * value * (sig * (1.0 + gate * (1.0 - sig)))).astype(bf)
        for g in range(2):
            g_out[g] = mm(side_by_side(mm(s_fold[...], gd3[g, 0]), lambda t: t), wt[g]).astype(bf)
            for copy in (hop(2, g_out, g_in, g, 2), hop(3, g_out, gskip_in, g, 0)):
                copy.start()
                sends.append(copy)
            sends += spread(gd3.at[g, 0], gd3, d_send, d_recv, g)
        for g in range(2):
            for k in (1, 3, 2):
                spread_wait(gh.at[g, 0], gh, a_send, a_recv, g, k)
            source = gh[g].reshape(4 * ROWS, GW)
            for k in range(4):
                for i in range(2):
                    left[i, g, rows_of(k, 4 * SLOT), :] = block_rows(g, k, i, source).astype(bf)
        for g in range(2):
            fill_taps(0, s_fold[...], gd3[g, 0])
            for k in (1, 3, 2):
                spread_wait(gd3.at[g, 0], gd3, d_send, d_recv, g, k)
                fill_taps(k, s_fold[...], gd3[g, k])
            for k in (2, 1, 3, 0):
                block = sum(mm(left[i, g, rows_of(k, 4 * SLOT), :], taps[block_tap(g, k, i)]) for i in range(2))
                sends += hand_block(g, k, block)
        for copy in sends:
            copy.wait_send()

    sends = []
    for g in range(2):
        for k in (1, 3, 2):
            remote(pack.at[g, k], r_buf.at[g, k], r_send.at[g, k], r_recv.at[g, k], reduce_peer[g](k)).wait_recv()
        r_sum[g] = r_sum[g] + r_buf[g, 1].astype(f32) + r_buf[g, 2].astype(f32) + r_buf[g, 3].astype(f32)
    for k in (2, 1, 3):
        z_out[k] = z_slot(k).astype(bf)
        copy = remote(z_out.at[k], z_buf.at[4 - k], z_send.at[k], z_recv.at[4 - k], z_peer(k))
        copy.start()
        sends.append(copy)
    total = z_slot(0)
    for k in (1, 3, 2):
        remote(z_out.at[k], z_buf.at[k], z_send.at[k], z_recv.at[k], z_peer(k)).wait_recv()
        total = total + z_buf[k].astype(f32)
    lane = lax.broadcasted_iota(jnp.int32, (SLOT, GW), 1)
    side = total[:, 512:640]
    moved = pltpu.roll(jnp.concatenate([total[:, 256:512], side], axis=1), 64, 1)
    upper = jnp.where((lane < 64) | (lane >= CH), jnp.concatenate([side, side, side], axis=1), moved)
    out[:, 0, :] = jnp.concatenate([total[:, 0:256], upper], axis=1)[0:SHARE]
    for copy in sends:
        copy.wait_send()


def on_device(images, targets, kernels):
    bf = jnp.bfloat16

    def by_rows(grids):
        return jnp.transpose(grids, (1, 2, 0, 3))

    consts = [jnp.asarray(t, bf) for t in tables()]
    vm = pltpu.VMEM
    dma = pltpu.SemaphoreType.DMA
    hop = vm((2, ROWS, GW), bf)
    result = pl.pallas_call(
        body,
        out_shape=jax.ShapeDtypeStruct((SHARE, 1, 2 * CH), jnp.float32),
        in_specs=[pl.BlockSpec(memory_space=pltpu.HBM)] * 7,
        out_specs=pl.BlockSpec(memory_space=pltpu.VMEM),
        scratch_shapes=[
            vm((TAPS * CH, 2 * CH), bf),
            vm((1, 12, 2, 12 * CH), bf),
            vm((CELLS, GW), bf),
            vm((TAPS * ROWS, ROWS), bf),
            vm((TAPS * ROWS, CELLS), bf),
            vm((TAPS * ROWS, 4 * ROWS), bf),
            vm((4 * ROWS, CELLS), bf),
            vm((2, KW, GW), bf),
            vm((2, KW, GW), bf),
            vm((2, 4 * ROWS, KW), bf),
            vm((2, ROWS, GW), jnp.float32),
            vm((2, 4 * ROWS, GW), jnp.float32),
            vm((4 * ROWS, GW), jnp.float32),
            vm((TAPS * ROWS, GW), bf),
            hop, hop, hop, hop, hop, hop,
            vm((2, 4, 1, 12, 2, 12 * CH), bf),
            vm((2, 4, ROWS, GW), bf),
            vm((2, 4, ROWS, GW), bf),
            vm((2, 4, 4 * ROWS, GW), bf),
            vm((TAPS, 4 * ROWS, GW), bf),
            vm((4 * SLOT, GW), jnp.int32),
            vm((2, 2, 16 * SLOT, 4 * ROWS), bf),
            vm((2, 4, 5 * SLOT, 256), bf),
            vm((2, 4, 5 * SLOT, 256), bf),
            vm((2, 5 * SLOT, 256), jnp.float32),
            vm((4, SLOT, 2 * CH), bf),
            vm((4, SLOT, 2 * CH), bf),
            dma((10,)), dma((4, 2)), dma((4, 2)),
            dma((2, 4)), dma((2, 4)), dma((2, 4)), dma((2, 4)), dma((2, 4)), dma((2, 4)), dma((4,)), dma((4,)),
        ],
        compiler_params=pltpu.CompilerParams(
            collective_id=0, has_side_effects=True, vmem_limit_bytes=63 * 1024 * 1024
        ),
    )(by_rows(images), by_rows(targets), kernels, *consts)
    return jnp.transpose(result, (1, 0, 2))


def solution(mesh):
    return jax.shard_map(
        on_device,
        mesh=mesh,
        in_specs=(P(None, "dp", None, None), P(None, "dp", None, None), P("section", None, None)),
        out_specs=P("section", "dp", None),
        check_vma=False,
    )
```
